32 devices in a mesh: blk: 16 (over z, x, core), head: 2 (over y).
Axes of the slice: x: 2, y: 2, z: 4, core: 2. Of those that a mesh axis runs over, the one named last changes fastest.
Arguments:
- queries: bfloat16 [2, 2048, 32, 128], P(None, 'blk', 'head'), may hold values from -30 to 30
- new_keys: bfloat16 [2, 2048, 16, 128], P(None, 'blk', 'head'), may hold values from -30 to 30
- new_values: bfloat16 [2, 2048, 16, 128], P(None, 'blk', 'head'), may hold values from -6 to 6
- pool_keys: bfloat16 [32, 128, 16, 128], P('blk', None, 'head'), may hold values from -30 to 30
- pool_values: bfloat16 [32, 128, 16, 128], P('blk', None, 'head'), may hold values from -6 to 6
- page_table: int32 [2, 16], replicated, may hold values from 0 to 31, as said below
- cache_len: int32 [2], replicated, may hold values from 512 to 2048, as said below
- out_weight: bfloat16 [32, 128, 4608], P('head'), may hold values from -0.09375 to 0.09375
- residual: bfloat16 [2, 2048, 4608], P(None, ('blk', 'head')), may hold values from -6 to 6
- post_gain: float32 [4608], replicated, may hold values from 0.1 to 1.9
Outputs:
- mixed: bfloat16 [2, 2048, 4608], P(None, ('blk', 'head'))
The draws below stay inside these ranges and needn't reach their ends.
Inputs may be any that keep to these rules, and one draw needn't show every extreme that they name: `page_table`: every pool page appears exactly once in the table. `cache_len`: one request has exactly 2048 cached tokens.
All inputs are finite; a program needn't handle non-finite values.
Results may differ from the reference program's by a relative error of at most 0.015.
Values may be sent and summed in bfloat16 or wider, within the bound.
No kernel may reach another device: no remote copies, remote signals or barrier semaphores. Data moves between devices by JAX's collectives and lax.ppermute only.
A program may use at most 128 MiB of HBM per device.

```python
import jax
import jax.numpy as jnp
from jax import lax

D = 4608
QH = 32
KVH = 16
HD = 128
PAGE = 128
REQ = 2
TOK_DEV = 256
NEW = 2048
POOL = 32
MAXP = 16


def draw_page_table(key, part):
    order = jax.random.permutation(key, REQ * MAXP)
    return order.reshape(REQ, MAXP).astype(jnp.int32)


def draw_cache_len(key, part):
    full_len = MAXP * PAGE
    chosen = jax.random.randint(jax.random.fold_in(key, 11), (), 0, REQ)
    others = jax.random.randint(jax.random.fold_in(key, 12), (REQ,), full_len // 4, full_len + 1)
    return jnp.where(jnp.arange(REQ) == chosen, full_len, others).astype(jnp.int32)


def block_scale(key, shape, cuts, smallest, top_value):
    def one(dim, parts):
        heights = jax.random.uniform(jax.random.fold_in(jax.random.fold_in(key, 6), dim), (parts,), jnp.float32, smallest / len(cuts), top_value / len(cuts))
        return jnp.repeat(jnp.exp(heights), shape[dim] // parts).reshape((-1,) + (1,) * (len(shape) - dim - 1))

    gain = one(*cuts[0])
    for cut in cuts[1:]:
        gain = gain * one(*cut)
    return gain


def normal_values(own_key, extent, width, most, shards=(), held_as=jnp.bfloat16):
    level = block_scale(own_key, extent, shards, -0.22, 0.18) if shards else 1.0
    values = jax.random.normal(own_key, extent, jnp.float32) * width * level
    return jnp.minimum(jnp.maximum(values, -most), most).astype(held_as)


def setup_inputs(seed: int = 0) -> dict:
    arg_keys = jax.random.split(jax.random.key(seed), 11)
    queries = normal_values(arg_keys[0], (REQ, NEW, QH, HD), 5.0, 30.0, ((1, 16), (2, 2)))
    new_keys = normal_values(arg_keys[1], (REQ, NEW, KVH, HD), 5.0, 30.0, ((1, 16), (2, 2)))
    new_values = normal_values(arg_keys[2], (REQ, NEW, KVH, HD), 1.0, 6.0, ((1, 16), (2, 2)))
    pool_keys = normal_values(arg_keys[3], (POOL, PAGE, KVH, HD), 5.0, 30.0, ((0, 16), (2, 2)))
    pool_values = normal_values(arg_keys[4], (POOL, PAGE, KVH, HD), 1.0, 6.0, ((0, 16), (2, 2)))
    page_table = draw_page_table(jax.random.fold_in(arg_keys[10], 71), 0)
    cache_len = draw_cache_len(jax.random.fold_in(arg_keys[10], 71), 0)
    out_weight = normal_values(arg_keys[7], (QH, HD, D), (QH * HD) ** -0.5, 0.09375, ((0, 2),))
    residual = normal_values(arg_keys[8], (REQ, NEW, D), 1.0, 6.0, ((1, 32),))
    post_gain = jnp.clip(1.0 + 0.18 * jax.random.normal(arg_keys[9], (D,), jnp.float32), 0.1, 1.9)
    return dict(queries=queries, new_keys=new_keys, new_values=new_values, pool_keys=pool_keys, pool_values=pool_values, page_table=page_table, cache_len=cache_len, out_weight=out_weight, residual=residual, post_gain=post_gain)


soft_cap = 50.0
score_scale = 144.0 ** (-0.5)
norm_eps = 1e-06

def reference(queries, new_keys, new_values, pool_keys, pool_values, page_table, cache_len, out_weight, residual, post_gain):
    group = QH // KVH
    cache_tokens = MAXP * PAGE
    attended_all = []
    for request in range(REQ):
        slots = page_table[request].astype(jnp.int32)
        cache_k = pool_keys[slots].reshape(cache_tokens, KVH, HD)
        cache_v = pool_values[slots].reshape(cache_tokens, KVH, HD)
        key_all = jnp.concatenate([cache_k, new_keys[request]], 0).astype(jnp.float32)
        value_all = jnp.concatenate([cache_v, new_values[request]], 0).astype(jnp.float32)
        cache_ok = jnp.arange(cache_tokens, dtype=jnp.int32) < cache_len[request]
        query_req = queries[request].reshape(NEW // TOK_DEV, TOK_DEV, KVH, group, HD)

        def block_attend(inputs):
            query_block, block_index = inputs
            query_index = block_index * TOK_DEV + jnp.arange(TOK_DEV, dtype=jnp.int32)
            new_ok = jnp.arange(NEW, dtype=jnp.int32)[None, :] <= query_index[:, None]
            valid_keys = jnp.concatenate([jnp.broadcast_to(cache_ok[None, :], (TOK_DEV, cache_tokens)), new_ok], 1)
            scores = jnp.einsum('tkgd,skd->kgts', query_block.astype(jnp.float32), key_all, precision=lax.Precision.HIGHEST) * score_scale
            capped = soft_cap * jnp.tanh(scores / soft_cap)
            weights = jnp.where(valid_keys[None, None], jnp.exp(capped), 0.0).astype(jnp.bfloat16)
            weights = lax.optimization_barrier(weights).astype(jnp.float32)
            numerator = jnp.einsum('kgts,skd->tkgd', weights, value_all, precision=lax.Precision.HIGHEST)
            denominator = lax.optimization_barrier(jnp.sum(weights, axis=-1))
            return (numerator / jnp.transpose(denominator, (2, 0, 1))[..., None]).astype(jnp.bfloat16)
        blocks_out = lax.map(block_attend, (query_req, jnp.arange(NEW // TOK_DEV, dtype=jnp.int32)))
        attended_all.append(blocks_out.reshape(NEW, QH * HD))
    attended = jnp.concatenate(attended_all, 0)
    projected = jnp.dot(attended, out_weight.reshape(QH * HD, D), preferred_element_type=jnp.float32)
    inv_rms = lax.rsqrt(lax.optimization_barrier(jnp.mean(projected * projected, axis=-1, keepdims=True)) + norm_eps)
    mixed_out = residual.reshape(REQ * NEW, D).astype(jnp.float32) + post_gain * projected * inv_rms
    return mixed_out.reshape(REQ, NEW, D).astype(jnp.bfloat16)
```

```python
import jax
import jax.numpy as jnp
from jax import lax
from jax.experimental import pallas as pl
from jax.experimental.pallas import tpu as pltpu
from jax.sharding import PartitionSpec as P

soft_cap = 50.0
score_scale = 144.0 ** (-0.5)
norm_eps = 1e-06
log2_e = 1.4426950408889634
key_chunk = 512


def split_heads(source, heads, staged):
    rows = source.shape[0]
    count = source.shape[1]
    staged[0 : rows * count, :] = source[...].reshape(rows * count, source.shape[2]).astype(jnp.float32)
    for head in heads:
        yield staged[pl.ds(head, rows, stride=count), :].astype(jnp.bfloat16)


def pack_message_kernel(pool_k, pool_v, new_k, new_v, out, staged):
    step = pl.program_id(0)
    kv_heads = pool_k.shape[2]
    for head, rows in enumerate(split_heads(pool_k[0], range(kv_heads), staged)):
        out[head, 0, step] = rows
    for head, rows in enumerate(split_heads(pool_v[0], range(kv_heads), staged)):
        out[head, 1, step] = rows
    for head, rows in enumerate(split_heads(new_k[0], range(kv_heads), staged)):
        out[head, step, 2] = rows
    for head, rows in enumerate(split_heads(new_v[0], range(kv_heads), staged)):
        out[head, step, 3] = rows


def pack_message(pool_keys, pool_values, new_keys, new_values):
    steps, rows, kv_heads, head_dim = pool_keys.shape
    source = pl.BlockSpec((1, rows, kv_heads, head_dim), lambda i: (i, 0, 0, 0))
    return pl.pallas_call(
        pack_message_kernel,
        grid=(steps,),
        in_specs=[source] * 4,
        out_specs=pl.BlockSpec((kv_heads, 2, 4, rows, head_dim), lambda i: (0, 0, 0, 0, 0)),
        out_shape=jax.ShapeDtypeStruct((kv_heads, 2, 4, rows, head_dim), jnp.bfloat16),
        scratch_shapes=[pltpu.VMEM((rows * kv_heads, head_dim), jnp.float32)],
        compiler_params=pltpu.CompilerParams(vmem_limit_bytes=24 * 1024 * 1024),
        cost_estimate=pl.CostEstimate(flops=0, bytes_accessed=4 * 1024 * 1024, transcendentals=0),
        name="pack_message",
    )(pool_keys, pool_values, new_keys, new_values)


def pack_queries_kernel(queries, out, staged):
    group = out.shape[2]
    for head, rows in enumerate(split_heads(queries[0], range(queries.shape[2]), staged)):
        out[head // group, 0, head % group] = rows


def pack_queries(queries, kv_heads):
    steps, rows, heads, head_dim = queries.shape
    group = heads // kv_heads
    return pl.pallas_call(
        pack_queries_kernel,
        grid=(steps,),
        in_specs=[pl.BlockSpec((1, rows, heads, head_dim), lambda i: (i, 0, 0, 0))],
        out_specs=pl.BlockSpec((kv_heads, 1, group, rows, head_dim), lambda i: (0, i, 0, 0, 0)),
        out_shape=jax.ShapeDtypeStruct((kv_heads, steps, group, rows, head_dim), jnp.bfloat16),
        scratch_shapes=[pltpu.VMEM((rows * heads, head_dim), jnp.float32)],
        compiler_params=pltpu.CompilerParams(vmem_limit_bytes=24 * 1024 * 1024),
        cost_estimate=pl.CostEstimate(flops=0, bytes_accessed=2 * 1024 * 1024, transcendentals=0),
        name="pack_queries",
    )(queries)


def attend_kernel(core_ref, pages_ref, len_ref, message, other, queries, out, cache_k, cache_v, new_v):
    blocks, _, rows, head_dim = message.shape
    group = queries.shape[1]
    slots = pages_ref.shape[1]
    core = core_ref[0]
    cached = len_ref[core]
    for slot in range(slots):
        page = pages_ref[core, slot]
        mine = message[page // 2, page % 2]
        theirs = other[page // 2, page % 2]
        seen = slot * rows + lax.broadcasted_iota(jnp.int32, (rows, head_dim), 0) < cached
        here = pl.ds(slot * rows, rows)
        keys = jnp.where(core == 0, mine, theirs)
        values = jnp.where(core == 0, theirs, mine).astype(jnp.float32)
        cache_k[here, :] = keys
        cache_v[here, 0:head_dim] = jnp.where(seen, values, 0.0).astype(jnp.bfloat16)
        cache_v[here, head_dim : 2 * head_dim] = jnp.where(seen, 1.0, 0.0).astype(jnp.bfloat16)
    for block in range(blocks):
        here = pl.ds(block * rows, rows)
        new_v[here, 0:head_dim] = message[block, 3]
    new_v[:, head_dim : 2 * head_dim] = jnp.ones((blocks * rows, head_dim), jnp.bfloat16)

    chunk = min(key_chunk, blocks * rows)
    chunk_blocks = chunk // rows

    def weights_of(query, keys):
        scores = lax.dot_general(query, keys, (((1,), (1,)), ((), ())), preferred_element_type=jnp.float32)
        return jnp.exp2((soft_cap * log2_e) * jnp.tanh(scores * (score_scale / soft_cap)))

    def new_keys_of(part):
        return message[pl.ds(part * chunk_blocks, chunk_blocks), 2].reshape(chunk, head_dim)

    @pl.loop(0, blocks)
    def _(block):
        query = queries[block].reshape(group * rows, head_dim)
        total = jnp.zeros((group * rows, 2 * head_dim), jnp.float32)
        for part in range(slots * rows // chunk):
            here = pl.ds(part * chunk, chunk)
            weights = weights_of(query, cache_k[here, :]).astype(jnp.bfloat16)
            total += jnp.dot(weights, cache_v[here, :], preferred_element_type=jnp.float32)

        def full(part, total):
            weights = weights_of(query, new_keys_of(part)).astype(jnp.bfloat16)
            here = pl.ds(pl.multiple_of(part * chunk, chunk), chunk)
            return total + jnp.dot(weights, new_v[here, :], preferred_element_type=jnp.float32)

        last = block // chunk_blocks
        total = lax.fori_loop(0, last, full, total)
        key_at = last * chunk + lax.broadcasted_iota(jnp.int32, (rows, chunk), 1)
        query_at = block * rows + lax.broadcasted_iota(jnp.int32, (rows, chunk), 0)
        seen = jnp.concatenate([key_at <= query_at] * group, axis=0)
        weights = jnp.where(seen, weights_of(query, new_keys_of(last)), 0.0).astype(jnp.bfloat16)
        here = pl.ds(pl.multiple_of(last * chunk, chunk), chunk)
        total += jnp.dot(weights, new_v[here, :], preferred_element_type=jnp.float32)
        attended = (total[:, 0:head_dim] / total[:, head_dim : 2 * head_dim]).astype(jnp.bfloat16)
        for head in range(group):
            out[block, :, head * head_dim : (head + 1) * head_dim] = attended[head * rows : (head + 1) * rows, :]


def attend(core, page_table, cache_len, message, other, queries):
    blocks, _, rows, head_dim = message.shape
    group = queries.shape[1]
    slots = page_table.shape[1]
    in_smem = pl.BlockSpec(memory_space=pltpu.SMEM)
    in_vmem = pl.BlockSpec(memory_space=pltpu.VMEM)
    seen = blocks * rows * (slots * rows + blocks * rows // 2) * group
    return pl.pallas_call(
        attend_kernel,
        in_specs=[in_smem] * 3 + [in_vmem] * 3,
        out_specs=in_vmem,
        out_shape=jax.ShapeDtypeStruct((blocks, rows, group * head_dim), jnp.bfloat16),
        scratch_shapes=[
            pltpu.VMEM((slots * rows, head_dim), jnp.bfloat16),
            pltpu.VMEM((slots * rows, 2 * head_dim), jnp.bfloat16),
            pltpu.VMEM((blocks * rows, 2 * head_dim), jnp.bfloat16),
        ],
        compiler_params=pltpu.CompilerParams(vmem_limit_bytes=32 * 1024 * 1024),
        cost_estimate=pl.CostEstimate(
            flops=4 * seen * head_dim, bytes_accessed=message.size * 4 + queries.size * 4, transcendentals=2 * seen
        ),
        name="attend",
    )(core, page_table, cache_len, message, other, queries)


def by_heads(
    queries,
    new_keys,
    new_values,
    pool_keys,
    pool_values,
    page_table,
    cache_len,
    out_weight,
    residual,
    post_gain,
):
    req_count, per_req, heads_here, head_dim = queries.shape
    kv_here = new_keys.shape[2]
    blk_count = lax.axis_size("blk")
    group = heads_here // kv_here
    core = lax.axis_index("blk") % 2
    message = pack_message(pool_keys, pool_values, new_keys, new_values)
    message = message.reshape(blk_count, 4, per_req, head_dim)
    message = lax.all_to_all(message, "blk", 0, 0, tiled=True)
    packed = pack_queries(queries, kv_here).reshape(blk_count, group, per_req, head_dim)
    packed = lax.all_to_all(packed, "blk", 0, 0, tiled=True)
    other = lax.ppermute(message[:, 0:2], "blk", [(i, i ^ 1) for i in range(blk_count)])
    attended = attend(core[None], page_table, cache_len, message, other, packed)
    attended = lax.all_to_all(attended, "blk", 0, 0, tiled=True)
    attended = attended.reshape(kv_here, req_count, per_req, group * head_dim)
    head_count = lax.axis_size("head")
    share = per_req // head_count
    attended = attended.reshape(kv_here, req_count, head_count, share, group * head_dim)
    weight = out_weight.reshape(kv_here, group * head_dim, out_weight.shape[2])

    def project(rows):
        rows = rows.transpose(1, 2, 0, 3).reshape(req_count * share, kv_here * group * head_dim)
        return jnp.dot(rows, weight.reshape(-1, weight.shape[2]), preferred_element_type=jnp.float32)

    mine = lax.axis_index("head")
    theirs = project(lax.dynamic_index_in_dim(attended, 1 - mine, 2, keepdims=False)).astype(jnp.bfloat16)
    arrived = lax.ppermute(theirs, "head", [(0, 1), (1, 0)])
    own = project(lax.dynamic_index_in_dim(attended, mine, 2, keepdims=False))
    projected = (own + arrived.astype(jnp.float32)).reshape(req_count, share, -1)
    inv_rms = lax.rsqrt(jnp.mean(projected * projected, axis=-1, keepdims=True) + norm_eps)
    mixed_out = residual.astype(jnp.float32) + post_gain * projected * inv_rms
    return mixed_out.astype(jnp.bfloat16)


def group_pages(page_count, page_len):
    width = max(1, min(page_count, 2048 // page_len))
    while page_count % width:
        width -= 1
    return width


def attend_pages(running, grouped, key_pages, value_pages, valid_keys):
    page_count, page_len, kv_heads, head_dim = key_pages.shape
    tok_rows = valid_keys.shape[1]
    width = group_pages(page_count, page_len)
    groups = page_count // width
    key_groups = key_pages.reshape(groups, width * page_len, kv_heads, head_dim)
    value_groups = value_pages.reshape(groups, width * page_len, kv_heads, head_dim)
    valid_groups = (
        valid_keys.reshape(groups, width, tok_rows, page_len)
        .transpose(0, 2, 1, 3)
        .reshape(groups, tok_rows, width * page_len)
    )

    def compute(carry_in, key_block, value_block, valid_block):
        numerator, denominator = carry_in
        scores = (
            jnp.einsum("tkgd,skd->kgts", grouped, key_block, preferred_element_type=jnp.float32)
            * score_scale
        )
        capped = soft_cap * jnp.tanh(scores / soft_cap)
        weights = jnp.where(valid_block[None, None], jnp.exp(capped), 0.0).astype(jnp.bfloat16)
        numerator = numerator + jnp.einsum(
            "kgts,skd->tkgd", weights, value_block, preferred_element_type=jnp.float32
        )
        denominator = denominator + jnp.sum(weights.astype(jnp.float32), axis=-1)
        return (numerator, denominator)

    def one_group(carry_in, inputs):
        key_block, value_block, valid_block = inputs
        carry_out = compute(carry_in, key_block, value_block, valid_block)
        return (carry_out, None)

    result, _ = lax.scan(one_group, running, (key_groups, value_groups, valid_groups))
    return result


def shards(
    queries,
    new_keys,
    new_values,
    pool_keys,
    pool_values,
    page_table,
    cache_len,
    out_weight,
    residual,
    post_gain,
):
    req_count, per_req, heads_here, head_dim = queries.shape
    tok_dev = req_count * per_req
    kv_here = new_keys.shape[2]
    page_len = pool_keys.shape[1]
    slot_count = page_table.shape[1]
    blk_place = lax.axis_index("blk")
    row_ids = jnp.arange(tok_dev, dtype=jnp.int32)
    row_request = row_ids // per_req
    row_offset = blk_place * per_req + row_ids % per_req
    grouped = queries.reshape(tok_dev, kv_here, heads_here // kv_here, head_dim)
    page_rows = jnp.arange(page_len, dtype=jnp.int32)
    request_ids = jnp.arange(req_count, dtype=jnp.int32)
    row_onehot = row_request[:, None] == request_ids[None, :]
    start_carry = (
        jnp.zeros((tok_dev, kv_here, heads_here // kv_here, head_dim), jnp.float32),
        jnp.zeros((kv_here, heads_here // kv_here, tok_dev), jnp.float32),
    )
    pieces = (
        lax.all_gather(pool_keys, "blk", axis=0, tiled=True),
        lax.all_gather(pool_values, "blk", axis=0, tiled=True),
    )
    page_ids = jnp.arange(pieces[0].shape[0], dtype=jnp.int32)
    matches = page_ids[:, None, None] == page_table[None, :, :]
    slot_index = jnp.sum(
        jnp.where(matches, jnp.arange(slot_count, dtype=jnp.int32)[None, None, :], 0), axis=2
    )
    owned_page = jnp.any(matches, axis=2)
    position = slot_index[:, :, None] * page_len + page_rows[None, None, :]
    keep_keys = owned_page[:, :, None] & (position < cache_len[None, :, None])
    running = attend_pages(
        start_carry,
        grouped,
        pieces[0],
        pieces[1],
        jnp.any(keep_keys[:, None, :, :] & row_onehot[None, :, :, None], axis=2),
    )
    pieces = (
        lax.all_gather(new_keys, "blk", axis=1, tiled=True),
        lax.all_gather(new_values, "blk", axis=1, tiled=True),
    )
    piece_pages = pieces[0].shape[1] // page_len
    page_index = jnp.arange(req_count * piece_pages, dtype=jnp.int32)
    firsts = page_index % piece_pages * page_len
    key_pages = pieces[0].reshape(req_count * piece_pages, page_len, kv_here, head_dim)
    value_pages = pieces[1].reshape(req_count * piece_pages, page_len, kv_here, head_dim)
    offsets = firsts[:, None] + page_rows[None, :]
    same_request = (page_index // piece_pages)[:, None] == row_request[None, :]
    running = attend_pages(
        running,
        grouped,
        key_pages,
        value_pages,
        same_request[:, :, None] & (offsets[:, None, :] <= row_offset[None, :, None]),
    )
    numerator, denominator = running
    attended = (numerator / jnp.transpose(denominator, (2, 0, 1))[..., None]).astype(jnp.bfloat16)
    head_count = lax.axis_size("head")
    share = per_req // head_count
    feature_len = heads_here * head_dim
    attended = (
        attended.reshape(req_count, head_count, share, feature_len)
        .transpose(1, 0, 2, 3)
        .reshape(tok_dev, feature_len)
    )
    weight_rows = out_weight.reshape(feature_len, out_weight.shape[2])
    projected = lax.psum_scatter(
        jnp.dot(attended, weight_rows, preferred_element_type=jnp.float32).astype(jnp.bfloat16),
        "head",
        scatter_dimension=0,
        tiled=True,
    ).astype(jnp.float32)
    projected = projected.reshape(req_count, share, projected.shape[1])
    inv_rms = lax.rsqrt(jnp.mean(projected * projected, axis=-1, keepdims=True) + norm_eps)
    mixed_out = residual.astype(jnp.float32) + post_gain * projected * inv_rms
    return mixed_out.astype(jnp.bfloat16)


def solution(mesh):
    placed = (
        P(None, "blk", "head", None),
        P(None, "blk", "head", None),
        P(None, "blk", "head", None),
        P("blk", None, "head", None),
        P("blk", None, "head", None),
        P(),
        P(),
        P("head", None, None),
        P(None, ("blk", "head"), None),
        P(),
    )
    def one_device(queries, new_keys, *rest):
        owners = mesh.shape["blk"] == 2 * new_keys.shape[2] and mesh.shape["head"] == 2
        fits = queries.shape[0] == 2 and rest[1].shape[0] == 2 and rest[1].shape[1] == queries.shape[1]
        return (by_heads if owners and fits else shards)(queries, new_keys, *rest)

    return jax.shard_map(
        one_device,
        mesh=mesh,
        in_specs=placed,
        out_specs=P(None, ("blk", "head"), None),
        check_vma=False,
    )
```

```python
import functools

import jax
import jax.numpy as jnp
from jax import lax
from jax.experimental import pallas as pl
from jax.experimental.pallas import tpu as pltpu
from jax.sharding import PartitionSpec as P

soft_cap = 50.0
score_scale = 144.0 ** (-0.5)
norm_eps = 1e-06
log2_e = 1.4426950408889634
chunks = 2
key_tile = 256
mib = 1024 * 1024
in_vmem = pl.BlockSpec(memory_space=pltpu.VMEM)
in_smem = pl.BlockSpec(memory_space=pltpu.SMEM)


def kernel_params(limit_mib):
    return pltpu.CompilerParams(vmem_limit_bytes=limit_mib * mib)


def split_heads(source, staged):
    rows, heads, head_dim = source.shape
    staged[0 : rows * heads, :] = source.reshape(rows * heads, head_dim).astype(jnp.float32)
    for head in range(heads):
        yield head, staged[pl.ds(head, rows, stride=heads), :].astype(jnp.bfloat16)


def put_queries(queries, out, part, staged):
    _, shares, _, rows, heads, head_dim = queries.shape
    group = heads // out.shape[0]
    source = queries[...].reshape(shares * rows, heads, head_dim)
    for head, picked in split_heads(source, staged):
        first = head % group * shares * rows
        out[head // group, 0, part, first : first + shares * rows, :] = picked


def pack_first(pool_keys, pool_values, new_keys, new_values, queries):
    steps, rows, kv_heads, head_dim = new_keys.shape
    pages = pool_keys.shape[0]
    parts = pages + 3

    def kernel(pool_k, pool_v, new_k, new_v, some_queries, out, staged):
        core = pl.program_id(0)

        @pl.when(core == 0)
        def _():
            for page in range(pages):
                for head, picked in split_heads(pool_k[page], staged):
                    out[head, 0, page] = picked

        @pl.when(core == 1)
        def _():
            for page in range(pages):
                for head, picked in split_heads(pool_v[page], staged):
                    out[head, 0, page] = picked

        for head, picked in split_heads(new_k[0], staged):
            out[head, 0, pages] = picked
        for head, picked in split_heads(new_v[0], staged):
            out[head, 0, pages + 1] = picked
        put_queries(some_queries, out, pages + 2, staged)

    whole = pl.BlockSpec((pages, rows, kv_heads, head_dim), lambda i: (0, 0, 0, 0))
    one = pl.BlockSpec((1, rows, kv_heads, head_dim), lambda i: (i, 0, 0, 0))
    _, shares, _, chunk_rows, heads, _ = queries.shape
    some = pl.BlockSpec((1, shares, 1, chunk_rows, heads, head_dim), lambda i: (i, 0, 0, 0, 0, 0))
    sources = [pltpu.with_memory_space_constraint(x, pltpu.HBM) for x in (pool_keys, pool_values, new_keys, new_values, queries)]
    return pl.pallas_call(
        kernel,
        grid=(steps,),
        in_specs=[whole, whole, one, one, some],
        out_specs=pl.BlockSpec((kv_heads, 1, parts, rows, head_dim), lambda i: (0, i, 0, 0, 0)),
        out_shape=jax.ShapeDtypeStruct((kv_heads, steps, parts, rows, head_dim), jnp.bfloat16),
        scratch_shapes=[pltpu.VMEM((rows * kv_heads, head_dim), jnp.float32)],
        compiler_params=kernel_params(24),
        cost_estimate=pl.CostEstimate(flops=0, bytes_accessed=6 * mib, transcendentals=0),
        name="pack_first",
    )(*sources)


def pack_queries(queries, kv_heads, chunk):
    steps, shares, _, rows, heads, head_dim = queries.shape
    group = heads // kv_heads

    def kernel(some_queries, out, staged):
        put_queries(some_queries, out, 0, staged)

    return pl.pallas_call(
        kernel,
        grid=(steps,),
        in_specs=[pl.BlockSpec((1, shares, 1, rows, heads, head_dim), lambda i: (i, 0, chunk, 0, 0, 0))],
        out_specs=pl.BlockSpec((kv_heads, 1, 1, group * shares * rows, head_dim), lambda i: (0, i, 0, 0, 0)),
        out_shape=jax.ShapeDtypeStruct((kv_heads, steps, 1, group * shares * rows, head_dim), jnp.bfloat16),
        scratch_shapes=[pltpu.VMEM((shares * rows * heads, head_dim), jnp.float32)],
        compiler_params=kernel_params(24),
        cost_estimate=pl.CostEstimate(flops=0, bytes_accessed=mib, transcendentals=0),
        name="pack_queries",
    )(pltpu.with_memory_space_constraint(queries, pltpu.HBM))


def attend_kernel(pages, chunk, shares, core_ref, table_ref, len_ref, message, other, *rest):
    out, cache_k, cache_v, new_v, total = rest[-5:]
    queries, query_part = (rest[0], 0) if len(rest) > 5 else (message, pages + 2)
    blocks, _, page_rows, head_dim = message.shape
    slots = table_ref.shape[1]
    block_rows = queries.shape[2]
    group = out.shape[2] // head_dim
    core = core_ref[0]
    cached = len_ref[core]
    for slot in range(slots):
        page = table_ref[core, slot]
        mine = message[page // pages, page % pages]
        theirs = other[page // pages, page % pages]
        seen = slot * page_rows + lax.broadcasted_iota(jnp.int32, (page_rows, head_dim), 0) < cached
        here = pl.ds(slot * page_rows, page_rows)
        cache_k[here, :] = jnp.where(core == 0, mine, theirs)
        values = jnp.where(core == 0, theirs, mine).astype(jnp.float32)
        cache_v[here, 0:head_dim] = jnp.where(seen, values, 0.0).astype(jnp.bfloat16)
        cache_v[here, head_dim : 2 * head_dim] = jnp.where(seen, 1.0, 0.0).astype(jnp.bfloat16)
    for block in range(blocks):
        new_v[block * page_rows : (block + 1) * page_rows, 0:head_dim] = message[block, pages + 1]
    new_v[:, head_dim : 2 * head_dim] = jnp.ones((blocks * page_rows, head_dim), jnp.bfloat16)

    def add(first_block, block_count, keys, values, begin=False, causal=False):
        rows = block_count * block_rows
        query = queries[first_block : first_block + block_count, query_part].reshape(rows, head_dim)
        scores = lax.dot_general(query, keys, (((1,), (1,)), ((), ())), preferred_element_type=jnp.float32)
        weights = jnp.exp2((soft_cap * log2_e) * jnp.tanh(scores * (score_scale / soft_cap)))
        if causal:
            row = lax.broadcasted_iota(jnp.int32, weights.shape, 0)
            in_chunk = block_rows // (group * shares)
            offset = row // block_rows * page_rows + row // in_chunk % shares * (page_rows // shares)
            offset += chunk * in_chunk + row % in_chunk
            weights = jnp.where(lax.broadcasted_iota(jnp.int32, weights.shape, 1) <= offset, weights, 0.0)
        product = jnp.dot(weights.astype(jnp.bfloat16), values, preferred_element_type=jnp.float32)
        here = pl.ds(first_block * block_rows, rows)
        total[here, :] = product if begin else total[here, :] + product

    half = blocks // 2
    for first in (0, half):
        for tile in range(0, slots * page_rows, key_tile):
            add(first, half, cache_k[tile : tile + key_tile, :], cache_v[tile : tile + key_tile, :], begin=tile == 0)
    tile_blocks = key_tile // page_rows
    for block in range(0, blocks, tile_blocks):
        keys = message[block : block + tile_blocks, pages].reshape(key_tile, head_dim)
        values = new_v[block * page_rows : block * page_rows + key_tile, :]
        add(block, tile_blocks, keys, values, causal=True)
        later = block + tile_blocks
        while later < blocks:
            count = min(half, blocks - later)
            add(later, count, keys, values)
            later += count
    per_head = block_rows // group
    for block in range(blocks):
        here = pl.ds(block * block_rows, block_rows)
        attended = (total[here, 0:head_dim] / total[here, head_dim : 2 * head_dim]).astype(jnp.bfloat16)
        for head in range(group):
            out[block, :, head * head_dim : (head + 1) * head_dim] = attended[head * per_head : (head + 1) * per_head, :]


def attend(core, page_table, cache_len, message, other, queries, chunk, pages, shares, group):
    blocks, _, page_rows, head_dim = message.shape
    slots = page_table.shape[1]
    block_rows = page_rows * group // chunks
    operands = [message, other] + ([] if queries is None else [queries])
    seen = blocks * block_rows * (slots + blocks // 2) * page_rows
    return pl.pallas_call(
        functools.partial(attend_kernel, pages, chunk, shares),
        in_specs=[in_smem] * 3 + [in_vmem] * len(operands),
        out_specs=in_vmem,
        out_shape=jax.ShapeDtypeStruct((blocks, block_rows // group, group * head_dim), jnp.bfloat16),
        scratch_shapes=[
            pltpu.VMEM((slots * page_rows, head_dim), jnp.bfloat16),
            pltpu.VMEM((slots * page_rows, 2 * head_dim), jnp.bfloat16),
            pltpu.VMEM((blocks * page_rows, 2 * head_dim), jnp.bfloat16),
            pltpu.VMEM((blocks * block_rows, 2 * head_dim), jnp.float32),
        ],
        compiler_params=kernel_params(24),
        cost_estimate=pl.CostEstimate(flops=8 * seen * head_dim, bytes_accessed=8 * mib, transcendentals=2 * seen),
        name="attend",
    )(core, page_table, cache_len, *operands)


def project_kernel(shares, place_ref, attended, weight, own, theirs, rows):
    place = place_ref[0]
    sources, share_rows, features = attended.shape
    requests = 2
    count = share_rows // shares
    for source in range(sources):
        first = source // requests * features
        for share in range(shares):
            at = pl.multiple_of((share ^ place) * (requests * count), requests * count) + source % requests * count
            rows[pl.ds(at, count), first : first + features] = attended[source, share * count : (share + 1) * count, :]
    width = weight.shape[1]
    tile = 512 if width % 512 == 0 else width
    for first in range(0, width, tile):
        product = jnp.dot(rows[...], weight[:, first : first + tile], preferred_element_type=jnp.float32)
        own[:, first : first + tile] = product[0 : requests * count, :]
        theirs[:, first : first + tile] = product[requests * count :, :].astype(jnp.bfloat16)


def project(place, attended, weight, shares):
    sources, share_rows, features = attended.shape
    depth, width = weight.shape
    rows = 2 * share_rows
    return pl.pallas_call(
        functools.partial(project_kernel, shares),
        in_specs=[in_smem, in_vmem, in_vmem],
        out_specs=[in_vmem, in_vmem],
        out_shape=[
            jax.ShapeDtypeStruct((rows // shares, width), jnp.float32),
            jax.ShapeDtypeStruct((rows // shares, width), jnp.bfloat16),
        ],
        scratch_shapes=[pltpu.VMEM((rows, depth), jnp.bfloat16)],
        compiler_params=kernel_params(16),
        cost_estimate=pl.CostEstimate(flops=2 * rows * depth * width, bytes_accessed=2 * depth * width, transcendentals=0),
        name="project",
    )(place, attended, pltpu.with_memory_space_constraint(weight, pltpu.VMEM))


def finish(own, arrived, residual, gain, chunk, earlier):
    requests, per_req, width = residual.shape
    rows = own.shape[0] // requests

    def kernel(own_ref, arrived_ref, residual_ref, gain_ref, *rest):
        out = rest[-1]
        projected = own_ref[...] + arrived_ref[...].astype(jnp.float32)
        inv_rms = lax.rsqrt(jnp.mean(projected * projected, axis=-1, keepdims=True) + norm_eps)
        out[0] = (residual_ref[0].astype(jnp.float32) + gain_ref[...] * projected * inv_rms).astype(jnp.bfloat16)

    some = pl.BlockSpec((rows, width), lambda i: (i, 0))
    place = pl.BlockSpec((1, rows, width), lambda i: (i, chunk, 0))
    operands = [own, arrived, residual, gain.reshape(1, width)]
    specs = [some, some, place, pl.BlockSpec((1, width), lambda i: (0, 0))]
    if earlier is not None:
        operands.append(earlier)
        specs.append(pl.BlockSpec(memory_space=pl.ANY))
    return pl.pallas_call(
        kernel,
        grid=(requests,),
        in_specs=specs,
        out_specs=place,
        out_shape=jax.ShapeDtypeStruct(residual.shape, jnp.bfloat16),
        input_output_aliases={} if earlier is None else {4: 0},
        compiler_params=kernel_params(16),
        cost_estimate=pl.CostEstimate(flops=0, bytes_accessed=4 * mib, transcendentals=0),
        name="finish",
    )(*operands)


def by_heads(
    queries,
    new_keys,
    new_values,
    pool_keys,
    pool_values,
    page_table,
    cache_len,
    out_weight,
    residual,
    post_gain,
):
    req_count, per_req, heads_here, head_dim = queries.shape
    kv_here = new_keys.shape[2]
    pages = pool_keys.shape[0]
    blk_count = lax.axis_size("blk")
    shares = lax.axis_size("head")
    group = heads_here // kv_here
    core = (lax.axis_index("blk") % 2)[None]
    place = lax.axis_index("head")[None]
    weight = out_weight.reshape(heads_here * head_dim, out_weight.shape[2])
    queries = queries.reshape(req_count, shares, chunks, per_req // (shares * chunks), heads_here, head_dim)
    exchange = functools.partial(lax.all_to_all, axis_name="blk", split_axis=0, concat_axis=0, tiled=True)
    message = pack_first(pool_keys, pool_values, new_keys, new_values, queries)
    message = exchange(message.reshape(blk_count, pages + 3, per_req, head_dim))
    asked = [None]
    for chunk in range(1, chunks):
        packed = pack_queries(queries, kv_here, chunk)
        asked.append(exchange(packed.reshape((blk_count,) + packed.shape[2:])))
    other = lax.ppermute(message[:, 0:pages], "blk", [(i, i ^ 1) for i in range(blk_count)])
    mixed_out = None
    for chunk in range(chunks):
        attended = attend(core, page_table, cache_len, message, other, asked[chunk], chunk, pages, shares, group)
        own, theirs = project(place, exchange(attended), weight, shares)
        arrived = lax.ppermute(theirs, "head", [(0, 1), (1, 0)])
        mixed_out = finish(own, arrived, residual, post_gain, chunk, mixed_out)
    return mixed_out


def group_pages(page_count, page_len):
    width = max(1, min(page_count, 2048 // page_len))
    while page_count % width:
        width -= 1
    return width


def attend_pages(running, grouped, key_pages, value_pages, valid_keys):
    page_count, page_len, kv_heads, head_dim = key_pages.shape
    tok_rows = valid_keys.shape[1]
    width = group_pages(page_count, page_len)
    groups = page_count // width
    key_groups = key_pages.reshape(groups, width * page_len, kv_heads, head_dim)
    value_groups = value_pages.reshape(groups, width * page_len, kv_heads, head_dim)
    valid_groups = (
        valid_keys.reshape(groups, width, tok_rows, page_len)
        .transpose(0, 2, 1, 3)
        .reshape(groups, tok_rows, width * page_len)
    )

    def compute(carry_in, key_block, value_block, valid_block):
        numerator, denominator = carry_in
        scores = (
            jnp.einsum("tkgd,skd->kgts", grouped, key_block, preferred_element_type=jnp.float32)
            * score_scale
        )
        capped = soft_cap * jnp.tanh(scores / soft_cap)
        weights = jnp.where(valid_block[None, None], jnp.exp(capped), 0.0).astype(jnp.bfloat16)
        numerator = numerator + jnp.einsum(
            "kgts,skd->tkgd", weights, value_block, preferred_element_type=jnp.float32
        )
        denominator = denominator + jnp.sum(weights.astype(jnp.float32), axis=-1)
        return (numerator, denominator)

    def one_group(carry_in, inputs):
        key_block, value_block, valid_block = inputs
        carry_out = compute(carry_in, key_block, value_block, valid_block)
        return (carry_out, None)

    result, _ = lax.scan(one_group, running, (key_groups, value_groups, valid_groups))
    return result


def shards(
    queries,
    new_keys,
    new_values,
    pool_keys,
    pool_values,
    page_table,
    cache_len,
    out_weight,
    residual,
    post_gain,
):
    req_count, per_req, heads_here, head_dim = queries.shape
    tok_dev = req_count * per_req
    kv_here = new_keys.shape[2]
    page_len = pool_keys.shape[1]
    slot_count = page_table.shape[1]
    blk_place = lax.axis_index("blk")
    row_ids = jnp.arange(tok_dev, dtype=jnp.int32)
    row_request = row_ids // per_req
    row_offset = blk_place * per_req + row_ids % per_req
    grouped = queries.reshape(tok_dev, kv_here, heads_here // kv_here, head_dim)
    page_rows = jnp.arange(page_len, dtype=jnp.int32)
    request_ids = jnp.arange(req_count, dtype=jnp.int32)
    row_onehot = row_request[:, None] == request_ids[None, :]
    start_carry = (
        jnp.zeros((tok_dev, kv_here, heads_here // kv_here, head_dim), jnp.float32),
        jnp.zeros((kv_here, heads_here // kv_here, tok_dev), jnp.float32),
    )
    pieces = (
        lax.all_gather(pool_keys, "blk", axis=0, tiled=True),
        lax.all_gather(pool_values, "blk", axis=0, tiled=True),
    )
    page_ids = jnp.arange(pieces[0].shape[0], dtype=jnp.int32)
    matches = page_ids[:, None, None] == page_table[None, :, :]
    slot_index = jnp.sum(
        jnp.where(matches, jnp.arange(slot_count, dtype=jnp.int32)[None, None, :], 0), axis=2
    )
    owned_page = jnp.any(matches, axis=2)
    position = slot_index[:, :, None] * page_len + page_rows[None, None, :]
    keep_keys = owned_page[:, :, None] & (position < cache_len[None, :, None])
    running = attend_pages(
        start_carry,
        grouped,
        pieces[0],
        pieces[1],
        jnp.any(keep_keys[:, None, :, :] & row_onehot[None, :, :, None], axis=2),
    )
    pieces = (
        lax.all_gather(new_keys, "blk", axis=1, tiled=True),
        lax.all_gather(new_values, "blk", axis=1, tiled=True),
    )
    piece_pages = pieces[0].shape[1] // page_len
    page_index = jnp.arange(req_count * piece_pages, dtype=jnp.int32)
    firsts = page_index % piece_pages * page_len
    key_pages = pieces[0].reshape(req_count * piece_pages, page_len, kv_here, head_dim)
    value_pages = pieces[1].reshape(req_count * piece_pages, page_len, kv_here, head_dim)
    offsets = firsts[:, None] + page_rows[None, :]
    same_request = (page_index // piece_pages)[:, None] == row_request[None, :]
    running = attend_pages(
        running,
        grouped,
        key_pages,
        value_pages,
        same_request[:, :, None] & (offsets[:, None, :] <= row_offset[None, :, None]),
    )
    numerator, denominator = running
    attended = (numerator / jnp.transpose(denominator, (2, 0, 1))[..., None]).astype(jnp.bfloat16)
    head_count = lax.axis_size("head")
    share = per_req // head_count
    feature_len = heads_here * head_dim
    attended = (
        attended.reshape(req_count, head_count, share, feature_len)
        .transpose(1, 0, 2, 3)
        .reshape(tok_dev, feature_len)
    )
    weight_rows = out_weight.reshape(feature_len, out_weight.shape[2])
    projected = lax.psum_scatter(
        jnp.dot(attended, weight_rows, preferred_element_type=jnp.float32).astype(jnp.bfloat16),
        "head",
        scatter_dimension=0,
        tiled=True,
    ).astype(jnp.float32)
    projected = projected.reshape(req_count, share, projected.shape[1])
    inv_rms = lax.rsqrt(jnp.mean(projected * projected, axis=-1, keepdims=True) + norm_eps)
    mixed_out = residual.astype(jnp.float32) + post_gain * projected * inv_rms
    return mixed_out.astype(jnp.bfloat16)


def solution(mesh):
    placed = (
        P(None, "blk", "head", None),
        P(None, "blk", "head", None),
        P(None, "blk", "head", None),
        P("blk", None, "head", None),
        P("blk", None, "head", None),
        P(),
        P(),
        P("head", None, None),
        P(None, ("blk", "head"), None),
        P(),
    )
    def one_device(queries, new_keys, *rest):
        requests, per_req = queries.shape[0], queries.shape[1]
        owners = mesh.shape["blk"] == 2 * new_keys.shape[2] and mesh.shape["head"] == 2 and requests == 2
        fits = rest[1].shape[1] == per_req == 128 and queries.shape[2] == 2 * new_keys.shape[2]
        return (by_heads if owners and fits else shards)(queries, new_keys, *rest)

    return jax.shard_map(
        one_device,
        mesh=mesh,
        in_specs=placed,
        out_specs=P(None, ("blk", "head"), None),
        check_vma=False,
    )
```

```python
import functools

import jax
import jax.numpy as jnp
from jax import lax
from jax.experimental import pallas as pl
from jax.experimental.pallas import tpu as pltpu
from jax.sharding import PartitionSpec as P

soft_cap = 50.0
score_scale = 144.0 ** (-0.5)
norm_eps = 1e-06
log2_e = 1.4426950408889634
chunks = 2
pieces = 2
key_tile = 256
mib = 1024 * 1024
in_vmem = pl.BlockSpec(memory_space=pltpu.VMEM)
in_hbm = pl.BlockSpec(memory_space=pltpu.HBM)
in_smem = pl.BlockSpec(memory_space=pltpu.SMEM)


def kernel_params(limit_mib):
    return pltpu.CompilerParams(vmem_limit_bytes=limit_mib * mib)


def split_heads(source, staged):
    rows, heads, head_dim = source.shape
    staged[0 : rows * heads, :] = source.reshape(rows * heads, head_dim).astype(jnp.float32)
    for head in range(heads):
        yield head, staged[pl.ds(head, rows, stride=heads), :].astype(jnp.bfloat16)


def pack_first_kernel(pool_k, pool_v, new_k, new_v, queries, out, held_kv, held_q, made, staged, in_sem, out_sem):
    pages = pool_k.shape[0]
    cores = new_k.shape[0]
    _, shares, _, rows, heads, head_dim = queries.shape
    group = heads // out.shape[0]
    tasks = []
    for core, pool in enumerate((pool_k, pool_v)):
        tasks += [(pool.at[page], core, page) for page in range(pages)]
    for part, new in enumerate((new_k, new_v)):
        tasks += [(new.at[core], core, pages + part) for core in range(cores)]
    arrivals = [pltpu.make_async_copy(source, held_kv.at[i], in_sem.at[i]) for i, (source, _, _) in enumerate(tasks)]
    for core in range(cores):
        at = len(tasks) + core
        arrivals.append(pltpu.make_async_copy(queries.at[core, :, 0], held_q.at[core], in_sem.at[at]))
    for arrival in arrivals:
        arrival.start()
    leaving = []

    def leave(core, part):
        here = made.at[:, core, part]
        leaving.append(pltpu.make_async_copy(here, out.at[:, core, part], out_sem.at[len(leaving)]))
        leaving[-1].start()

    for i, (_, core, part) in enumerate(tasks):
        arrivals[i].wait()
        for head, picked in split_heads(held_kv[i], staged.at[i % 2]):
            made[head, core, part] = picked
        leave(core, part)
    for core in range(cores):
        arrivals[len(tasks) + core].wait()
        source = held_q[core].reshape(shares * rows, heads, head_dim)
        for head, picked in split_heads(source, staged.at[core % 2]):
            first = head % group * shares * rows
            made[head // group, core, pages + 2, first : first + shares * rows, :] = picked
        leave(core, pages + 2)
    for copy in leaving:
        copy.wait()


def pack_first(pool_keys, pool_values, new_keys, new_values, queries):
    cores, rows, kv_heads, head_dim = new_keys.shape
    pages = pool_keys.shape[0]
    parts = pages + 3
    _, shares, _, chunk_rows, heads, _ = queries.shape
    pieces = 2 * pages + 2 * cores
    sources = [pltpu.with_memory_space_constraint(x, pltpu.HBM) for x in (pool_keys, pool_values, new_keys, new_values, queries)]
    return pl.pallas_call(
        pack_first_kernel,
        in_specs=[in_hbm] * 5,
        out_specs=in_hbm,
        out_shape=pltpu.HBM((kv_heads, cores, parts, rows, head_dim), jnp.bfloat16),
        scratch_shapes=[
            pltpu.VMEM((pieces, rows, kv_heads, head_dim), jnp.bfloat16),
            pltpu.VMEM((cores, shares, chunk_rows, heads, head_dim), jnp.bfloat16),
            pltpu.VMEM((kv_heads, cores, parts, rows, head_dim), jnp.bfloat16),
            pltpu.VMEM((2, max(rows * kv_heads, shares * chunk_rows * heads), head_dim), jnp.float32),
            pltpu.SemaphoreType.DMA((pieces + cores,)),
            pltpu.SemaphoreType.DMA((pieces + cores,)),
        ],
        compiler_params=kernel_params(10),
        cost_estimate=pl.CostEstimate(flops=0, bytes_accessed=6 * mib, transcendentals=0),
        name="pack_first",
    )(*sources)


def pack_queries(queries, kv_heads, chunk):
    steps, shares, _, rows, heads, head_dim = queries.shape
    group = heads // kv_heads

    def kernel(some_queries, out, staged):
        source = some_queries[...].reshape(shares * rows, heads, head_dim)
        for head, picked in split_heads(source, staged):
            first = head % group * shares * rows
            out[head // group, 0, 0, first : first + shares * rows, :] = picked

    return pl.pallas_call(
        kernel,
        grid=(steps,),
        in_specs=[pl.BlockSpec((1, shares, 1, rows, heads, head_dim), lambda i: (i, 0, chunk, 0, 0, 0))],
        out_specs=pl.BlockSpec((kv_heads, 1, 1, group * shares * rows, head_dim), lambda i: (0, i, 0, 0, 0)),
        out_shape=jax.ShapeDtypeStruct((kv_heads, steps, 1, group * shares * rows, head_dim), jnp.bfloat16),
        scratch_shapes=[pltpu.VMEM((shares * rows * heads, head_dim), jnp.float32)],
        compiler_params=kernel_params(6),
        cost_estimate=pl.CostEstimate(flops=0, bytes_accessed=mib, transcendentals=0),
        name="pack_queries",
    )(pltpu.with_memory_space_constraint(queries, pltpu.HBM))


def attend_kernel(pages, chunk, shares, core_ref, table_ref, len_ref, message, other, *rest):
    out, cache_k, cache_v, new_v, total, made, held, others, in_sem, other_sem, out_sem = rest[-11:]
    fetch = pltpu.make_async_copy(other.at[:, 0:pages], others, other_sem)
    fetch.start()
    queries, query_part = message, pages + 2
    if len(rest) > 11:
        queries, query_part = held, 0
        arrival = pltpu.make_async_copy(rest[0], held, in_sem)
        arrival.start()
    blocks, _, page_rows, head_dim = message.shape
    slots = table_ref.shape[1]
    group = out.shape[2] // head_dim
    block_rows = out.shape[1] * group
    core = core_ref[0]
    cached = len_ref[core]
    for block in range(blocks):
        new_v[block * page_rows : (block + 1) * page_rows, 0:head_dim] = message[block, pages + 1]
    new_v[:, head_dim : 2 * head_dim] = jnp.ones((blocks * page_rows, head_dim), jnp.bfloat16)
    fetch.wait()
    for slot in range(slots):
        page = table_ref[core, slot]
        mine = message[page // pages, page % pages]
        theirs = others[page // pages, page % pages]
        seen = slot * page_rows + lax.broadcasted_iota(jnp.int32, (page_rows, head_dim), 0) < cached
        here = pl.ds(slot * page_rows, page_rows)
        cache_k[here, :] = jnp.where(core == 0, mine, theirs)
        values = jnp.where(core == 0, theirs, mine).astype(jnp.float32)
        cache_v[here, 0:head_dim] = jnp.where(seen, values, 0.0).astype(jnp.bfloat16)
        cache_v[here, head_dim : 2 * head_dim] = jnp.where(seen, 1.0, 0.0).astype(jnp.bfloat16)
    if len(rest) > 11:
        arrival.wait()

    def add(first_block, block_count, keys, values, begin=False, causal=False):
        rows = block_count * block_rows
        query = queries[first_block : first_block + block_count, query_part].reshape(rows, head_dim)
        scores = lax.dot_general(query, keys, (((1,), (1,)), ((), ())), preferred_element_type=jnp.float32)
        weights = jnp.exp2((soft_cap * log2_e) * jnp.tanh(scores * (score_scale / soft_cap)))
        if causal:
            row = lax.broadcasted_iota(jnp.int32, weights.shape, 0)
            in_chunk = block_rows // (group * shares)
            offset = row // block_rows * page_rows + row // in_chunk % shares * (page_rows // shares)
            offset += chunk * in_chunk + row % in_chunk
            weights = jnp.where(lax.broadcasted_iota(jnp.int32, weights.shape, 1) <= offset, weights, 0.0)
        product = jnp.dot(weights.astype(jnp.bfloat16), values, preferred_element_type=jnp.float32)
        here = pl.ds(first_block * block_rows, rows)
        total[here, :] = product if begin else total[here, :] + product

    half = blocks // 2
    for first in (0, half):
        for tile in range(0, slots * page_rows, key_tile):
            add(first, half, cache_k[tile : tile + key_tile, :], cache_v[tile : tile + key_tile, :], begin=tile == 0)
    tile_blocks = key_tile // page_rows
    for block in range(0, blocks, tile_blocks):
        keys = message[block : block + tile_blocks, pages].reshape(key_tile, head_dim)
        values = new_v[block * page_rows : block * page_rows + key_tile, :]
        add(block, tile_blocks, keys, values, causal=True)
        later = block + tile_blocks
        while later < blocks:
            count = min(half, blocks - later)
            add(later, count, keys, values)
            later += count
    per_head = block_rows // group
    copies = []
    for block in range(blocks):
        here = pl.ds(block * block_rows, block_rows)
        attended = (total[here, 0:head_dim] / total[here, head_dim : 2 * head_dim]).astype(jnp.bfloat16)
        for head in range(group):
            made[block, :, head * head_dim : (head + 1) * head_dim] = attended[head * per_head : (head + 1) * per_head, :]
        if block % half == half - 1:
            here = pl.ds(block + 1 - half, half)
            copies.append(pltpu.make_async_copy(made.at[here], out.at[here], out_sem.at[len(copies)]))
            copies[-1].start()
    for copy in copies:
        copy.wait()


def attend(core, page_table, cache_len, message, other, queries, chunk, *, pages, shares, group):
    blocks, _, page_rows, head_dim = message.shape
    slots = page_table.shape[1]
    block_rows = page_rows * group // chunks
    operands = [message, pltpu.with_memory_space_constraint(other, pltpu.HBM)]
    specs = [in_smem] * 3 + [in_vmem, in_hbm]
    if queries is not None:
        operands.append(pltpu.with_memory_space_constraint(queries, pltpu.HBM))
        specs.append(in_hbm)
    seen = blocks * block_rows * (slots + blocks // 2) * page_rows
    return pl.pallas_call(
        functools.partial(attend_kernel, pages, chunk, shares),
        in_specs=specs,
        out_specs=in_hbm,
        out_shape=pltpu.HBM((blocks, block_rows // group, group * head_dim), jnp.bfloat16),
        scratch_shapes=[
            pltpu.VMEM((slots * page_rows, head_dim), jnp.bfloat16),
            pltpu.VMEM((slots * page_rows, 2 * head_dim), jnp.bfloat16),
            pltpu.VMEM((blocks * page_rows, 2 * head_dim), jnp.bfloat16),
            pltpu.VMEM((blocks * block_rows, 2 * head_dim), jnp.float32),
            pltpu.VMEM((blocks, block_rows // group, group * head_dim), jnp.bfloat16),
            pltpu.VMEM((blocks, 1, block_rows, head_dim) if len(operands) > 2 else (8, 128), jnp.bfloat16),
            pltpu.VMEM((blocks, pages, page_rows, head_dim), jnp.bfloat16),
            pltpu.SemaphoreType.DMA(()),
            pltpu.SemaphoreType.DMA(()),
            pltpu.SemaphoreType.DMA((2,)),
        ],
        compiler_params=kernel_params(12),
        cost_estimate=pl.CostEstimate(flops=8 * seen * head_dim, bytes_accessed=8 * mib, transcendentals=2 * seen),
        name="attend",
    )(core, page_table, cache_len, *operands)


def project_kernel(shares, begin, place_ref, attended, weight, own, theirs, rows, held, sem):
    tiles, _, tile = held.shape
    arrivals = []
    for i in range(tiles):
        columns = pl.ds(begin + i * tile, tile)
        arrivals.append(pltpu.make_async_copy(weight.at[:, columns], held.at[i], sem.at[i]))
        arrivals[-1].start()
    place = place_ref[0]
    sources, share_rows, features = attended.shape
    requests = 2
    count = share_rows // shares
    for source in range(sources):
        first = source // requests * features
        for share in range(shares):
            at = pl.multiple_of((share ^ place) * (requests * count), requests * count) + source % requests * count
            rows[pl.ds(at, count), first : first + features] = attended[source, share * count : (share + 1) * count, :]
    for i in range(tiles):
        arrivals[i].wait()
        product = jnp.dot(rows[...], held[i], preferred_element_type=jnp.float32)
        own[:, i * tile : (i + 1) * tile] = product[0 : requests * count, :]
        theirs[:, i * tile : (i + 1) * tile] = product[requests * count :, :].astype(jnp.bfloat16)


def project(place, attended, weight, shares, piece):
    sources, share_rows, features = attended.shape
    depth, width = weight.shape
    columns = width // pieces
    tile = columns // 3
    rows = 2 * share_rows
    return pl.pallas_call(
        functools.partial(project_kernel, shares, piece * columns),
        in_specs=[in_smem, in_vmem, in_hbm],
        out_specs=[in_vmem, in_vmem],
        out_shape=[
            jax.ShapeDtypeStruct((rows // shares, columns), jnp.float32),
            jax.ShapeDtypeStruct((rows // shares, columns), jnp.bfloat16),
        ],
        scratch_shapes=[
            pltpu.VMEM((rows, depth), jnp.bfloat16),
            pltpu.VMEM((columns // tile, depth, tile), jnp.bfloat16),
            pltpu.SemaphoreType.DMA((columns // tile,)),
        ],
        compiler_params=kernel_params(16),
        cost_estimate=pl.CostEstimate(flops=2 * rows * depth * columns, bytes_accessed=2 * depth * columns, transcendentals=0),
        name="project",
    )(place, attended, pltpu.with_memory_space_constraint(weight, pltpu.HBM))


def finish(own, arrived, residual, gain, chunk, earlier):
    requests, per_req, width = residual.shape
    rows = own[0].shape[0] // requests
    columns = width // pieces
    summed = [a + b.astype(jnp.float32) for a, b in zip(own[:-1], arrived[:-1])]

    def kernel(*refs):
        arrived_ref, residual_ref, gain_ref = refs[pieces : pieces + 3]
        out = refs[-1]
        projected = [ref[...] for ref in refs[0:pieces]]
        projected[-1] += arrived_ref[...].astype(jnp.float32)
        squares = sum(jnp.sum(x * x, axis=-1, keepdims=True) for x in projected)
        inv_rms = lax.rsqrt(squares / width + norm_eps)
        for i, x in enumerate(projected):
            here = slice(i * columns, (i + 1) * columns)
            mixed = residual_ref[0, :, here].astype(jnp.float32) + gain_ref[:, here] * x * inv_rms
            out[0, :, here] = mixed.astype(jnp.bfloat16)

    some = pl.BlockSpec((rows, columns), lambda i: (i, 0))
    place = pl.BlockSpec((1, rows, width), lambda i: (i, chunk, 0))
    operands = [*summed, own[-1], arrived[-1], residual, gain.reshape(1, width)]
    specs = [some] * (pieces + 1) + [place, pl.BlockSpec((1, width), lambda i: (0, 0))]
    if earlier is not None:
        operands.append(earlier)
        specs.append(pl.BlockSpec(memory_space=pl.ANY))
    return pl.pallas_call(
        kernel,
        grid=(requests,),
        in_specs=specs,
        out_specs=place,
        out_shape=jax.ShapeDtypeStruct(residual.shape, jnp.bfloat16),
        input_output_aliases={} if earlier is None else {len(operands) - 1: 0},
        compiler_params=kernel_params(8),
        cost_estimate=pl.CostEstimate(flops=0, bytes_accessed=4 * mib, transcendentals=0),
        name="finish",
    )(*operands)


def by_heads(
    queries,
    new_keys,
    new_values,
    pool_keys,
    pool_values,
    page_table,
    cache_len,
    out_weight,
    residual,
    post_gain,
):
    req_count, per_req, heads_here, head_dim = queries.shape
    kv_here = new_keys.shape[2]
    pages = pool_keys.shape[0]
    blk_count = lax.axis_size("blk")
    shares = lax.axis_size("head")
    group = heads_here // kv_here
    core = (lax.axis_index("blk") % 2)[None]
    place = lax.axis_index("head")[None]
    weight = out_weight.reshape(heads_here * head_dim, out_weight.shape[2])
    queries = queries.reshape(req_count, shares, chunks, per_req // (shares * chunks), heads_here, head_dim)
    exchange = functools.partial(lax.all_to_all, axis_name="blk", split_axis=0, concat_axis=0, tiled=True)
    message = pack_first(pool_keys, pool_values, new_keys, new_values, queries)
    message = exchange(message.reshape(blk_count, pages + 3, per_req, head_dim))
    packed = pack_queries(queries, kv_here, 1)
    message, packed = lax.optimization_barrier((message, packed))
    asked = exchange(packed.reshape((blk_count,) + packed.shape[2:]))
    other = lax.ppermute(message, "blk", [(i, i ^ 1) for i in range(blk_count)])
    attend_chunk = functools.partial(attend, core, page_table, cache_len, message, other, pages=pages, shares=shares, group=group)

    def project_piece(gathered, piece):
        own, theirs = project(place, gathered, weight, shares, piece)
        return own, lax.ppermute(theirs, "head", [(0, 1), (1, 0)])

    first = attend_chunk(None, 0)
    first, asked = lax.optimization_barrier((first, asked))
    first = exchange(first)
    second = attend_chunk(asked, 1)
    first, second = lax.optimization_barrier((first, second))
    second = exchange(second)
    own, arrived = zip(*[project_piece(first, piece) for piece in range(pieces)])
    own, second = lax.optimization_barrier((own, second))
    begun = project_piece(second, 0)
    mixed_out = finish(own, arrived, residual, post_gain, 0, None)
    second, mixed_out = lax.optimization_barrier((second, mixed_out))
    own, arrived = zip(begun, *[project_piece(second, piece) for piece in range(1, pieces)])
    return finish(own, arrived, residual, post_gain, 1, mixed_out)


def group_pages(page_count, page_len):
    width = max(1, min(page_count, 2048 // page_len))
    while page_count % width:
        width -= 1
    return width


def attend_pages(running, grouped, key_pages, value_pages, valid_keys):
    page_count, page_len, kv_heads, head_dim = key_pages.shape
    tok_rows = valid_keys.shape[1]
    width = group_pages(page_count, page_len)
    groups = page_count // width
    key_groups = key_pages.reshape(groups, width * page_len, kv_heads, head_dim)
    value_groups = value_pages.reshape(groups, width * page_len, kv_heads, head_dim)
    valid_groups = (
        valid_keys.reshape(groups, width, tok_rows, page_len)
        .transpose(0, 2, 1, 3)
        .reshape(groups, tok_rows, width * page_len)
    )

    def compute(carry_in, key_block, value_block, valid_block):
        numerator, denominator = carry_in
        scores = (
            jnp.einsum("tkgd,skd->kgts", grouped, key_block, preferred_element_type=jnp.float32)
            * score_scale
        )
        capped = soft_cap * jnp.tanh(scores / soft_cap)
        weights = jnp.where(valid_block[None, None], jnp.exp(capped), 0.0).astype(jnp.bfloat16)
        numerator = numerator + jnp.einsum(
            "kgts,skd->tkgd", weights, value_block, preferred_element_type=jnp.float32
        )
        denominator = denominator + jnp.sum(weights.astype(jnp.float32), axis=-1)
        return (numerator, denominator)

    def one_group(carry_in, inputs):
        key_block, value_block, valid_block = inputs
        carry_out = compute(carry_in, key_block, value_block, valid_block)
        return (carry_out, None)

    result, _ = lax.scan(one_group, running, (key_groups, value_groups, valid_groups))
    return result


def shards(
    queries,
    new_keys,
    new_values,
    pool_keys,
    pool_values,
    page_table,
    cache_len,
    out_weight,
    residual,
    post_gain,
):
    req_count, per_req, heads_here, head_dim = queries.shape
    tok_dev = req_count * per_req
    kv_here = new_keys.shape[2]
    page_len = pool_keys.shape[1]
    slot_count = page_table.shape[1]
    blk_place = lax.axis_index("blk")
    row_ids = jnp.arange(tok_dev, dtype=jnp.int32)
    row_request = row_ids // per_req
    row_offset = blk_place * per_req + row_ids % per_req
    grouped = queries.reshape(tok_dev, kv_here, heads_here // kv_here, head_dim)
    page_rows = jnp.arange(page_len, dtype=jnp.int32)
    request_ids = jnp.arange(req_count, dtype=jnp.int32)
    row_onehot = row_request[:, None] == request_ids[None, :]
    start_carry = (
        jnp.zeros((tok_dev, kv_here, heads_here // kv_here, head_dim), jnp.float32),
        jnp.zeros((kv_here, heads_here // kv_here, tok_dev), jnp.float32),
    )
    pieces = (
        lax.all_gather(pool_keys, "blk", axis=0, tiled=True),
        lax.all_gather(pool_values, "blk", axis=0, tiled=True),
    )
    page_ids = jnp.arange(pieces[0].shape[0], dtype=jnp.int32)
    matches = page_ids[:, None, None] == page_table[None, :, :]
    slot_index = jnp.sum(
        jnp.where(matches, jnp.arange(slot_count, dtype=jnp.int32)[None, None, :], 0), axis=2
    )
    owned_page = jnp.any(matches, axis=2)
    position = slot_index[:, :, None] * page_len + page_rows[None, None, :]
    keep_keys = owned_page[:, :, None] & (position < cache_len[None, :, None])
    running = attend_pages(
        start_carry,
        grouped,
        pieces[0],
        pieces[1],
        jnp.any(keep_keys[:, None, :, :] & row_onehot[None, :, :, None], axis=2),
    )
    pieces = (
        lax.all_gather(new_keys, "blk", axis=1, tiled=True),
        lax.all_gather(new_values, "blk", axis=1, tiled=True),
    )
    piece_pages = pieces[0].shape[1] // page_len
    page_index = jnp.arange(req_count * piece_pages, dtype=jnp.int32)
    firsts = page_index % piece_pages * page_len
    key_pages = pieces[0].reshape(req_count * piece_pages, page_len, kv_here, head_dim)
    value_pages = pieces[1].reshape(req_count * piece_pages, page_len, kv_here, head_dim)
    offsets = firsts[:, None] + page_rows[None, :]
    same_request = (page_index // piece_pages)[:, None] == row_request[None, :]
    running = attend_pages(
        running,
        grouped,
        key_pages,
        value_pages,
        same_request[:, :, None] & (offsets[:, None, :] <= row_offset[None, :, None]),
    )
    numerator, denominator = running
    attended = (numerator / jnp.transpose(denominator, (2, 0, 1))[..., None]).astype(jnp.bfloat16)
    head_count = lax.axis_size("head")
    share = per_req // head_count
    feature_len = heads_here * head_dim
    attended = (
        attended.reshape(req_count, head_count, share, feature_len)
        .transpose(1, 0, 2, 3)
        .reshape(tok_dev, feature_len)
    )
    weight_rows = out_weight.reshape(feature_len, out_weight.shape[2])
    projected = lax.psum_scatter(
        jnp.dot(attended, weight_rows, preferred_element_type=jnp.float32).astype(jnp.bfloat16),
        "head",
        scatter_dimension=0,
        tiled=True,
    ).astype(jnp.float32)
    projected = projected.reshape(req_count, share, projected.shape[1])
    inv_rms = lax.rsqrt(jnp.mean(projected * projected, axis=-1, keepdims=True) + norm_eps)
    mixed_out = residual.astype(jnp.float32) + post_gain * projected * inv_rms
    return mixed_out.astype(jnp.bfloat16)


def solution(mesh):
    placed = (
        P(None, "blk", "head", None),
        P(None, "blk", "head", None),
        P(None, "blk", "head", None),
        P("blk", None, "head", None),
        P("blk", None, "head", None),
        P(),
        P(),
        P("head", None, None),
        P(None, ("blk", "head"), None),
        P(),
    )
    def one_device(queries, new_keys, *rest):
        requests, per_req = queries.shape[0], queries.shape[1]
        owners = mesh.shape["blk"] == 2 * new_keys.shape[2] and mesh.shape["head"] == 2 and requests == 2
        fits = rest[1].shape[1] == per_req == 128 and queries.shape[2] == 2 * new_keys.shape[2]
        return (by_heads if owners and fits else shards)(queries, new_keys, *rest)

    return jax.shard_map(
        one_device,
        mesh=mesh,
        in_specs=placed,
        out_specs=P(None, ("blk", "head"), None),
        check_vma=False,
    )
```

```python
import functools

import jax
import jax.numpy as jnp
from jax import lax
from jax.experimental import pallas as pl
from jax.experimental.pallas import tpu as pltpu
from jax.sharding import PartitionSpec as P

soft_cap = 50.0
score_scale = 144.0 ** (-0.5)
norm_eps = 1e-06
log2_e = 1.4426950408889634
key_tile = 256
mib = 1024 * 1024
in_vmem = pl.BlockSpec(memory_space=pltpu.VMEM)
in_hbm = pl.BlockSpec(memory_space=pltpu.HBM)
in_smem = pl.BlockSpec(memory_space=pltpu.SMEM)


def kernel_params(limit_mib):
    return pltpu.CompilerParams(vmem_limit_bytes=limit_mib * mib)


def split_heads(source, staged):
    rows, heads, head_dim = source.shape
    staged[0 : rows * heads, :] = source.reshape(rows * heads, head_dim).astype(jnp.float32)
    for head in range(heads):
        yield head, staged[pl.ds(head, rows, stride=heads), :].astype(jnp.bfloat16)


def pack_kernel(share_ref, *refs):
    *caches, queries, out, held_kv, held_q, made, staged, in_sem, out_sem = refs
    cores, _, rows, heads, head_dim = queries.shape
    group = heads // out.shape[0]
    tasks = []
    if caches:
        pool_k, pool_v, new_k, new_v = caches
        pages = pool_k.shape[0]
        for core, pool in enumerate((pool_k, pool_v)):
            tasks += [(pool.at[page], core, page) for page in range(pages)]
        for part, new in enumerate((new_k, new_v)):
            tasks += [(new.at[core], core, pages + part) for core in range(cores)]
    arrivals = [pltpu.make_async_copy(source, held_kv.at[i], in_sem.at[i]) for i, (source, _, _) in enumerate(tasks)]
    for core in range(cores):
        source = queries.at[core, share_ref[0]]
        arrivals.append(pltpu.make_async_copy(source, held_q.at[core], in_sem.at[len(tasks) + core]))
    for arrival in arrivals:
        arrival.start()
    leaving = []

    def leave(core, part):
        leaving.append(pltpu.make_async_copy(made.at[:, core, part], out.at[:, core, part], out_sem.at[len(leaving)]))
        leaving[-1].start()

    for i, (_, core, part) in enumerate(tasks):
        arrivals[i].wait()
        for head, picked in split_heads(held_kv[i], staged.at[i % 2]):
            made[head, core, part] = picked
        leave(core, part)
    last = out.shape[2] - 1
    for core in range(cores):
        arrivals[len(tasks) + core].wait()
        for head, picked in split_heads(held_q[core], staged.at[core % 2]):
            first = head % group * rows
            made[head // group, core, last, first : first + rows, :] = picked
        leave(core, last)
    for copy in leaving:
        copy.wait()


def pack(share, queries, kv_heads, caches=()):
    cores, _, rows, heads, head_dim = queries.shape
    group = heads // kv_heads
    parts, pieces, page_rows = 1, 0, group * rows
    if caches:
        pages = caches[0].shape[0]
        parts, pieces = pages + 3, 2 * pages + 2 * cores
    shape = (kv_heads, cores, parts, page_rows, head_dim)
    operands = [pltpu.with_memory_space_constraint(x, pltpu.HBM) for x in (*caches, queries)]
    return pl.pallas_call(
        pack_kernel,
        in_specs=[in_smem] + [in_hbm] * len(operands),
        out_specs=in_hbm,
        out_shape=pltpu.HBM(shape, jnp.bfloat16),
        scratch_shapes=[
            pltpu.VMEM((max(pieces, 1), page_rows, kv_heads, head_dim), jnp.bfloat16),
            pltpu.VMEM((cores, rows, heads, head_dim), jnp.bfloat16),
            pltpu.VMEM(shape, jnp.bfloat16),
            pltpu.VMEM((2, rows * heads, head_dim), jnp.float32),
            pltpu.SemaphoreType.DMA((pieces + cores,)),
            pltpu.SemaphoreType.DMA((pieces + cores,)),
        ],
        compiler_params=kernel_params(12 if caches else 6),
        cost_estimate=pl.CostEstimate(flops=0, bytes_accessed=parts * mib, transcendentals=0),
        name="pack_cache" if caches else "pack_queries",
    )(share, *operands)


def attend_kernel(pages, core_ref, share_ref, table_ref, len_ref, message, other, *rest):
    out, cache_k, cache_v, new_v, total, made, held, others, in_sem, other_sem, out_sem = rest[-11:]
    fetch = pltpu.make_async_copy(other.at[:, 0:pages], others, other_sem)
    fetch.start()
    queries, query_part = message, pages + 2
    if len(rest) > 11:
        queries, query_part = held, 0
        arrival = pltpu.make_async_copy(rest[0], held, in_sem)
        arrival.start()
    blocks, _, page_rows, head_dim = message.shape
    slots = table_ref.shape[1]
    group = out.shape[2] // head_dim
    per_head = out.shape[1]
    block_rows = per_head * group
    core = core_ref[0]
    cached = len_ref[core]
    for block in range(blocks):
        new_v[block * page_rows : (block + 1) * page_rows, 0:head_dim] = message[block, pages + 1]
    new_v[:, head_dim : 2 * head_dim] = jnp.ones((blocks * page_rows, head_dim), jnp.bfloat16)
    fetch.wait()
    for slot in range(slots):
        page = table_ref[core, slot]
        mine = message[page // pages, page % pages]
        theirs = others[page // pages, page % pages]
        seen = slot * page_rows + lax.broadcasted_iota(jnp.int32, (page_rows, head_dim), 0) < cached
        here = pl.ds(slot * page_rows, page_rows)
        cache_k[here, :] = jnp.where(core == 0, mine, theirs)
        values = jnp.where(core == 0, theirs, mine).astype(jnp.float32)
        cache_v[here, 0:head_dim] = jnp.where(seen, values, 0.0).astype(jnp.bfloat16)
        cache_v[here, head_dim : 2 * head_dim] = jnp.where(seen, 1.0, 0.0).astype(jnp.bfloat16)
    if len(rest) > 11:
        arrival.wait()

    def add(first_block, block_count, keys, values, begin=False, causal=False):
        rows = block_count * block_rows
        query = queries[first_block : first_block + block_count, query_part].reshape(rows, head_dim)
        scores = lax.dot_general(query, keys, (((1,), (1,)), ((), ())), preferred_element_type=jnp.float32)
        weights = jnp.exp2((soft_cap * log2_e) * jnp.tanh(scores * (score_scale / soft_cap)))
        if causal:
            row = lax.broadcasted_iota(jnp.int32, weights.shape, 0)
            offset = row // block_rows * page_rows + row % per_head + share_ref[0] * per_head
            weights = jnp.where(lax.broadcasted_iota(jnp.int32, weights.shape, 1) <= offset, weights, 0.0)
        product = jnp.dot(weights.astype(jnp.bfloat16), values, preferred_element_type=jnp.float32)
        here = pl.ds(first_block * block_rows, rows)
        total[here, :] = product if begin else total[here, :] + product

    half = blocks // 2
    for first in (0, half):
        for tile in range(0, slots * page_rows, key_tile):
            add(first, half, cache_k[tile : tile + key_tile, :], cache_v[tile : tile + key_tile, :], begin=tile == 0)
    tile_blocks = key_tile // page_rows
    for block in range(0, blocks, tile_blocks):
        keys = message[block : block + tile_blocks, pages].reshape(key_tile, head_dim)
        values = new_v[block * page_rows : block * page_rows + key_tile, :]
        add(block, tile_blocks, keys, values, causal=True)
        later = block + tile_blocks
        while later < blocks:
            count = min(half, blocks - later)
            add(later, count, keys, values)
            later += count
    copies = []
    for block in range(blocks):
        here = pl.ds(block * block_rows, block_rows)
        attended = (total[here, 0:head_dim] / total[here, head_dim : 2 * head_dim]).astype(jnp.bfloat16)
        for head in range(group):
            made[block, :, head * head_dim : (head + 1) * head_dim] = attended[head * per_head : (head + 1) * per_head, :]
        if block % half == half - 1:
            here = pl.ds(block + 1 - half, half)
            copies.append(pltpu.make_async_copy(made.at[here], out.at[here], out_sem.at[len(copies)]))
            copies[-1].start()
    for copy in copies:
        copy.wait()


def attend(core, page_table, cache_len, message, other, queries, share, *, pages, group):
    blocks, _, page_rows, head_dim = message.shape
    slots = page_table.shape[1]
    block_rows = page_rows
    operands = [message, pltpu.with_memory_space_constraint(other, pltpu.HBM)]
    specs = [in_smem] * 4 + [in_vmem, in_hbm]
    if queries is not None:
        operands.append(pltpu.with_memory_space_constraint(queries, pltpu.HBM))
        specs.append(in_hbm)
    seen = blocks * block_rows * (slots + blocks // 2) * page_rows
    return pl.pallas_call(
        functools.partial(attend_kernel, pages),
        in_specs=specs,
        out_specs=in_hbm,
        out_shape=pltpu.HBM((blocks, block_rows // group, group * head_dim), jnp.bfloat16),
        scratch_shapes=[
            pltpu.VMEM((slots * page_rows, head_dim), jnp.bfloat16),
            pltpu.VMEM((slots * page_rows, 2 * head_dim), jnp.bfloat16),
            pltpu.VMEM((blocks * page_rows, 2 * head_dim), jnp.bfloat16),
            pltpu.VMEM((blocks * block_rows, 2 * head_dim), jnp.float32),
            pltpu.VMEM((blocks, block_rows // group, group * head_dim), jnp.bfloat16),
            pltpu.VMEM((blocks, 1, block_rows, head_dim) if len(operands) > 2 else (8, 128), jnp.bfloat16),
            pltpu.VMEM((blocks, pages, page_rows, head_dim), jnp.bfloat16),
            pltpu.SemaphoreType.DMA(()),
            pltpu.SemaphoreType.DMA(()),
            pltpu.SemaphoreType.DMA((2,)),
        ],
        compiler_params=kernel_params(12),
        cost_estimate=pl.CostEstimate(flops=8 * seen * head_dim, bytes_accessed=8 * mib, transcendentals=2 * seen),
        name="attend",
    )(core, share, page_table, cache_len, *operands)


def project_kernel(begin, attended, weight, *refs):
    (*arrived, out), (rows, held, sem) = refs[:-3], refs[-3:]
    if arrived:
        *arrived, out, squares_out = (*arrived, out)
    tiles, _, tile = held.shape
    arrivals = []
    for i in range(tiles):
        columns = pl.ds(begin + i * tile, tile)
        arrivals.append(pltpu.make_async_copy(weight.at[:, columns], held.at[i], sem.at[i]))
        arrivals[-1].start()
    sources, count, features = attended.shape
    requests = rows.shape[0] // count
    for source in range(sources):
        at, first = source % requests * count, source // requests * features
        rows[at : at + count, first : first + features] = attended[source]
    squares = 0.0
    for i in range(tiles):
        here = slice(i * tile, (i + 1) * tile)
        arrivals[i].wait()
        product = jnp.dot(rows[...], held[i], preferred_element_type=jnp.float32)
        at = i * tile
        for piece in arrived:
            if 0 <= at < piece.shape[1]:
                product += piece[:, at : at + tile].astype(jnp.float32)
                squares += squares_by_lane(product)
            at -= piece.shape[1]
        out[:, here] = product.astype(out.dtype)
    if arrived:
        squares_out[...] = squares


def squares_by_lane(x):
    return sum(x[:, i : i + 128] * x[:, i : i + 128] for i in range(0, x.shape[1], 128))


def project(attended, weight, requests, begin, columns, tile, dtype, arrived=()):
    sources, count, features = attended.shape
    depth = weight.shape[0]
    rows = requests * count
    operands = [attended, pltpu.with_memory_space_constraint(weight, pltpu.HBM)]
    outs = [jax.ShapeDtypeStruct((rows, columns), dtype)]
    if arrived:
        operands += arrived
        outs.append(jax.ShapeDtypeStruct((rows, 128), jnp.float32))
    return pl.pallas_call(
        functools.partial(project_kernel, begin),
        in_specs=[in_vmem, in_hbm] + [in_vmem] * (len(operands) - 2),
        out_specs=[in_vmem] * len(outs),
        out_shape=outs,
        scratch_shapes=[
            pltpu.VMEM((rows, depth), jnp.bfloat16),
            pltpu.VMEM((columns // tile, depth, tile), jnp.bfloat16),
            pltpu.SemaphoreType.DMA((columns // tile,)),
        ],
        compiler_params=kernel_params(6 + 2 * depth * columns // mib),
        cost_estimate=pl.CostEstimate(flops=2 * rows * depth * columns, bytes_accessed=2 * depth * columns, transcendentals=0),
        name="project",
    )(*operands)


def finish_kernel(projected, squares_ref, arrived, residual, gain, out, made, sem):
    requests, count, width = residual.shape
    rows = made.shape[1]
    split = width - arrived.shape[1]
    copies = []
    for step in range(made.shape[0]):
        request, first = step * rows // count, step * rows % count
        here = slice(step * rows, (step + 1) * rows)
        place = slice(first, first + rows)
        last = projected[here, split:] + arrived[here, :].astype(jnp.float32)
        squares = jnp.sum(squares_ref[here, :] + squares_by_lane(last), axis=-1, keepdims=True)
        inv_rms = lax.rsqrt(squares / width + norm_eps)
        for columns, x in ((slice(0, split), projected[here, 0:split]), (slice(split, width), last)):
            mixed = residual[request, place, columns].astype(jnp.float32) + gain[:, columns] * x * inv_rms
            made[step, :, columns] = mixed.astype(jnp.bfloat16)
        copies.append(pltpu.make_async_copy(made.at[step], out.at[request, place], sem.at[step]))
        copies[-1].start()
    for copy in copies:
        copy.wait()


def finish(projected, squares, arrived, residual, gain):
    requests, count, width = residual.shape
    rows = 32
    steps = requests * count // rows
    return pl.pallas_call(
        finish_kernel,
        in_specs=[in_vmem] * 5,
        out_specs=in_hbm,
        out_shape=pltpu.HBM(residual.shape, jnp.bfloat16),
        scratch_shapes=[pltpu.VMEM((steps, rows, width), jnp.bfloat16), pltpu.SemaphoreType.DMA((steps,))],
        compiler_params=kernel_params(12),
        cost_estimate=pl.CostEstimate(flops=0, bytes_accessed=6 * mib, transcendentals=0),
        name="finish",
    )(projected, squares, arrived, residual, gain.reshape(1, width))


def by_heads(
    queries,
    new_keys,
    new_values,
    pool_keys,
    pool_values,
    page_table,
    cache_len,
    out_weight,
    residual,
    post_gain,
):
    req_count, per_req, heads_here, head_dim = queries.shape
    kv_here = new_keys.shape[2]
    pages = pool_keys.shape[0]
    blk_count = lax.axis_size("blk")
    shares = lax.axis_size("head")
    group = heads_here // kv_here
    core = (lax.axis_index("blk") % 2)[None]
    mine = lax.axis_index("head")[None]
    theirs = 1 - mine
    width = out_weight.shape[2]
    weight = out_weight.reshape(heads_here * head_dim, width)
    queries = queries.reshape(req_count, shares, per_req // shares, heads_here, head_dim)
    exchange = functools.partial(lax.all_to_all, axis_name="blk", split_axis=0, concat_axis=0, tiled=True)
    message = pack(theirs, queries, kv_here, (pool_keys, pool_values, new_keys, new_values))
    message = exchange(message.reshape((blk_count,) + message.shape[2:]))
    packed = pack(mine, queries, kv_here)
    message, packed = lax.optimization_barrier((message, packed))
    asked = exchange(packed.reshape((blk_count,) + packed.shape[2:]))
    other = lax.ppermute(message, "blk", [(i, i ^ 1) for i in range(blk_count)])
    attend_share = functools.partial(attend, core, page_table, cache_len, message, other, pages=pages, group=group)

    first = attend_share(None, theirs)
    first, asked = lax.optimization_barrier((first, asked))
    first = exchange(first)
    second = attend_share(asked, mine)
    first, second = lax.optimization_barrier((first, second))
    tile = width // 9
    begin = 0
    arrived = []
    for piece, tiles in enumerate((2, 3, 4)):
        if piece == 2:
            first, arrived[0] = lax.optimization_barrier((first, arrived[0]))
        (sent,) = project(first, weight, req_count, begin, tiles * tile, tile, jnp.bfloat16)
        begin += tiles * tile
        if piece == 0:
            sent, second = lax.optimization_barrier((sent, second))
            second = exchange(second)
        else:
            first, sent = lax.optimization_barrier((first, sent))
        arrived.append(lax.ppermute(sent, "head", [(0, 1), (1, 0)]))
    projected, squares = project(second, weight, req_count, 0, width, tile, jnp.float32, arrived[:2])
    return finish(projected, squares, arrived[2], residual, post_gain)


def group_pages(page_count, page_len):
    width = max(1, min(page_count, 2048 // page_len))
    while page_count % width:
        width -= 1
    return width


def attend_pages(running, grouped, key_pages, value_pages, valid_keys):
    page_count, page_len, kv_heads, head_dim = key_pages.shape
    tok_rows = valid_keys.shape[1]
    width = group_pages(page_count, page_len)
    groups = page_count // width
    key_groups = key_pages.reshape(groups, width * page_len, kv_heads, head_dim)
    value_groups = value_pages.reshape(groups, width * page_len, kv_heads, head_dim)
    valid_groups = (
        valid_keys.reshape(groups, width, tok_rows, page_len)
        .transpose(0, 2, 1, 3)
        .reshape(groups, tok_rows, width * page_len)
    )

    def compute(carry_in, key_block, value_block, valid_block):
        numerator, denominator = carry_in
        scores = (
            jnp.einsum("tkgd,skd->kgts", grouped, key_block, preferred_element_type=jnp.float32)
            * score_scale
        )
        capped = soft_cap * jnp.tanh(scores / soft_cap)
        weights = jnp.where(valid_block[None, None], jnp.exp(capped), 0.0).astype(jnp.bfloat16)
        numerator = numerator + jnp.einsum(
            "kgts,skd->tkgd", weights, value_block, preferred_element_type=jnp.float32
        )
        denominator = denominator + jnp.sum(weights.astype(jnp.float32), axis=-1)
        return (numerator, denominator)

    def one_group(carry_in, inputs):
        key_block, value_block, valid_block = inputs
        carry_out = compute(carry_in, key_block, value_block, valid_block)
        return (carry_out, None)

    result, _ = lax.scan(one_group, running, (key_groups, value_groups, valid_groups))
    return result


def shards(
    queries,
    new_keys,
    new_values,
    pool_keys,
    pool_values,
    page_table,
    cache_len,
    out_weight,
    residual,
    post_gain,
):
    req_count, per_req, heads_here, head_dim = queries.shape
    tok_dev = req_count * per_req
    kv_here = new_keys.shape[2]
    page_len = pool_keys.shape[1]
    slot_count = page_table.shape[1]
    blk_place = lax.axis_index("blk")
    row_ids = jnp.arange(tok_dev, dtype=jnp.int32)
    row_request = row_ids // per_req
    row_offset = blk_place * per_req + row_ids % per_req
    grouped = queries.reshape(tok_dev, kv_here, heads_here // kv_here, head_dim)
    page_rows = jnp.arange(page_len, dtype=jnp.int32)
    request_ids = jnp.arange(req_count, dtype=jnp.int32)
    row_onehot = row_request[:, None] == request_ids[None, :]
    start_carry = (
        jnp.zeros((tok_dev, kv_here, heads_here // kv_here, head_dim), jnp.float32),
        jnp.zeros((kv_here, heads_here // kv_here, tok_dev), jnp.float32),
    )
    pieces = (
        lax.all_gather(pool_keys, "blk", axis=0, tiled=True),
        lax.all_gather(pool_values, "blk", axis=0, tiled=True),
    )
    page_ids = jnp.arange(pieces[0].shape[0], dtype=jnp.int32)
    matches = page_ids[:, None, None] == page_table[None, :, :]
    slot_index = jnp.sum(
        jnp.where(matches, jnp.arange(slot_count, dtype=jnp.int32)[None, None, :], 0), axis=2
    )
    owned_page = jnp.any(matches, axis=2)
    position = slot_index[:, :, None] * page_len + page_rows[None, None, :]
    keep_keys = owned_page[:, :, None] & (position < cache_len[None, :, None])
    running = attend_pages(
        start_carry,
        grouped,
        pieces[0],
        pieces[1],
        jnp.any(keep_keys[:, None, :, :] & row_onehot[None, :, :, None], axis=2),
    )
    pieces = (
        lax.all_gather(new_keys, "blk", axis=1, tiled=True),
        lax.all_gather(new_values, "blk", axis=1, tiled=True),
    )
    piece_pages = pieces[0].shape[1] // page_len
    page_index = jnp.arange(req_count * piece_pages, dtype=jnp.int32)
    firsts = page_index % piece_pages * page_len
    key_pages = pieces[0].reshape(req_count * piece_pages, page_len, kv_here, head_dim)
    value_pages = pieces[1].reshape(req_count * piece_pages, page_len, kv_here, head_dim)
    offsets = firsts[:, None] + page_rows[None, :]
    same_request = (page_index // piece_pages)[:, None] == row_request[None, :]
    running = attend_pages(
        running,
        grouped,
        key_pages,
        value_pages,
        same_request[:, :, None] & (offsets[:, None, :] <= row_offset[None, :, None]),
    )
    numerator, denominator = running
    attended = (numerator / jnp.transpose(denominator, (2, 0, 1))[..., None]).astype(jnp.bfloat16)
    head_count = lax.axis_size("head")
    share = per_req // head_count
    feature_len = heads_here * head_dim
    attended = (
        attended.reshape(req_count, head_count, share, feature_len)
        .transpose(1, 0, 2, 3)
        .reshape(tok_dev, feature_len)
    )
    weight_rows = out_weight.reshape(feature_len, out_weight.shape[2])
    projected = lax.psum_scatter(
        jnp.dot(attended, weight_rows, preferred_element_type=jnp.float32).astype(jnp.bfloat16),
        "head",
        scatter_dimension=0,
        tiled=True,
    ).astype(jnp.float32)
    projected = projected.reshape(req_count, share, projected.shape[1])
    inv_rms = lax.rsqrt(jnp.mean(projected * projected, axis=-1, keepdims=True) + norm_eps)
    mixed_out = residual.astype(jnp.float32) + post_gain * projected * inv_rms
    return mixed_out.astype(jnp.bfloat16)


def solution(mesh):
    placed = (
        P(None, "blk", "head", None),
        P(None, "blk", "head", None),
        P(None, "blk", "head", None),
        P("blk", None, "head", None),
        P("blk", None, "head", None),
        P(),
        P(),
        P("head", None, None),
        P(None, ("blk", "head"), None),
        P(),
    )
    def one_device(queries, new_keys, *rest):
        requests, per_req = queries.shape[0], queries.shape[1]
        owners = mesh.shape["blk"] == 2 * new_keys.shape[2] and mesh.shape["head"] == 2 and requests == 2
        fits = rest[1].shape[1] == per_req == 128 and queries.shape[2] == 2 * new_keys.shape[2]
        return (by_heads if owners and fits else shards)(queries, new_keys, *rest)

    return jax.shard_map(
        one_device,
        mesh=mesh,
        in_specs=placed,
        out_specs=P(None, ("blk", "head"), None),
        check_vma=False,
    )
```

```python
import functools

import jax
import jax.numpy as jnp
from jax import lax
from jax.experimental import pallas as pl
from jax.experimental.pallas import tpu as pltpu
from jax.sharding import PartitionSpec as P

soft_cap = 50.0
score_scale = 144.0 ** (-0.5)
norm_eps = 1e-06
log2_e = 1.4426950408889634
key_tile = 256
mib = 1024 * 1024
in_vmem = pl.BlockSpec(memory_space=pltpu.VMEM)
in_hbm = pl.BlockSpec(memory_space=pltpu.HBM)
in_smem = pl.BlockSpec(memory_space=pltpu.SMEM)


def kernel_params(limit_mib):
    return pltpu.CompilerParams(vmem_limit_bytes=limit_mib * mib)


def split_heads(source, staged):
    rows, heads, head_dim = source.shape
    staged[0 : rows * heads, :] = source.reshape(rows * heads, head_dim).astype(jnp.float32)
    for head in range(heads):
        yield head, staged[pl.ds(head, rows, stride=heads), :].astype(jnp.bfloat16)


def pack_kernel(share_ref, *refs):
    *caches, queries, out, held_kv, held_q, made, staged, in_sem, out_sem = refs
    cores, _, rows, heads, head_dim = queries.shape
    group = heads // out.shape[0]
    tasks = []
    if caches:
        pool_k, pool_v, new_k, new_v = caches
        pages = pool_k.shape[0]
        for core, pool in enumerate((pool_k, pool_v)):
            tasks += [(pool.at[page], core, page) for page in range(pages)]
        for part, new in enumerate((new_k, new_v)):
            tasks += [(new.at[core], core, pages + part) for core in range(cores)]
    arrivals = [pltpu.make_async_copy(source, held_kv.at[i], in_sem.at[i]) for i, (source, _, _) in enumerate(tasks)]
    for core in range(cores):
        source = queries.at[core, share_ref[0]]
        arrivals.append(pltpu.make_async_copy(source, held_q.at[core], in_sem.at[len(tasks) + core]))
    for arrival in arrivals:
        arrival.start()
    leaving = []

    def leave(core, part):
        leaving.append(pltpu.make_async_copy(made.at[:, core, part], out.at[:, core, part], out_sem.at[len(leaving)]))
        leaving[-1].start()

    for i, (_, core, part) in enumerate(tasks):
        arrivals[i].wait()
        for head, picked in split_heads(held_kv[i], staged.at[i % 2]):
            made[head, core, part] = picked
        leave(core, part)
    last = out.shape[2] - 1
    for core in range(cores):
        arrivals[len(tasks) + core].wait()
        for head, picked in split_heads(held_q[core], staged.at[core % 2]):
            first = head % group * rows
            made[head // group, core, last, first : first + rows, :] = picked
        leave(core, last)
    for copy in leaving:
        copy.wait()


def pack(share, queries, kv_heads, caches=()):
    cores, _, rows, heads, head_dim = queries.shape
    group = heads // kv_heads
    parts, pieces, page_rows = 1, 0, group * rows
    if caches:
        pages = caches[0].shape[0]
        parts, pieces = pages + 3, 2 * pages + 2 * cores
    shape = (kv_heads, cores, parts, page_rows, head_dim)
    operands = [pltpu.with_memory_space_constraint(x, pltpu.HBM) for x in (*caches, queries)]
    return pl.pallas_call(
        pack_kernel,
        in_specs=[in_smem] + [in_hbm] * len(operands),
        out_specs=in_hbm,
        out_shape=pltpu.HBM(shape, jnp.bfloat16),
        scratch_shapes=[
            pltpu.VMEM((max(pieces, 1), page_rows, kv_heads, head_dim), jnp.bfloat16),
            pltpu.VMEM((cores, rows, heads, head_dim), jnp.bfloat16),
            pltpu.VMEM(shape, jnp.bfloat16),
            pltpu.VMEM((2, rows * heads, head_dim), jnp.float32),
            pltpu.SemaphoreType.DMA((pieces + cores,)),
            pltpu.SemaphoreType.DMA((pieces + cores,)),
        ],
        compiler_params=kernel_params(12 if caches else 6),
        cost_estimate=pl.CostEstimate(flops=0, bytes_accessed=parts * mib, transcendentals=0),
        name="pack_cache" if caches else "pack_queries",
    )(share, *operands)


def spread_kernel(place_ref, queries, got, keep, send, held, made, staged, sems):
    core, share, side = place_ref[0], place_ref[1], place_ref[3]
    own = pltpu.make_async_copy(queries.at[core, share], held.at[core], sems.at[0])
    other = pltpu.make_async_copy(got, held.at[1 - core], sems.at[1])
    own.start()
    other.start()
    own.wait()
    other.wait()
    rows, heads, _ = got.shape
    group = heads // (2 * made.shape[1])
    for block in range(2):
        for head, picked in split_heads(held[block], staged.at[block]):
            owner, first = head // group, head % group * rows
            made[owner % 2, owner // 2, block, first : first + rows, :] = picked
    copies = [
        pltpu.make_async_copy(made.at[side], keep, sems.at[2]),
        pltpu.make_async_copy(made.at[1 - side], send, sems.at[3]),
    ]
    for copy in copies:
        copy.start()
    for copy in copies:
        copy.wait()


def spread(place, queries, got, kv_heads):
    rows, heads, head_dim = got.shape
    shape = (kv_heads // 2, 2, heads // kv_heads * rows, head_dim)
    return pl.pallas_call(
        spread_kernel,
        in_specs=[in_smem, in_hbm, in_hbm],
        out_specs=[in_hbm, in_hbm],
        out_shape=[pltpu.HBM(shape, jnp.bfloat16)] * 2,
        scratch_shapes=[
            pltpu.VMEM((2, rows, heads, head_dim), jnp.bfloat16),
            pltpu.VMEM((2,) + shape, jnp.bfloat16),
            pltpu.VMEM((2, rows * heads, head_dim), jnp.float32),
            pltpu.SemaphoreType.DMA((4,)),
        ],
        compiler_params=kernel_params(6),
        cost_estimate=pl.CostEstimate(flops=0, bytes_accessed=mib, transcendentals=0),
        name="spread_queries",
    )(place, *[pltpu.with_memory_space_constraint(x, pltpu.HBM) for x in (queries, got)])


def gather_kernel(place_ref, keep, got, *refs):
    *outs, sems = refs
    side, level = place_ref[3], place_ref[2]
    copies = []
    for step, out in enumerate(outs):
        copies.append(pltpu.make_async_copy(keep.at[level ^ step], out.at[side], sems.at[2 * step]))
        copies.append(pltpu.make_async_copy(got.at[level ^ step], out.at[1 - side], sems.at[2 * step + 1]))
    for copy in copies:
        copy.start()
    for copy in copies:
        copy.wait()


def gather(place, keep, got):
    levels = keep.shape[0]
    return pl.pallas_call(
        gather_kernel,
        in_specs=[in_smem, in_hbm, in_hbm],
        out_specs=[in_hbm] * levels,
        out_shape=[pltpu.HBM((2,) + keep.shape[1:], jnp.bfloat16)] * levels,
        scratch_shapes=[pltpu.SemaphoreType.DMA((2 * levels,))],
        compiler_params=kernel_params(1),
        cost_estimate=pl.CostEstimate(flops=0, bytes_accessed=mib, transcendentals=0),
        name="gather_queries",
    )(place, *[pltpu.with_memory_space_constraint(x, pltpu.HBM) for x in (keep, got)])


def attend_kernel(pages, own_share, place_ref, table_ref, len_ref, message, other, *rest):
    out, cache_k, cache_v, new_v, total, made, held, others, in_sem, other_sem, out_sem = rest[-11:]
    fetch = pltpu.make_async_copy(other.at[:, 0:pages], others, other_sem)
    fetch.start()
    share = place_ref[1] if own_share else 1 - place_ref[1]
    queries, query_part = message, pages + 2
    arrivals = []
    if own_share:
        queries, query_part = held, 0
        for step, source in enumerate(rest[:-11]):
            count = source.shape[0]
            here = pl.ds((place_ref[2] ^ step) * count, count)
            arrivals.append(pltpu.make_async_copy(source, held.at[here], in_sem.at[step]))
            arrivals[-1].start()
    blocks, _, page_rows, head_dim = message.shape
    slots = table_ref.shape[1]
    group = out.shape[2] // head_dim
    per_head = out.shape[1]
    block_rows = per_head * group
    core = place_ref[0]
    cached = len_ref[core]
    for block in range(blocks):
        new_v[block * page_rows : (block + 1) * page_rows, 0:head_dim] = message[block, pages + 1]
    new_v[:, head_dim : 2 * head_dim] = jnp.ones((blocks * page_rows, head_dim), jnp.bfloat16)
    fetch.wait()
    for slot in range(slots):
        page = table_ref[core, slot]
        mine = message[page // pages, page % pages]
        theirs = others[page // pages, page % pages]
        seen = slot * page_rows + lax.broadcasted_iota(jnp.int32, (page_rows, head_dim), 0) < cached
        here = pl.ds(slot * page_rows, page_rows)
        cache_k[here, :] = jnp.where(core == 0, mine, theirs)
        values = jnp.where(core == 0, theirs, mine).astype(jnp.float32)
        cache_v[here, 0:head_dim] = jnp.where(seen, values, 0.0).astype(jnp.bfloat16)
        cache_v[here, head_dim : 2 * head_dim] = jnp.where(seen, 1.0, 0.0).astype(jnp.bfloat16)
    for arrival in arrivals:
        arrival.wait()

    def add(first_block, block_count, keys, values, begin=False, causal=False):
        rows = block_count * block_rows
        query = queries[first_block : first_block + block_count, query_part].reshape(rows, head_dim)
        scores = lax.dot_general(query, keys, (((1,), (1,)), ((), ())), preferred_element_type=jnp.float32)
        weights = jnp.exp2((soft_cap * log2_e) * jnp.tanh(scores * (score_scale / soft_cap)))
        if causal:
            row = lax.broadcasted_iota(jnp.int32, weights.shape, 0)
            offset = row // block_rows * page_rows + row % per_head + share * per_head
            weights = jnp.where(lax.broadcasted_iota(jnp.int32, weights.shape, 1) <= offset, weights, 0.0)
        product = jnp.dot(weights.astype(jnp.bfloat16), values, preferred_element_type=jnp.float32)
        here = pl.ds(first_block * block_rows, rows)
        total[here, :] = product if begin else total[here, :] + product

    half = blocks // 2
    for first in (0, half):
        for tile in range(0, slots * page_rows, key_tile):
            add(first, half, cache_k[tile : tile + key_tile, :], cache_v[tile : tile + key_tile, :], begin=tile == 0)
    tile_blocks = key_tile // page_rows
    for block in range(0, blocks, tile_blocks):
        keys = message[block : block + tile_blocks, pages].reshape(key_tile, head_dim)
        values = new_v[block * page_rows : block * page_rows + key_tile, :]
        add(block, tile_blocks, keys, values, causal=True)
        later = block + tile_blocks
        while later < blocks:
            count = min(half, blocks - later)
            add(later, count, keys, values)
            later += count
    copies = []
    for block in range(blocks):
        here = pl.ds(block * block_rows, block_rows)
        attended = (total[here, 0:head_dim] / total[here, head_dim : 2 * head_dim]).astype(jnp.bfloat16)
        for head in range(group):
            made[block, :, head * head_dim : (head + 1) * head_dim] = attended[head * per_head : (head + 1) * per_head, :]
        if block % half == half - 1:
            here = pl.ds(block + 1 - half, half)
            copies.append(pltpu.make_async_copy(made.at[here], out.at[here], out_sem.at[len(copies)]))
            copies[-1].start()
    for copy in copies:
        copy.wait()


def attend(place, page_table, cache_len, message, other, queries, *, pages, group):
    blocks, _, page_rows, head_dim = message.shape
    slots = page_table.shape[1]
    block_rows = page_rows
    operands = [message, other]
    operands += [pltpu.with_memory_space_constraint(x, pltpu.HBM) for x in queries]
    specs = [in_smem] * 3 + [in_vmem, pl.BlockSpec(memory_space=pl.ANY)] + [in_hbm] * len(queries)
    seen = blocks * block_rows * (slots + blocks // 2) * page_rows
    return pl.pallas_call(
        functools.partial(attend_kernel, pages, bool(queries)),
        in_specs=specs,
        out_specs=in_hbm,
        out_shape=pltpu.HBM((blocks, block_rows // group, group * head_dim), jnp.bfloat16),
        scratch_shapes=[
            pltpu.VMEM((slots * page_rows, head_dim), jnp.bfloat16),
            pltpu.VMEM((slots * page_rows, 2 * head_dim), jnp.bfloat16),
            pltpu.VMEM((blocks * page_rows, 2 * head_dim), jnp.bfloat16),
            pltpu.VMEM((blocks * block_rows, 2 * head_dim), jnp.float32),
            pltpu.VMEM((blocks, block_rows // group, group * head_dim), jnp.bfloat16),
            pltpu.VMEM((blocks, 1, block_rows, head_dim) if queries else (8, 128), jnp.bfloat16),
            pltpu.VMEM((blocks, pages, page_rows, head_dim), jnp.bfloat16),
            pltpu.SemaphoreType.DMA((max(len(queries), 1),)),
            pltpu.SemaphoreType.DMA(()),
            pltpu.SemaphoreType.DMA((2,)),
        ],
        compiler_params=kernel_params(12),
        cost_estimate=pl.CostEstimate(flops=8 * seen * head_dim, bytes_accessed=8 * mib, transcendentals=2 * seen),
        name="attend",
    )(place, page_table, cache_len, *operands)


def project_kernel(begin, attended, weight, *refs):
    (*arrived, out), (rows, held, sem) = refs[:-3], refs[-3:]
    if arrived:
        *arrived, out, squares_out = (*arrived, out)
    tiles, _, tile = held.shape
    arrivals = []
    for i in range(tiles):
        columns = pl.ds(begin + i * tile, tile)
        arrivals.append(pltpu.make_async_copy(weight.at[:, columns], held.at[i], sem.at[i]))
        arrivals[-1].start()
    sources, count, features = attended.shape
    requests = rows.shape[0] // count
    for source in range(sources):
        at, first = source % requests * count, source // requests * features
        rows[at : at + count, first : first + features] = attended[source]
    squares = 0.0
    for i in range(tiles):
        here = slice(i * tile, (i + 1) * tile)
        arrivals[i].wait()
        product = jnp.dot(rows[...], held[i], preferred_element_type=jnp.float32)
        at = i * tile
        for piece in arrived:
            if 0 <= at < piece.shape[1]:
                product += piece[:, at : at + tile].astype(jnp.float32)
                squares += squares_by_lane(product)
            at -= piece.shape[1]
        out[:, here] = product.astype(out.dtype)
    if arrived:
        squares_out[...] = squares


def squares_by_lane(x):
    return sum(x[:, i : i + 128] * x[:, i : i + 128] for i in range(0, x.shape[1], 128))


def project(attended, weight, requests, begin, columns, tile, dtype, arrived=()):
    sources, count, features = attended.shape
    depth = weight.shape[0]
    rows = requests * count
    operands = [attended, pltpu.with_memory_space_constraint(weight, pltpu.HBM)]
    outs = [jax.ShapeDtypeStruct((rows, columns), dtype)]
    if arrived:
        operands += arrived
        outs.append(jax.ShapeDtypeStruct((rows, 128), jnp.float32))
    return pl.pallas_call(
        functools.partial(project_kernel, begin),
        in_specs=[in_vmem, in_hbm] + [in_vmem] * (len(operands) - 2),
        out_specs=[in_vmem] * len(outs),
        out_shape=outs,
        scratch_shapes=[
            pltpu.VMEM((rows, depth), jnp.bfloat16),
            pltpu.VMEM((columns // tile, depth, tile), jnp.bfloat16),
            pltpu.SemaphoreType.DMA((columns // tile,)),
        ],
        compiler_params=kernel_params(6 + 2 * depth * columns // mib),
        cost_estimate=pl.CostEstimate(flops=2 * rows * depth * columns, bytes_accessed=2 * depth * columns, transcendentals=0),
        name="project",
    )(*operands)


def wait_here(x):
    return pl.pallas_call(
        lambda *_: None,
        in_specs=[pl.BlockSpec(memory_space=pl.ANY)],
        out_specs=pl.BlockSpec(memory_space=pl.ANY),
        out_shape=jax.ShapeDtypeStruct(x.shape, x.dtype),
        input_output_aliases={0: 0},
        cost_estimate=pl.CostEstimate(flops=5000000000, bytes_accessed=0, transcendentals=0),
        name="wait_here",
    )(x)


def finish_kernel(projected, squares_ref, arrived, residual, gain, out, made, sem):
    requests, count, width = residual.shape
    rows = made.shape[1]
    split = width - arrived.shape[1]
    copies = []
    for step in range(made.shape[0]):
        request, first = step * rows // count, step * rows % count
        here = slice(step * rows, (step + 1) * rows)
        place = slice(first, first + rows)
        last = projected[here, split:] + arrived[here, :].astype(jnp.float32)
        squares = jnp.sum(squares_ref[here, :] + squares_by_lane(last), axis=-1, keepdims=True)
        inv_rms = lax.rsqrt(squares / width + norm_eps)
        for columns, x in ((slice(0, split), projected[here, 0:split]), (slice(split, width), last)):
            mixed = residual[request, place, columns].astype(jnp.float32) + gain[:, columns] * x * inv_rms
            made[step, :, columns] = mixed.astype(jnp.bfloat16)
        copies.append(pltpu.make_async_copy(made.at[step], out.at[request, place], sem.at[step]))
        copies[-1].start()
    for copy in copies:
        copy.wait()


def finish(projected, squares, arrived, residual, gain):
    requests, count, width = residual.shape
    rows = 32
    steps = requests * count // rows
    return pl.pallas_call(
        finish_kernel,
        in_specs=[in_vmem] * 5,
        out_specs=in_hbm,
        out_shape=pltpu.HBM(residual.shape, jnp.bfloat16),
        scratch_shapes=[pltpu.VMEM((steps, rows, width), jnp.bfloat16), pltpu.SemaphoreType.DMA((steps,))],
        compiler_params=kernel_params(12),
        cost_estimate=pl.CostEstimate(flops=0, bytes_accessed=6 * mib, transcendentals=0),
        name="finish",
    )(projected, squares, arrived, residual, gain.reshape(1, width))


def by_heads(
    queries,
    new_keys,
    new_values,
    pool_keys,
    pool_values,
    page_table,
    cache_len,
    out_weight,
    residual,
    post_gain,
):
    req_count, per_req, heads_here, head_dim = queries.shape
    kv_here = new_keys.shape[2]
    pages = pool_keys.shape[0]
    blk_count = lax.axis_size("blk")
    shares = lax.axis_size("head")
    group = heads_here // kv_here
    blk = lax.axis_index("blk")
    core, mine = blk % 2, lax.axis_index("head")
    place = jnp.stack([core, mine, blk // 4, blk // 2 % 2])
    width = out_weight.shape[2]
    weight = out_weight.reshape(heads_here * head_dim, width)
    queries = queries.reshape(req_count, shares, per_req // shares, heads_here, head_dim)
    exchange = functools.partial(lax.all_to_all, axis_name="blk", split_axis=0, concat_axis=0, tiled=True)

    def across(x, bits):
        return lax.ppermute(x, "blk", [(i, i ^ bits) for i in range(blk_count)])

    message = pack((1 - mine)[None], queries, kv_here, (pool_keys, pool_values, new_keys, new_values))
    message = exchange(message.reshape((blk_count,) + message.shape[2:]))
    got = lax.dynamic_slice(queries, (1 - core, mine, 0, 0, 0), (1, 1) + queries.shape[2:])
    got = across(got.reshape(queries.shape[2:]), 1)
    keep, send = spread(place, queries, got, kv_here)
    asked = gather(place, keep, across(send, 2))
    message, *asked = lax.optimization_barrier((message, *asked))
    other = across(message, 1)
    asked = [across(x, 4 * step) if step else x for step, x in enumerate(asked)]
    asked = [x.reshape(4, 1, *x.shape[2:]) for x in asked]
    attend_share = functools.partial(attend, place, page_table, cache_len, message, other, pages=pages, group=group)

    first = attend_share([])
    first, *asked = lax.optimization_barrier((first, *asked))
    first = exchange(first)
    second = attend_share(asked)
    first, second = lax.optimization_barrier((first, second))
    tile = width // 9
    begin = 0
    arrived = []
    for piece, tiles in enumerate((3, 3, 3)):
        if piece == 2:
            first, arrived[0] = lax.optimization_barrier((first, wait_here(arrived[0])))
        (sent,) = project(first, weight, req_count, begin, tiles * tile, tile, jnp.bfloat16)
        begin += tiles * tile
        if piece == 0:
            sent, second = lax.optimization_barrier((sent, second))
            second = exchange(second)
        else:
            first, sent = lax.optimization_barrier((first, sent))
        arrived.append(lax.ppermute(sent, "head", [(0, 1), (1, 0)]))
    projected, squares = project(second, weight, req_count, 0, width, tile, jnp.float32, arrived[:2])
    return finish(projected, squares, arrived[2], residual, post_gain)


def group_pages(page_count, page_len):
    width = max(1, min(page_count, 2048 // page_len))
    while page_count % width:
        width -= 1
    return width


def attend_pages(running, grouped, key_pages, value_pages, valid_keys):
    page_count, page_len, kv_heads, head_dim = key_pages.shape
    tok_rows = valid_keys.shape[1]
    width = group_pages(page_count, page_len)
    groups = page_count // width
    key_groups = key_pages.reshape(groups, width * page_len, kv_heads, head_dim)
    value_groups = value_pages.reshape(groups, width * page_len, kv_heads, head_dim)
    valid_groups = (
        valid_keys.reshape(groups, width, tok_rows, page_len)
        .transpose(0, 2, 1, 3)
        .reshape(groups, tok_rows, width * page_len)
    )

    def compute(carry_in, key_block, value_block, valid_block):
        numerator, denominator = carry_in
        scores = (
            jnp.einsum("tkgd,skd->kgts", grouped, key_block, preferred_element_type=jnp.float32)
            * score_scale
        )
        capped = soft_cap * jnp.tanh(scores / soft_cap)
        weights = jnp.where(valid_block[None, None], jnp.exp(capped), 0.0).astype(jnp.bfloat16)
        numerator = numerator + jnp.einsum(
            "kgts,skd->tkgd", weights, value_block, preferred_element_type=jnp.float32
        )
        denominator = denominator + jnp.sum(weights.astype(jnp.float32), axis=-1)
        return (numerator, denominator)

    def one_group(carry_in, inputs):
        key_block, value_block, valid_block = inputs
        carry_out = compute(carry_in, key_block, value_block, valid_block)
        return (carry_out, None)

    result, _ = lax.scan(one_group, running, (key_groups, value_groups, valid_groups))
    return result


def shards(
    queries,
    new_keys,
    new_values,
    pool_keys,
    pool_values,
    page_table,
    cache_len,
    out_weight,
    residual,
    post_gain,
):
    req_count, per_req, heads_here, head_dim = queries.shape
    tok_dev = req_count * per_req
    kv_here = new_keys.shape[2]
    page_len = pool_keys.shape[1]
    slot_count = page_table.shape[1]
    blk_place = lax.axis_index("blk")
    row_ids = jnp.arange(tok_dev, dtype=jnp.int32)
    row_request = row_ids // per_req
    row_offset = blk_place * per_req + row_ids % per_req
    grouped = queries.reshape(tok_dev, kv_here, heads_here // kv_here, head_dim)
    page_rows = jnp.arange(page_len, dtype=jnp.int32)
    request_ids = jnp.arange(req_count, dtype=jnp.int32)
    row_onehot = row_request[:, None] == request_ids[None, :]
    start_carry = (
        jnp.zeros((tok_dev, kv_here, heads_here // kv_here, head_dim), jnp.float32),
        jnp.zeros((kv_here, heads_here // kv_here, tok_dev), jnp.float32),
    )
    pieces = (
        lax.all_gather(pool_keys, "blk", axis=0, tiled=True),
        lax.all_gather(pool_values, "blk", axis=0, tiled=True),
    )
    page_ids = jnp.arange(pieces[0].shape[0], dtype=jnp.int32)
    matches = page_ids[:, None, None] == page_table[None, :, :]
    slot_index = jnp.sum(
        jnp.where(matches, jnp.arange(slot_count, dtype=jnp.int32)[None, None, :], 0), axis=2
    )
    owned_page = jnp.any(matches, axis=2)
    position = slot_index[:, :, None] * page_len + page_rows[None, None, :]
    keep_keys = owned_page[:, :, None] & (position < cache_len[None, :, None])
    running = attend_pages(
        start_carry,
        grouped,
        pieces[0],
        pieces[1],
        jnp.any(keep_keys[:, None, :, :] & row_onehot[None, :, :, None], axis=2),
    )
    pieces = (
        lax.all_gather(new_keys, "blk", axis=1, tiled=True),
        lax.all_gather(new_values, "blk", axis=1, tiled=True),
    )
    piece_pages = pieces[0].shape[1] // page_len
    page_index = jnp.arange(req_count * piece_pages, dtype=jnp.int32)
    firsts = page_index % piece_pages * page_len
    key_pages = pieces[0].reshape(req_count * piece_pages, page_len, kv_here, head_dim)
    value_pages = pieces[1].reshape(req_count * piece_pages, page_len, kv_here, head_dim)
    offsets = firsts[:, None] + page_rows[None, :]
    same_request = (page_index // piece_pages)[:, None] == row_request[None, :]
    running = attend_pages(
        running,
        grouped,
        key_pages,
        value_pages,
        same_request[:, :, None] & (offsets[:, None, :] <= row_offset[None, :, None]),
    )
    numerator, denominator = running
    attended = (numerator / jnp.transpose(denominator, (2, 0, 1))[..., None]).astype(jnp.bfloat16)
    head_count = lax.axis_size("head")
    share = per_req // head_count
    feature_len = heads_here * head_dim
    attended = (
        attended.reshape(req_count, head_count, share, feature_len)
        .transpose(1, 0, 2, 3)
        .reshape(tok_dev, feature_len)
    )
    weight_rows = out_weight.reshape(feature_len, out_weight.shape[2])
    projected = lax.psum_scatter(
        jnp.dot(attended, weight_rows, preferred_element_type=jnp.float32).astype(jnp.bfloat16),
        "head",
        scatter_dimension=0,
        tiled=True,
    ).astype(jnp.float32)
    projected = projected.reshape(req_count, share, projected.shape[1])
    inv_rms = lax.rsqrt(jnp.mean(projected * projected, axis=-1, keepdims=True) + norm_eps)
    mixed_out = residual.astype(jnp.float32) + post_gain * projected * inv_rms
    return mixed_out.astype(jnp.bfloat16)


def solution(mesh):
    placed = (
        P(None, "blk", "head", None),
        P(None, "blk", "head", None),
        P(None, "blk", "head", None),
        P("blk", None, "head", None),
        P("blk", None, "head", None),
        P(),
        P(),
        P("head", None, None),
        P(None, ("blk", "head"), None),
        P(),
    )
    def one_device(queries, new_keys, *rest):
        requests, per_req = queries.shape[0], queries.shape[1]
        owners = mesh.shape["blk"] == 2 * new_keys.shape[2] == 16 and mesh.shape["head"] == 2 and requests == 2
        fits = rest[1].shape[1] == per_req == 128 and queries.shape[2] == 2 * new_keys.shape[2]
        return (by_heads if owners and fits else shards)(queries, new_keys, *rest)

    return jax.shard_map(
        one_device,
        mesh=mesh,
        in_specs=placed,
        out_specs=P(None, ("blk", "head"), None),
        check_vma=False,
    )
```

```python
import functools

import jax
import jax.numpy as jnp
from jax import lax
from jax.experimental import pallas as pl
from jax.experimental.pallas import tpu as pltpu
from jax.sharding import PartitionSpec as P

soft_cap = 50.0
score_scale = 144.0 ** (-0.5)
norm_eps = 1e-06
log2_e = 1.4426950408889634
key_tile = 256
mib = 1024 * 1024
in_vmem = pl.BlockSpec(memory_space=pltpu.VMEM)
in_hbm = pl.BlockSpec(memory_space=pltpu.HBM)
in_smem = pl.BlockSpec(memory_space=pltpu.SMEM)


def kernel_params(limit_mib):
    return pltpu.CompilerParams(vmem_limit_bytes=limit_mib * mib)


def split_heads(source, staged):
    rows, heads, head_dim = source.shape
    staged[0 : rows * heads, :] = source.reshape(rows * heads, head_dim).astype(jnp.float32)
    for head in range(heads):
        yield head, staged[pl.ds(head, rows, stride=heads), :].astype(jnp.bfloat16)


def pack_kernel(share_ref, *refs):
    *caches, queries, out, held_kv, held_q, made, staged, in_sem, out_sem = refs
    cores, _, rows, heads, head_dim = queries.shape
    group = heads // out.shape[0]
    tasks = []
    if caches:
        pool_k, pool_v, new_k, new_v = caches
        pages = pool_k.shape[0]
        for core, pool in enumerate((pool_k, pool_v)):
            tasks += [(pool.at[page], core, page) for page in range(pages)]
        for part, new in enumerate((new_k, new_v)):
            tasks += [(new.at[core], core, pages + part) for core in range(cores)]
    arrivals = [pltpu.make_async_copy(source, held_kv.at[i], in_sem.at[i]) for i, (source, _, _) in enumerate(tasks)]
    for core in range(cores):
        source = queries.at[core, share_ref[0]]
        arrivals.append(pltpu.make_async_copy(source, held_q.at[core], in_sem.at[len(tasks) + core]))
    for arrival in arrivals:
        arrival.start()
    leaving = []

    def leave(core, part):
        leaving.append(pltpu.make_async_copy(made.at[:, core, part], out.at[:, core, part], out_sem.at[len(leaving)]))
        leaving[-1].start()

    for i, (_, core, part) in enumerate(tasks):
        arrivals[i].wait()
        for head, picked in split_heads(held_kv[i], staged.at[i % 2]):
            made[head, core, part] = picked
        leave(core, part)
    last = out.shape[2] - 1
    for core in range(cores):
        arrivals[len(tasks) + core].wait()
        for head, picked in split_heads(held_q[core], staged.at[core % 2]):
            first = head % group * rows
            made[head // group, core, last, first : first + rows, :] = picked
        leave(core, last)
    for copy in leaving:
        copy.wait()


def pack(share, queries, kv_heads, caches=()):
    cores, _, rows, heads, head_dim = queries.shape
    group = heads // kv_heads
    parts, pieces, page_rows = 1, 0, group * rows
    if caches:
        pages = caches[0].shape[0]
        parts, pieces = pages + 3, 2 * pages + 2 * cores
    shape = (kv_heads, cores, parts, page_rows, head_dim)
    operands = [pltpu.with_memory_space_constraint(x, pltpu.HBM) for x in (*caches, queries)]
    return pl.pallas_call(
        pack_kernel,
        in_specs=[in_smem] + [in_hbm] * len(operands),
        out_specs=in_hbm,
        out_shape=pltpu.HBM(shape, jnp.bfloat16),
        scratch_shapes=[
            pltpu.VMEM((max(pieces, 1), page_rows, kv_heads, head_dim), jnp.bfloat16),
            pltpu.VMEM((cores, rows, heads, head_dim), jnp.bfloat16),
            pltpu.VMEM(shape, jnp.bfloat16),
            pltpu.VMEM((2, rows * heads, head_dim), jnp.float32),
            pltpu.SemaphoreType.DMA((pieces + cores,)),
            pltpu.SemaphoreType.DMA((pieces + cores,)),
        ],
        compiler_params=kernel_params(16),
        cost_estimate=pl.CostEstimate(flops=0, bytes_accessed=parts * mib, transcendentals=0),
        name="pack_cache" if caches else "pack_queries",
    )(share, *operands)


def spread_kernel(place_ref, queries, got, keep, send, held, made, staged, sems):
    core, share, side = place_ref[0], place_ref[1], place_ref[3]
    own = pltpu.make_async_copy(queries.at[core, share], held.at[core], sems.at[0])
    other = pltpu.make_async_copy(got, held.at[1 - core], sems.at[1])
    own.start()
    other.start()
    own.wait()
    other.wait()
    rows, heads, _ = got.shape
    group = heads // (2 * made.shape[1])
    for block in range(2):
        for head, picked in split_heads(held[block], staged.at[block]):
            owner, first = head // group, head % group * rows
            made[owner % 2, owner // 2, block, first : first + rows, :] = picked
    copies = [
        pltpu.make_async_copy(made.at[side], keep, sems.at[2]),
        pltpu.make_async_copy(made.at[1 - side], send, sems.at[3]),
    ]
    for copy in copies:
        copy.start()
    for copy in copies:
        copy.wait()


def spread(place, queries, got, kv_heads):
    rows, heads, head_dim = got.shape
    shape = (kv_heads // 2, 2, heads // kv_heads * rows, head_dim)
    return pl.pallas_call(
        spread_kernel,
        in_specs=[in_smem, in_hbm, in_hbm],
        out_specs=[in_hbm, in_hbm],
        out_shape=[pltpu.HBM(shape, jnp.bfloat16)] * 2,
        scratch_shapes=[
            pltpu.VMEM((2, rows, heads, head_dim), jnp.bfloat16),
            pltpu.VMEM((2,) + shape, jnp.bfloat16),
            pltpu.VMEM((2, rows * heads, head_dim), jnp.float32),
            pltpu.SemaphoreType.DMA((4,)),
        ],
        compiler_params=kernel_params(12),
        cost_estimate=pl.CostEstimate(flops=0, bytes_accessed=mib, transcendentals=0),
        name="spread_queries",
    )(place, *[pltpu.with_memory_space_constraint(x, pltpu.HBM) for x in (queries, got)])


def gather_kernel(place_ref, keep, got, *refs):
    *outs, sems = refs
    side, level = place_ref[3], place_ref[2]
    copies = []
    for step, out in enumerate(outs):
        copies.append(pltpu.make_async_copy(keep.at[level ^ step], out.at[side], sems.at[2 * step]))
        copies.append(pltpu.make_async_copy(got.at[level ^ step], out.at[1 - side], sems.at[2 * step + 1]))
    for copy in copies:
        copy.start()
    for copy in copies:
        copy.wait()


def gather(place, keep, got):
    levels = keep.shape[0]
    return pl.pallas_call(
        gather_kernel,
        in_specs=[in_smem, in_hbm, in_hbm],
        out_specs=[in_hbm] * levels,
        out_shape=[pltpu.HBM((2,) + keep.shape[1:], jnp.bfloat16)] * levels,
        scratch_shapes=[pltpu.SemaphoreType.DMA((2 * levels,))],
        compiler_params=kernel_params(4),
        cost_estimate=pl.CostEstimate(flops=0, bytes_accessed=mib, transcendentals=0),
        name="gather_queries",
    )(place, *[pltpu.with_memory_space_constraint(x, pltpu.HBM) for x in (keep, got)])


def add_keys(
    queries, query_part, total, per_head, group, share, page_rows, first_block, block_count, keys, values, start=None, causal=False
):
    block_rows = per_head * group
    rows = block_count * block_rows
    query = queries[first_block : first_block + block_count, query_part].reshape(rows, keys.shape[1])
    scores = lax.dot_general(query, keys, (((1,), (1,)), ((), ())), preferred_element_type=jnp.float32)
    weights = jnp.exp2((soft_cap * log2_e) * jnp.tanh(scores * (score_scale / soft_cap)))
    if causal:
        row = lax.broadcasted_iota(jnp.int32, weights.shape, 0)
        offset = row // block_rows * page_rows + row % per_head + share * per_head
        weights = jnp.where(lax.broadcasted_iota(jnp.int32, weights.shape, 1) <= offset, weights, 0.0)
    product = jnp.dot(weights.astype(jnp.bfloat16), values, preferred_element_type=jnp.float32)
    here = pl.ds(first_block * block_rows, rows)
    total[here, :] = product if start is None else start[here, :] + product


def add_new_keys(add, message, pages):
    blocks, _, page_rows, head_dim = message.shape
    half, tile_blocks = blocks // 2, key_tile // page_rows
    ones = jnp.ones((key_tile, head_dim), jnp.bfloat16)
    for block in range(0, blocks, tile_blocks):
        keys = message[block : block + tile_blocks, pages].reshape(key_tile, head_dim)
        values = message[block : block + tile_blocks, pages + 1].reshape(key_tile, head_dim)
        values = jnp.concatenate([values, ones], axis=1)
        start = None if block == 0 else add.args[2]
        add(block, tile_blocks, keys, values, start=start, causal=True)
        later = block + tile_blocks
        while later < blocks:
            count = min(half, blocks - later)
            add(later, count, keys, values, start=start)
            later += count


def new_kernel(pages, group, place_ref, message, total):
    page_rows = message.shape[2]
    per_head = page_rows // group
    share = 1 - place_ref[1]
    add_new_keys(functools.partial(add_keys, message, pages + 2, total, per_head, group, share, page_rows), message, pages)


def attend_new(place, message, *, pages, group):
    blocks, _, page_rows, head_dim = message.shape
    seen = blocks * page_rows * blocks // 2 * page_rows
    return pl.pallas_call(
        functools.partial(new_kernel, pages, group),
        in_specs=[in_smem, in_vmem],
        out_specs=in_vmem,
        out_shape=jax.ShapeDtypeStruct((blocks * page_rows, 2 * head_dim), jnp.float32),
        compiler_params=kernel_params(20),
        cost_estimate=pl.CostEstimate(flops=8 * seen * head_dim, bytes_accessed=4 * mib, transcendentals=2 * seen),
        name="attend_new",
    )(place, message)


def attend_kernel(pages, own_share, given, place_ref, table_ref, len_ref, message, other, *rest):
    out, cache_k, cache_v, total, made, held, others, in_sem, other_sem, out_sem = rest[-10:]
    fetch = pltpu.make_async_copy(other.at[:, 0:pages], others, other_sem)
    fetch.start()
    share = place_ref[1] if own_share else 1 - place_ref[1]
    queries, query_part = (held, 0) if own_share else (message, pages + 2)
    arrivals = []
    for step, source in enumerate(rest[:-10] if own_share else ()):
        count = source.shape[0]
        here = pl.ds((place_ref[2] ^ step) * count, count)
        arrivals.append(pltpu.make_async_copy(source, held.at[here], in_sem.at[step]))
        arrivals[-1].start()
    blocks, _, page_rows, head_dim = message.shape
    slots = table_ref.shape[1]
    group = out.shape[2] // head_dim
    per_head = out.shape[1]
    block_rows = per_head * group
    core = place_ref[0]
    cached = len_ref[core]
    half = blocks // 2
    tile_blocks = key_tile // page_rows
    copies = []

    add = functools.partial(add_keys, queries, query_part, total, per_head, group, share, page_rows)

    def leave(first):
        for block in range(first, first + half):
            here = pl.ds(block * block_rows, block_rows)
            attended = (total[here, 0:head_dim] / total[here, head_dim : 2 * head_dim]).astype(jnp.bfloat16)
            for head in range(group):
                made[block, :, head * head_dim : (head + 1) * head_dim] = attended[head * per_head : (head + 1) * per_head, :]
        here = pl.ds(first, half)
        copies.append(pltpu.make_async_copy(made.at[here], out.at[here], out_sem.at[len(copies)]))
        copies[-1].start()

    for arrival in arrivals:
        arrival.wait()
    if not given:
        add_new_keys(add, message, pages)
    fetch.wait()
    for tile in range(0, slots, tile_blocks):
        for slot in range(tile, tile + tile_blocks):
            page = table_ref[core, slot]
            mine = message[page // pages, page % pages]
            theirs = others[page // pages, page % pages]
            seen = slot * page_rows + lax.broadcasted_iota(jnp.int32, (page_rows, head_dim), 0) < cached
            here = pl.ds(slot * page_rows, page_rows)
            cache_k[here, :] = jnp.where(core == 0, mine, theirs)
            values = jnp.where(core == 0, theirs, mine).astype(jnp.float32)
            cache_v[here, 0:head_dim] = jnp.where(seen, values, 0.0).astype(jnp.bfloat16)
            cache_v[here, head_dim : 2 * head_dim] = jnp.where(seen, 1.0, 0.0).astype(jnp.bfloat16)
        here = slice(tile * page_rows, tile * page_rows + key_tile)
        for first in (0, half):
            add(first, half, cache_k[here, :], cache_v[here, :], start=rest[0] if given and tile == 0 else total)
            if tile + tile_blocks == slots:
                leave(first)
    for copy in copies:
        copy.wait()


def attend(place, page_table, cache_len, message, other, queries, given=None, *, pages, group):
    blocks, _, page_rows, head_dim = message.shape
    slots = page_table.shape[1]
    block_rows = page_rows
    operands = [message, other]
    operands += [pltpu.with_memory_space_constraint(x, pltpu.HBM) for x in queries]
    specs = [in_smem] * 3 + [in_vmem, pl.BlockSpec(memory_space=pl.ANY)] + [in_hbm] * len(queries)
    if given is not None:
        operands.append(given)
        specs.append(in_vmem)
    seen = blocks * block_rows * (slots + blocks // 2) * page_rows
    return pl.pallas_call(
        functools.partial(attend_kernel, pages, bool(queries), given is not None),
        in_specs=specs,
        out_specs=in_hbm,
        out_shape=pltpu.HBM((blocks, block_rows // group, group * head_dim), jnp.bfloat16),
        scratch_shapes=[
            pltpu.VMEM((slots * page_rows, head_dim), jnp.bfloat16),
            pltpu.VMEM((slots * page_rows, 2 * head_dim), jnp.bfloat16),
            pltpu.VMEM((blocks * block_rows, 2 * head_dim), jnp.float32),
            pltpu.VMEM((blocks, block_rows // group, group * head_dim), jnp.bfloat16),
            pltpu.VMEM((blocks, 1, block_rows, head_dim) if queries else (8, 128), jnp.bfloat16),
            pltpu.VMEM((blocks, pages, page_rows, head_dim), jnp.bfloat16),
            pltpu.SemaphoreType.DMA((max(len(queries), 1),)),
            pltpu.SemaphoreType.DMA(()),
            pltpu.SemaphoreType.DMA((2,)),
        ],
        compiler_params=kernel_params(24),
        cost_estimate=pl.CostEstimate(flops=8 * seen * head_dim, bytes_accessed=8 * mib, transcendentals=2 * seen),
        name="attend",
    )(place, page_table, cache_len, *operands)


def project_kernel(begin, attended, weight, *refs):
    (*arrived, out), (rows, held, sem) = refs[:-3], refs[-3:]
    if arrived:
        *arrived, out, squares_out = (*arrived, out)
    tiles, _, tile = held.shape
    arrivals = []
    for i in range(tiles):
        columns = pl.ds(begin + i * tile, tile)
        arrivals.append(pltpu.make_async_copy(weight.at[:, columns], held.at[i], sem.at[i]))
        arrivals[-1].start()
    sources, count, features = attended.shape
    requests = rows.shape[0] // count
    for source in range(sources):
        at, first = source % requests * count, source // requests * features
        rows[at : at + count, first : first + features] = attended[source]
    squares = 0.0
    for i in range(tiles):
        here = slice(i * tile, (i + 1) * tile)
        arrivals[i].wait()
        product = jnp.dot(rows[...], held[i], preferred_element_type=jnp.float32)
        at = i * tile
        for piece in arrived:
            if 0 <= at < piece.shape[1]:
                product += piece[:, at : at + tile].astype(jnp.float32)
                squares += squares_by_lane(product)
            at -= piece.shape[1]
        out[:, here] = product.astype(out.dtype)
    if arrived:
        squares_out[...] = squares


def squares_by_lane(x):
    return sum(x[:, i : i + 128] * x[:, i : i + 128] for i in range(0, x.shape[1], 128))


def project(attended, weight, requests, begin, columns, tile, dtype, arrived=()):
    sources, count, features = attended.shape
    depth = weight.shape[0]
    rows = requests * count
    operands = [attended, pltpu.with_memory_space_constraint(weight, pltpu.HBM)]
    outs = [jax.ShapeDtypeStruct((rows, columns), dtype)]
    if arrived:
        operands += arrived
        outs.append(jax.ShapeDtypeStruct((rows, 128), jnp.float32))
    return pl.pallas_call(
        functools.partial(project_kernel, begin),
        in_specs=[in_vmem, in_hbm] + [in_vmem] * (len(operands) - 2),
        out_specs=[in_vmem] * len(outs),
        out_shape=outs,
        scratch_shapes=[
            pltpu.VMEM((rows, depth), jnp.bfloat16),
            pltpu.VMEM((columns // tile, depth, tile), jnp.bfloat16),
            pltpu.SemaphoreType.DMA((columns // tile,)),
        ],
        compiler_params=kernel_params(12 + 2 * depth * columns // mib),
        cost_estimate=pl.CostEstimate(flops=2 * rows * depth * columns, bytes_accessed=2 * depth * columns, transcendentals=0),
        name="project",
    )(*operands)


def wait_here(x):
    return pl.pallas_call(
        lambda *_: None,
        in_specs=[pl.BlockSpec(memory_space=pl.ANY)],
        out_specs=pl.BlockSpec(memory_space=pl.ANY),
        out_shape=jax.ShapeDtypeStruct(x.shape, x.dtype),
        input_output_aliases={0: 0},
        cost_estimate=pl.CostEstimate(flops=5000000000, bytes_accessed=0, transcendentals=0),
        name="wait_here",
    )(x)


def finish_kernel(projected, squares_ref, *refs):
    *arrived, residual, gain, out, made, sem = refs
    requests, count, width = residual.shape
    rows = made.shape[1]
    split = width - sum(piece.shape[1] for piece in arrived)
    copies = []
    for step in range(made.shape[0]):
        request, first = step * rows // count, step * rows % count
        here = slice(step * rows, (step + 1) * rows)
        place = slice(first, first + rows)
        parts, squares, begin = [(slice(0, split), projected[here, 0:split])], squares_ref[here, :], split
        for piece in arrived:
            columns = slice(begin, begin + piece.shape[1])
            x = projected[here, columns] + piece[here, :].astype(jnp.float32)
            parts.append((columns, x))
            squares += squares_by_lane(x)
            begin = columns.stop
        inv_rms = lax.rsqrt(jnp.sum(squares, axis=-1, keepdims=True) / width + norm_eps)
        for columns, x in parts:
            mixed = residual[request, place, columns].astype(jnp.float32) + gain[:, columns] * x * inv_rms
            made[step, :, columns] = mixed.astype(jnp.bfloat16)
        copies.append(pltpu.make_async_copy(made.at[step], out.at[request, place], sem.at[step]))
        copies[-1].start()
    for copy in copies:
        copy.wait()


def finish(projected, squares, arrived, residual, gain):
    requests, count, width = residual.shape
    rows = 32
    steps = requests * count // rows
    return pl.pallas_call(
        finish_kernel,
        in_specs=[in_vmem] * (len(arrived) + 4),
        out_specs=in_hbm,
        out_shape=pltpu.HBM(residual.shape, jnp.bfloat16),
        scratch_shapes=[pltpu.VMEM((steps, rows, width), jnp.bfloat16), pltpu.SemaphoreType.DMA((steps,))],
        compiler_params=kernel_params(16),
        cost_estimate=pl.CostEstimate(flops=0, bytes_accessed=6 * mib, transcendentals=0),
        name="finish",
    )(projected, squares, *arrived, residual, gain.reshape(1, width))


def by_heads(
    queries,
    new_keys,
    new_values,
    pool_keys,
    pool_values,
    page_table,
    cache_len,
    out_weight,
    residual,
    post_gain,
):
    req_count, per_req, heads_here, head_dim = queries.shape
    kv_here = new_keys.shape[2]
    pages = pool_keys.shape[0]
    blk_count = lax.axis_size("blk")
    shares = lax.axis_size("head")
    group = heads_here // kv_here
    blk = lax.axis_index("blk")
    core, mine = blk % 2, lax.axis_index("head")
    place = jnp.stack([core, mine, blk // 4, blk // 2 % 2])
    width = out_weight.shape[2]
    weight = out_weight.reshape(heads_here * head_dim, width)
    queries = queries.reshape(req_count, shares, per_req // shares, heads_here, head_dim)
    exchange = functools.partial(lax.all_to_all, axis_name="blk", split_axis=0, concat_axis=0, tiled=True)

    def across(x, bits):
        return lax.ppermute(x, "blk", [(i, i ^ bits) for i in range(blk_count)])

    message = pack((1 - mine)[None], queries, kv_here, (pool_keys, pool_values, new_keys, new_values))
    message = exchange(message.reshape((blk_count,) + message.shape[2:]))
    got = lax.dynamic_slice(queries, (1 - core, mine, 0, 0, 0), (1, 1) + queries.shape[2:])
    got = across(got.reshape(queries.shape[2:]), 1)
    keep, send = spread(place, queries, got, kv_here)
    asked = list(gather(place, keep, across(send, 2)))
    asked[1] = across(asked[1], 4)
    message, *asked = lax.optimization_barrier((message, *asked))
    other = across(message, 1)
    asked = [across(x, 4 * step) if step > 1 else x for step, x in enumerate(asked)]
    asked = [x.reshape(4, 1, *x.shape[2:]) for x in asked]
    attend_share = functools.partial(attend, place, page_table, cache_len, message, other, pages=pages, group=group)

    first = attend_share([], attend_new(place, message, pages=pages, group=group))
    first, *asked = lax.optimization_barrier((first, *asked))
    first = exchange(first)
    second = attend_share(asked)
    first, second = lax.optimization_barrier((first, second))
    tile = width // 9
    begin = 0
    arrived = []
    for piece, tiles in enumerate((3, 3, 3)):
        if piece == 2:
            first, arrived[0] = lax.optimization_barrier((first, wait_here(arrived[0])))
        (sent,) = project(first, weight, req_count, begin, tiles * tile, tile, jnp.bfloat16)
        begin += tiles * tile
        if piece == 0:
            sent, second = lax.optimization_barrier((sent, second))
            second = exchange(second)
        else:
            first, sent = lax.optimization_barrier((first, sent))
        arrived.append(lax.ppermute(sent, "head", [(0, 1), (1, 0)]))
    projected, squares = project(second, weight, req_count, 0, width, tile, jnp.float32, arrived[:1])
    return finish(projected, squares, arrived[1:], residual, post_gain)


def group_pages(page_count, page_len):
    width = max(1, min(page_count, 2048 // page_len))
    while page_count % width:
        width -= 1
    return width


def attend_pages(running, grouped, key_pages, value_pages, valid_keys):
    page_count, page_len, kv_heads, head_dim = key_pages.shape
    tok_rows = valid_keys.shape[1]
    width = group_pages(page_count, page_len)
    groups = page_count // width
    key_groups = key_pages.reshape(groups, width * page_len, kv_heads, head_dim)
    value_groups = value_pages.reshape(groups, width * page_len, kv_heads, head_dim)
    valid_groups = (
        valid_keys.reshape(groups, width, tok_rows, page_len)
        .transpose(0, 2, 1, 3)
        .reshape(groups, tok_rows, width * page_len)
    )

    def compute(carry_in, key_block, value_block, valid_block):
        numerator, denominator = carry_in
        scores = (
            jnp.einsum("tkgd,skd->kgts", grouped, key_block, preferred_element_type=jnp.float32)
            * score_scale
        )
        capped = soft_cap * jnp.tanh(scores / soft_cap)
        weights = jnp.where(valid_block[None, None], jnp.exp(capped), 0.0).astype(jnp.bfloat16)
        numerator = numerator + jnp.einsum(
            "kgts,skd->tkgd", weights, value_block, preferred_element_type=jnp.float32
        )
        denominator = denominator + jnp.sum(weights.astype(jnp.float32), axis=-1)
        return (numerator, denominator)

    def one_group(carry_in, inputs):
        key_block, value_block, valid_block = inputs
        carry_out = compute(carry_in, key_block, value_block, valid_block)
        return (carry_out, None)

    result, _ = lax.scan(one_group, running, (key_groups, value_groups, valid_groups))
    return result


def shards(
    queries,
    new_keys,
    new_values,
    pool_keys,
    pool_values,
    page_table,
    cache_len,
    out_weight,
    residual,
    post_gain,
):
    req_count, per_req, heads_here, head_dim = queries.shape
    tok_dev = req_count * per_req
    kv_here = new_keys.shape[2]
    page_len = pool_keys.shape[1]
    slot_count = page_table.shape[1]
    blk_place = lax.axis_index("blk")
    row_ids = jnp.arange(tok_dev, dtype=jnp.int32)
    row_request = row_ids // per_req
    row_offset = blk_place * per_req + row_ids % per_req
    grouped = queries.reshape(tok_dev, kv_here, heads_here // kv_here, head_dim)
    page_rows = jnp.arange(page_len, dtype=jnp.int32)
    request_ids = jnp.arange(req_count, dtype=jnp.int32)
    row_onehot = row_request[:, None] == request_ids[None, :]
    start_carry = (
        jnp.zeros((tok_dev, kv_here, heads_here // kv_here, head_dim), jnp.float32),
        jnp.zeros((kv_here, heads_here // kv_here, tok_dev), jnp.float32),
    )
    pieces = (
        lax.all_gather(pool_keys, "blk", axis=0, tiled=True),
        lax.all_gather(pool_values, "blk", axis=0, tiled=True),
    )
    page_ids = jnp.arange(pieces[0].shape[0], dtype=jnp.int32)
    matches = page_ids[:, None, None] == page_table[None, :, :]
    slot_index = jnp.sum(
        jnp.where(matches, jnp.arange(slot_count, dtype=jnp.int32)[None, None, :], 0), axis=2
    )
    owned_page = jnp.any(matches, axis=2)
    position = slot_index[:, :, None] * page_len + page_rows[None, None, :]
    keep_keys = owned_page[:, :, None] & (position < cache_len[None, :, None])
    running = attend_pages(
        start_carry,
        grouped,
        pieces[0],
        pieces[1],
        jnp.any(keep_keys[:, None, :, :] & row_onehot[None, :, :, None], axis=2),
    )
    pieces = (
        lax.all_gather(new_keys, "blk", axis=1, tiled=True),
        lax.all_gather(new_values, "blk", axis=1, tiled=True),
    )
    piece_pages = pieces[0].shape[1] // page_len
    page_index = jnp.arange(req_count * piece_pages, dtype=jnp.int32)
    firsts = page_index % piece_pages * page_len
    key_pages = pieces[0].reshape(req_count * piece_pages, page_len, kv_here, head_dim)
    value_pages = pieces[1].reshape(req_count * piece_pages, page_len, kv_here, head_dim)
    offsets = firsts[:, None] + page_rows[None, :]
    same_request = (page_index // piece_pages)[:, None] == row_request[None, :]
    running = attend_pages(
        running,
        grouped,
        key_pages,
        value_pages,
        same_request[:, :, None] & (offsets[:, None, :] <= row_offset[None, :, None]),
    )
    numerator, denominator = running
    attended = (numerator / jnp.transpose(denominator, (2, 0, 1))[..., None]).astype(jnp.bfloat16)
    head_count = lax.axis_size("head")
    share = per_req // head_count
    feature_len = heads_here * head_dim
    attended = (
        attended.reshape(req_count, head_count, share, feature_len)
        .transpose(1, 0, 2, 3)
        .reshape(tok_dev, feature_len)
    )
    weight_rows = out_weight.reshape(feature_len, out_weight.shape[2])
    projected = lax.psum_scatter(
        jnp.dot(attended, weight_rows, preferred_element_type=jnp.float32).astype(jnp.bfloat16),
        "head",
        scatter_dimension=0,
        tiled=True,
    ).astype(jnp.float32)
    projected = projected.reshape(req_count, share, projected.shape[1])
    inv_rms = lax.rsqrt(jnp.mean(projected * projected, axis=-1, keepdims=True) + norm_eps)
    mixed_out = residual.astype(jnp.float32) + post_gain * projected * inv_rms
    return mixed_out.astype(jnp.bfloat16)


def solution(mesh):
    placed = (
        P(None, "blk", "head", None),
        P(None, "blk", "head", None),
        P(None, "blk", "head", None),
        P("blk", None, "head", None),
        P("blk", None, "head", None),
        P(),
        P(),
        P("head", None, None),
        P(None, ("blk", "head"), None),
        P(),
    )
    def one_device(queries, new_keys, *rest):
        requests, per_req = queries.shape[0], queries.shape[1]
        owners = mesh.shape["blk"] == 2 * new_keys.shape[2] == 16 and mesh.shape["head"] == 2 and requests == 2
        fits = rest[1].shape[1] == per_req == 128 and queries.shape[2] == 2 * new_keys.shape[2]
        return (by_heads if owners and fits else shards)(queries, new_keys, *rest)

    return jax.shard_map(
        one_device,
        mesh=mesh,
        in_specs=placed,
        out_specs=P(None, ("blk", "head"), None),
        check_vma=False,
    )
```

```python
import functools

import jax
import jax.numpy as jnp
from jax import lax
from jax.experimental import pallas as pl
from jax.experimental.pallas import tpu as pltpu
from jax.sharding import PartitionSpec as P

soft_cap = 50.0
score_scale = 144.0 ** (-0.5)
norm_eps = 1e-06
log2_e = 1.4426950408889634
key_tile = 256
mib = 1024 * 1024
in_vmem = pl.BlockSpec(memory_space=pltpu.VMEM)
in_hbm = pl.BlockSpec(memory_space=pltpu.HBM)
in_smem = pl.BlockSpec(memory_space=pltpu.SMEM)


def kernel_params(limit_mib):
    return pltpu.CompilerParams(vmem_limit_bytes=limit_mib * mib)


def split_heads(source, staged):
    rows, heads, head_dim = source.shape
    staged[0 : rows * heads, :] = source.reshape(rows * heads, head_dim).astype(jnp.float32)
    for head in range(heads):
        yield head, staged[pl.ds(head, rows, stride=heads), :].astype(jnp.bfloat16)


def pack_kernel(share_ref, *refs):
    *caches, queries, out, held_kv, held_q, made, staged, in_sem, out_sem = refs
    cores, _, rows, heads, head_dim = queries.shape
    group = heads // out.shape[0]
    tasks = []
    if caches:
        pool_k, pool_v, new_k, new_v = caches
        pages = pool_k.shape[0]
        for core, pool in enumerate((pool_k, pool_v)):
            tasks += [(pool.at[page], core, page) for page in range(pages)]
        for part, new in enumerate((new_k, new_v)):
            tasks += [(new.at[core], core, pages + part) for core in range(cores)]
    arrivals = [pltpu.make_async_copy(source, held_kv.at[i], in_sem.at[i]) for i, (source, _, _) in enumerate(tasks)]
    for core in range(cores):
        source = queries.at[core, share_ref[0]]
        arrivals.append(pltpu.make_async_copy(source, held_q.at[core], in_sem.at[len(tasks) + core]))
    for arrival in arrivals:
        arrival.start()
    leaving = []

    def leave(core, part):
        leaving.append(pltpu.make_async_copy(made.at[:, core, part], out.at[:, core, part], out_sem.at[len(leaving)]))
        leaving[-1].start()

    for i, (_, core, part) in enumerate(tasks):
        arrivals[i].wait()
        for head, picked in split_heads(held_kv[i], staged.at[i % 2]):
            made[head, core, part] = picked
        leave(core, part)
    last = out.shape[2] - 1
    for core in range(cores):
        arrivals[len(tasks) + core].wait()
        for head, picked in split_heads(held_q[core], staged.at[core % 2]):
            first = head % group * rows
            made[head // group, core, last, first : first + rows, :] = picked
        leave(core, last)
    for copy in leaving:
        copy.wait()


def pack(share, queries, kv_heads, caches=()):
    cores, _, rows, heads, head_dim = queries.shape
    group = heads // kv_heads
    parts, pieces, page_rows = 1, 0, group * rows
    if caches:
        pages = caches[0].shape[0]
        parts, pieces = pages + 3, 2 * pages + 2 * cores
    shape = (kv_heads, cores, parts, page_rows, head_dim)
    operands = [pltpu.with_memory_space_constraint(x, pltpu.HBM) for x in (*caches, queries)]
    return pl.pallas_call(
        pack_kernel,
        in_specs=[in_smem] + [in_hbm] * len(operands),
        out_specs=in_hbm,
        out_shape=pltpu.HBM(shape, jnp.bfloat16),
        scratch_shapes=[
            pltpu.VMEM((max(pieces, 1), page_rows, kv_heads, head_dim), jnp.bfloat16),
            pltpu.VMEM((cores, rows, heads, head_dim), jnp.bfloat16),
            pltpu.VMEM(shape, jnp.bfloat16),
            pltpu.VMEM((2, rows * heads, head_dim), jnp.float32),
            pltpu.SemaphoreType.DMA((pieces + cores,)),
            pltpu.SemaphoreType.DMA((pieces + cores,)),
        ],
        compiler_params=kernel_params(16),
        cost_estimate=pl.CostEstimate(flops=0, bytes_accessed=parts * mib, transcendentals=0),
        name="pack_cache" if caches else "pack_queries",
    )(share, *operands)


def spread_kernel(place_ref, queries, got, keep, send, held, made, staged, sems):
    core, share, side = place_ref[0], place_ref[1], place_ref[3]
    own = pltpu.make_async_copy(queries.at[core, share], held.at[core], sems.at[0])
    other = pltpu.make_async_copy(got, held.at[1 - core], sems.at[1])
    own.start()
    other.start()
    own.wait()
    other.wait()
    rows, heads, _ = got.shape
    group = heads // (2 * made.shape[1])
    for block in range(2):
        for head, picked in split_heads(held[block], staged.at[block]):
            owner, first = head // group, head % group * rows
            made[owner % 2, owner // 2, block, first : first + rows, :] = picked
    copies = [
        pltpu.make_async_copy(made.at[side], keep, sems.at[2]),
        pltpu.make_async_copy(made.at[1 - side], send, sems.at[3]),
    ]
    for copy in copies:
        copy.start()
    for copy in copies:
        copy.wait()


def spread(place, queries, got, kv_heads):
    rows, heads, head_dim = got.shape
    shape = (kv_heads // 2, 2, heads // kv_heads * rows, head_dim)
    return pl.pallas_call(
        spread_kernel,
        in_specs=[in_smem, in_hbm, in_hbm],
        out_specs=[in_hbm, in_hbm],
        out_shape=[pltpu.HBM(shape, jnp.bfloat16)] * 2,
        scratch_shapes=[
            pltpu.VMEM((2, rows, heads, head_dim), jnp.bfloat16),
            pltpu.VMEM((2,) + shape, jnp.bfloat16),
            pltpu.VMEM((2, rows * heads, head_dim), jnp.float32),
            pltpu.SemaphoreType.DMA((4,)),
        ],
        compiler_params=kernel_params(12),
        cost_estimate=pl.CostEstimate(flops=0, bytes_accessed=mib, transcendentals=0),
        name="spread_queries",
    )(place, *[pltpu.with_memory_space_constraint(x, pltpu.HBM) for x in (queries, got)])


def gather_kernel(place_ref, keep, got, *refs):
    *outs, sems = refs
    side, level = place_ref[3], place_ref[2]
    copies = []
    for step, out in enumerate(outs):
        copies.append(pltpu.make_async_copy(keep.at[level ^ step], out.at[side], sems.at[2 * step]))
        copies.append(pltpu.make_async_copy(got.at[level ^ step], out.at[1 - side], sems.at[2 * step + 1]))
    for copy in copies:
        copy.start()
    for copy in copies:
        copy.wait()


def gather(place, keep, got):
    levels = keep.shape[0]
    return pl.pallas_call(
        gather_kernel,
        in_specs=[in_smem, in_hbm, in_hbm],
        out_specs=[in_hbm] * levels,
        out_shape=[pltpu.HBM((2,) + keep.shape[1:], jnp.bfloat16)] * levels,
        scratch_shapes=[pltpu.SemaphoreType.DMA((2 * levels,))],
        compiler_params=kernel_params(4),
        cost_estimate=pl.CostEstimate(flops=0, bytes_accessed=mib, transcendentals=0),
        name="gather_queries",
    )(place, *[pltpu.with_memory_space_constraint(x, pltpu.HBM) for x in (keep, got)])


def add_keys(
    queries, query_part, total, per_head, group, share, page_rows, first_block, block_count, keys, values, start=None, causal=False
):
    block_rows = per_head * group
    rows = block_count * block_rows
    query = queries[first_block : first_block + block_count, query_part].reshape(rows, keys.shape[1])
    scores = lax.dot_general(query, keys, (((1,), (1,)), ((), ())), preferred_element_type=jnp.float32)
    weights = jnp.exp2((soft_cap * log2_e) * jnp.tanh(scores * (score_scale / soft_cap)))
    if causal:
        row = lax.broadcasted_iota(jnp.int32, weights.shape, 0)
        offset = row // block_rows * page_rows + row % per_head + share * per_head
        weights = jnp.where(lax.broadcasted_iota(jnp.int32, weights.shape, 1) <= offset, weights, 0.0)
    product = jnp.dot(weights.astype(jnp.bfloat16), values, preferred_element_type=jnp.float32)
    here = pl.ds(first_block * block_rows, rows)
    total[here, :] = product if start is None else start[here, :] + product


def add_new_keys(add, message, pages):
    blocks, _, page_rows, head_dim = message.shape
    half, tile_blocks = blocks // 2, key_tile // page_rows
    ones = jnp.ones((key_tile, head_dim), jnp.bfloat16)
    for block in range(0, blocks, tile_blocks):
        keys = message[block : block + tile_blocks, pages].reshape(key_tile, head_dim)
        values = message[block : block + tile_blocks, pages + 1].reshape(key_tile, head_dim)
        values = jnp.concatenate([values, ones], axis=1)
        start = None if block == 0 else add.args[2]
        add(block, tile_blocks, keys, values, start=start, causal=True)
        later = block + tile_blocks
        while later < blocks:
            count = min(half, blocks - later)
            add(later, count, keys, values, start=start)
            later += count


def new_kernel(pages, group, place_ref, message, total):
    page_rows = message.shape[2]
    per_head = page_rows // group
    share = 1 - place_ref[1]
    add_new_keys(functools.partial(add_keys, message, pages + 2, total, per_head, group, share, page_rows), message, pages)


def attend_new(place, message, *, pages, group):
    blocks, _, page_rows, head_dim = message.shape
    seen = blocks * page_rows * blocks // 2 * page_rows
    return pl.pallas_call(
        functools.partial(new_kernel, pages, group),
        in_specs=[in_smem, in_vmem],
        out_specs=in_vmem,
        out_shape=jax.ShapeDtypeStruct((blocks * page_rows, 2 * head_dim), jnp.float32),
        compiler_params=kernel_params(20),
        cost_estimate=pl.CostEstimate(flops=8 * seen * head_dim, bytes_accessed=4 * mib, transcendentals=2 * seen),
        name="attend_new",
    )(place, message)


def attend_kernel(pages, own_share, given, place_ref, table_ref, len_ref, message, other, *rest):
    out, cache_k, cache_v, total, made, held, others, in_sem, other_sem, out_sem = rest[-10:]
    fetch = pltpu.make_async_copy(other.at[:, 0:pages], others, other_sem)
    fetch.start()
    share = place_ref[1] if own_share else 1 - place_ref[1]
    queries, query_part = (held, 0) if own_share else (message, pages + 2)
    arrivals = []
    for step, source in enumerate(rest[:-10] if own_share else ()):
        count = source.shape[0]
        here = pl.ds((place_ref[2] ^ step) * count, count)
        arrivals.append(pltpu.make_async_copy(source, held.at[here], in_sem.at[step]))
        arrivals[-1].start()
    blocks, _, page_rows, head_dim = message.shape
    slots = table_ref.shape[1]
    group = out.shape[2] // head_dim
    per_head = out.shape[1]
    block_rows = per_head * group
    core = place_ref[0]
    cached = len_ref[core]
    half = blocks // 2
    tile_blocks = key_tile // page_rows
    copies = []

    add = functools.partial(add_keys, queries, query_part, total, per_head, group, share, page_rows)

    def leave(first):
        for block in range(first, first + half):
            here = pl.ds(block * block_rows, block_rows)
            attended = (total[here, 0:head_dim] / total[here, head_dim : 2 * head_dim]).astype(jnp.bfloat16)
            for head in range(group):
                made[block, :, head * head_dim : (head + 1) * head_dim] = attended[head * per_head : (head + 1) * per_head, :]
        here = pl.ds(first, half)
        copies.append(pltpu.make_async_copy(made.at[here], out.at[here], out_sem.at[len(copies)]))
        copies[-1].start()

    for arrival in arrivals:
        arrival.wait()
    if not given:
        add_new_keys(add, message, pages)
    fetch.wait()
    for tile in range(0, slots, tile_blocks):
        for slot in range(tile, tile + tile_blocks):
            page = table_ref[core, slot]
            mine = message[page // pages, page % pages]
            theirs = others[page // pages, page % pages]
            seen = slot * page_rows + lax.broadcasted_iota(jnp.int32, (page_rows, head_dim), 0) < cached
            here = pl.ds(slot * page_rows, page_rows)
            cache_k[here, :] = jnp.where(core == 0, mine, theirs)
            values = jnp.where(core == 0, theirs, mine).astype(jnp.float32)
            cache_v[here, 0:head_dim] = jnp.where(seen, values, 0.0).astype(jnp.bfloat16)
            cache_v[here, head_dim : 2 * head_dim] = jnp.where(seen, 1.0, 0.0).astype(jnp.bfloat16)
        here = slice(tile * page_rows, tile * page_rows + key_tile)
        for first in (0, half):
            add(first, half, cache_k[here, :], cache_v[here, :], start=rest[0] if given and tile == 0 else total)
            if tile + tile_blocks == slots:
                leave(first)
    for copy in copies:
        copy.wait()


def attend(place, page_table, cache_len, message, other, queries, given=None, *, pages, group):
    blocks, _, page_rows, head_dim = message.shape
    slots = page_table.shape[1]
    block_rows = page_rows
    operands = [message, other]
    operands += [pltpu.with_memory_space_constraint(x, pltpu.HBM) for x in queries]
    specs = [in_smem] * 3 + [in_vmem, pl.BlockSpec(memory_space=pl.ANY)] + [in_hbm] * len(queries)
    if given is not None:
        operands.append(given)
        specs.append(in_vmem)
    seen = blocks * block_rows * (slots + blocks // 2) * page_rows
    return pl.pallas_call(
        functools.partial(attend_kernel, pages, bool(queries), given is not None),
        in_specs=specs,
        out_specs=in_hbm,
        out_shape=pltpu.HBM((blocks, block_rows // group, group * head_dim), jnp.bfloat16),
        scratch_shapes=[
            pltpu.VMEM((slots * page_rows, head_dim), jnp.bfloat16),
            pltpu.VMEM((slots * page_rows, 2 * head_dim), jnp.bfloat16),
            pltpu.VMEM((blocks * block_rows, 2 * head_dim), jnp.float32),
            pltpu.VMEM((blocks, block_rows // group, group * head_dim), jnp.bfloat16),
            pltpu.VMEM((blocks, 1, block_rows, head_dim) if queries else (8, 128), jnp.bfloat16),
            pltpu.VMEM((blocks, pages, page_rows, head_dim), jnp.bfloat16),
            pltpu.SemaphoreType.DMA((max(len(queries), 1),)),
            pltpu.SemaphoreType.DMA(()),
            pltpu.SemaphoreType.DMA((2,)),
        ],
        compiler_params=kernel_params(24),
        cost_estimate=pl.CostEstimate(flops=8 * seen * head_dim, bytes_accessed=8 * mib, transcendentals=2 * seen),
        name="attend",
    )(place, page_table, cache_len, *operands)


def project_kernel(begin, attended, weight, *refs):
    arrived = []
    if len(refs) == 4:
        out, rows, held, sem = refs
    else:
        source, out, squares_out, rows, held, sem, piece, piece_sem = refs
        arrived = [piece]
        come = pltpu.make_async_copy(source, piece, piece_sem)
        come.start()
    tiles, _, tile = held.shape
    arrivals = []
    for i in range(tiles):
        columns = pl.ds(begin + i * tile, tile)
        arrivals.append(pltpu.make_async_copy(weight.at[:, columns], held.at[i], sem.at[i]))
        arrivals[-1].start()
    sources, count, features = attended.shape
    requests = rows.shape[0] // count
    for source in range(sources):
        at, first = source % requests * count, source // requests * features
        rows[at : at + count, first : first + features] = attended[source]
    squares = 0.0
    if arrived:
        come.wait()
    for i in range(tiles):
        here = slice(i * tile, (i + 1) * tile)
        arrivals[i].wait()
        product = jnp.dot(rows[...], held[i], preferred_element_type=jnp.float32)
        at = i * tile
        for piece in arrived:
            if 0 <= at < piece.shape[1]:
                product += piece[:, at : at + tile].astype(jnp.float32)
                squares += squares_by_lane(product)
            at -= piece.shape[1]
        out[:, here] = product.astype(out.dtype)
    if arrived:
        squares_out[...] = squares


def squares_by_lane(x):
    return sum(x[:, i : i + 128] * x[:, i : i + 128] for i in range(0, x.shape[1], 128))


def project(attended, weight, requests, begin, columns, tile, dtype, arrived=()):
    sources, count, features = attended.shape
    depth = weight.shape[0]
    rows = requests * count
    operands = [attended, pltpu.with_memory_space_constraint(weight, pltpu.HBM)]
    outs = [jax.ShapeDtypeStruct((rows, columns), dtype)]
    if arrived:
        operands += arrived
        outs.append(jax.ShapeDtypeStruct((rows, 128), jnp.float32))
    return pl.pallas_call(
        functools.partial(project_kernel, begin),
        in_specs=[in_vmem, in_hbm] + [pl.BlockSpec(memory_space=pl.ANY)] * len(arrived),
        out_specs=[in_vmem] * len(outs),
        out_shape=outs,
        scratch_shapes=[
            pltpu.VMEM((rows, depth), jnp.bfloat16),
            pltpu.VMEM((columns // tile, depth, tile), jnp.bfloat16),
            pltpu.SemaphoreType.DMA((columns // tile,)),
        ]
        + [y for x in arrived for y in (pltpu.VMEM(x.shape, x.dtype), pltpu.SemaphoreType.DMA(()))],
        compiler_params=kernel_params(12 + 2 * depth * columns // mib),
        cost_estimate=pl.CostEstimate(flops=2 * rows * depth * columns, bytes_accessed=2 * depth * columns, transcendentals=0),
        name="project",
    )(*operands)


def wait_here(x):
    return pl.pallas_call(
        lambda *_: None,
        in_specs=[pl.BlockSpec(memory_space=pl.ANY)],
        out_specs=pl.BlockSpec(memory_space=pl.ANY),
        out_shape=jax.ShapeDtypeStruct(x.shape, x.dtype),
        input_output_aliases={0: 0},
        cost_estimate=pl.CostEstimate(flops=5000000000, bytes_accessed=0, transcendentals=0),
        name="wait_here",
    )(x)


def finish_kernel(projected, squares_ref, *refs):
    *arrived, residual, gain, out, made, sem = refs
    requests, count, width = residual.shape
    rows = made.shape[1]
    split = width - sum(piece.shape[1] for piece in arrived)
    copies = []
    for step in range(made.shape[0]):
        request, first = step * rows // count, step * rows % count
        here = slice(step * rows, (step + 1) * rows)
        place = slice(first, first + rows)
        parts, squares, begin = [(slice(0, split), projected[here, 0:split])], squares_ref[here, :], split
        for piece in arrived:
            columns = slice(begin, begin + piece.shape[1])
            x = projected[here, columns] + piece[here, :].astype(jnp.float32)
            parts.append((columns, x))
            squares += squares_by_lane(x)
            begin = columns.stop
        inv_rms = lax.rsqrt(jnp.sum(squares, axis=-1, keepdims=True) / width + norm_eps)
        for columns, x in parts:
            mixed = residual[request, place, columns].astype(jnp.float32) + gain[:, columns] * x * inv_rms
            made[step, :, columns] = mixed.astype(jnp.bfloat16)
        copies.append(pltpu.make_async_copy(made.at[step], out.at[request, place], sem.at[step]))
        copies[-1].start()
    for copy in copies:
        copy.wait()


def finish(projected, squares, arrived, residual, gain):
    requests, count, width = residual.shape
    rows = 16
    steps = requests * count // rows
    return pl.pallas_call(
        finish_kernel,
        in_specs=[in_vmem] * (len(arrived) + 4),
        out_specs=in_hbm,
        out_shape=pltpu.HBM(residual.shape, jnp.bfloat16),
        scratch_shapes=[pltpu.VMEM((steps, rows, width), jnp.bfloat16), pltpu.SemaphoreType.DMA((steps,))],
        compiler_params=kernel_params(16),
        cost_estimate=pl.CostEstimate(flops=0, bytes_accessed=6 * mib, transcendentals=0),
        name="finish",
    )(projected, squares, *arrived, residual, gain.reshape(1, width))


def by_heads(
    queries,
    new_keys,
    new_values,
    pool_keys,
    pool_values,
    page_table,
    cache_len,
    out_weight,
    residual,
    post_gain,
):
    req_count, per_req, heads_here, head_dim = queries.shape
    kv_here = new_keys.shape[2]
    pages = pool_keys.shape[0]
    blk_count = lax.axis_size("blk")
    shares = lax.axis_size("head")
    group = heads_here // kv_here
    blk = lax.axis_index("blk")
    core, mine = blk % 2, lax.axis_index("head")
    place = jnp.stack([core, mine, blk // 4, blk // 2 % 2])
    width = out_weight.shape[2]
    weight = out_weight.reshape(heads_here * head_dim, width)
    queries = queries.reshape(req_count, shares, per_req // shares, heads_here, head_dim)
    exchange = functools.partial(lax.all_to_all, axis_name="blk", split_axis=0, concat_axis=0, tiled=True)

    def across(x, bits):
        return lax.ppermute(x, "blk", [(i, i ^ bits) for i in range(blk_count)])

    message = pack((1 - mine)[None], queries, kv_here, (pool_keys, pool_values, new_keys, new_values))
    message = exchange(message.reshape((blk_count,) + message.shape[2:]))
    got = lax.dynamic_slice(queries, (1 - core, mine, 0, 0, 0), (1, 1) + queries.shape[2:])
    got = across(got.reshape(queries.shape[2:]), 1)
    keep, send = spread(place, queries, got, kv_here)
    asked = list(gather(place, keep, across(send, 2)))
    asked[1] = across(asked[1], 4)
    message, *asked = lax.optimization_barrier((message, *asked))
    other = across(message, 1)
    asked = [across(x, 4 * step) if step > 1 else x for step, x in enumerate(asked)]
    asked = [x.reshape(4, 1, *x.shape[2:]) for x in asked]
    attend_share = functools.partial(attend, place, page_table, cache_len, message, other, pages=pages, group=group)

    first = attend_share([], attend_new(place, message, pages=pages, group=group))
    first, *asked = lax.optimization_barrier((first, *asked))
    first = exchange(first)
    second = attend_share(asked)
    first, second = lax.optimization_barrier((first, second))
    tile = width // 9
    begin = 0
    arrived = []
    for piece, tiles in enumerate((3, 3, 3)):
        if piece == 2:
            first, arrived[0] = lax.optimization_barrier((first, wait_here(arrived[0])))
        (sent,) = project(first, weight, req_count, begin, tiles * tile, tile, jnp.bfloat16)
        begin += tiles * tile
        if piece == 0:
            sent, second = lax.optimization_barrier((sent, second))
            second = exchange(second)
        else:
            first, sent = lax.optimization_barrier((first, sent))
        arrived.append(lax.ppermute(sent, "head", [(0, 1), (1, 0)]))
    projected, squares = project(second, weight, req_count, 0, width, tile, jnp.float32, arrived[:1])
    return finish(projected, squares, arrived[1:], residual, post_gain)


def group_pages(page_count, page_len):
    width = max(1, min(page_count, 2048 // page_len))
    while page_count % width:
        width -= 1
    return width


def attend_pages(running, grouped, key_pages, value_pages, valid_keys):
    page_count, page_len, kv_heads, head_dim = key_pages.shape
    tok_rows = valid_keys.shape[1]
    width = group_pages(page_count, page_len)
    groups = page_count // width
    key_groups = key_pages.reshape(groups, width * page_len, kv_heads, head_dim)
    value_groups = value_pages.reshape(groups, width * page_len, kv_heads, head_dim)
    valid_groups = (
        valid_keys.reshape(groups, width, tok_rows, page_len)
        .transpose(0, 2, 1, 3)
        .reshape(groups, tok_rows, width * page_len)
    )

    def compute(carry_in, key_block, value_block, valid_block):
        numerator, denominator = carry_in
        scores = (
            jnp.einsum("tkgd,skd->kgts", grouped, key_block, preferred_element_type=jnp.float32)
            * score_scale
        )
        capped = soft_cap * jnp.tanh(scores / soft_cap)
        weights = jnp.where(valid_block[None, None], jnp.exp(capped), 0.0).astype(jnp.bfloat16)
        numerator = numerator + jnp.einsum(
            "kgts,skd->tkgd", weights, value_block, preferred_element_type=jnp.float32
        )
        denominator = denominator + jnp.sum(weights.astype(jnp.float32), axis=-1)
        return (numerator, denominator)

    def one_group(carry_in, inputs):
        key_block, value_block, valid_block = inputs
        carry_out = compute(carry_in, key_block, value_block, valid_block)
        return (carry_out, None)

    result, _ = lax.scan(one_group, running, (key_groups, value_groups, valid_groups))
    return result


def shards(
    queries,
    new_keys,
    new_values,
    pool_keys,
    pool_values,
    page_table,
    cache_len,
    out_weight,
    residual,
    post_gain,
):
    req_count, per_req, heads_here, head_dim = queries.shape
    tok_dev = req_count * per_req
    kv_here = new_keys.shape[2]
    page_len = pool_keys.shape[1]
    slot_count = page_table.shape[1]
    blk_place = lax.axis_index("blk")
    row_ids = jnp.arange(tok_dev, dtype=jnp.int32)
    row_request = row_ids // per_req
    row_offset = blk_place * per_req + row_ids % per_req
    grouped = queries.reshape(tok_dev, kv_here, heads_here // kv_here, head_dim)
    page_rows = jnp.arange(page_len, dtype=jnp.int32)
    request_ids = jnp.arange(req_count, dtype=jnp.int32)
    row_onehot = row_request[:, None] == request_ids[None, :]
    start_carry = (
        jnp.zeros((tok_dev, kv_here, heads_here // kv_here, head_dim), jnp.float32),
        jnp.zeros((kv_here, heads_here // kv_here, tok_dev), jnp.float32),
    )
    pieces = (
        lax.all_gather(pool_keys, "blk", axis=0, tiled=True),
        lax.all_gather(pool_values, "blk", axis=0, tiled=True),
    )
    page_ids = jnp.arange(pieces[0].shape[0], dtype=jnp.int32)
    matches = page_ids[:, None, None] == page_table[None, :, :]
    slot_index = jnp.sum(
        jnp.where(matches, jnp.arange(slot_count, dtype=jnp.int32)[None, None, :], 0), axis=2
    )
    owned_page = jnp.any(matches, axis=2)
    position = slot_index[:, :, None] * page_len + page_rows[None, None, :]
    keep_keys = owned_page[:, :, None] & (position < cache_len[None, :, None])
    running = attend_pages(
        start_carry,
        grouped,
        pieces[0],
        pieces[1],
        jnp.any(keep_keys[:, None, :, :] & row_onehot[None, :, :, None], axis=2),
    )
    pieces = (
        lax.all_gather(new_keys, "blk", axis=1, tiled=True),
        lax.all_gather(new_values, "blk", axis=1, tiled=True),
    )
    piece_pages = pieces[0].shape[1] // page_len
    page_index = jnp.arange(req_count * piece_pages, dtype=jnp.int32)
    firsts = page_index % piece_pages * page_len
    key_pages = pieces[0].reshape(req_count * piece_pages, page_len, kv_here, head_dim)
    value_pages = pieces[1].reshape(req_count * piece_pages, page_len, kv_here, head_dim)
    offsets = firsts[:, None] + page_rows[None, :]
    same_request = (page_index // piece_pages)[:, None] == row_request[None, :]
    running = attend_pages(
        running,
        grouped,
        key_pages,
        value_pages,
        same_request[:, :, None] & (offsets[:, None, :] <= row_offset[None, :, None]),
    )
    numerator, denominator = running
    attended = (numerator / jnp.transpose(denominator, (2, 0, 1))[..., None]).astype(jnp.bfloat16)
    head_count = lax.axis_size("head")
    share = per_req // head_count
    feature_len = heads_here * head_dim
    attended = (
        attended.reshape(req_count, head_count, share, feature_len)
        .transpose(1, 0, 2, 3)
        .reshape(tok_dev, feature_len)
    )
    weight_rows = out_weight.reshape(feature_len, out_weight.shape[2])
    projected = lax.psum_scatter(
        jnp.dot(attended, weight_rows, preferred_element_type=jnp.float32).astype(jnp.bfloat16),
        "head",
        scatter_dimension=0,
        tiled=True,
    ).astype(jnp.float32)
    projected = projected.reshape(req_count, share, projected.shape[1])
    inv_rms = lax.rsqrt(jnp.mean(projected * projected, axis=-1, keepdims=True) + norm_eps)
    mixed_out = residual.astype(jnp.float32) + post_gain * projected * inv_rms
    return mixed_out.astype(jnp.bfloat16)


def solution(mesh):
    placed = (
        P(None, "blk", "head", None),
        P(None, "blk", "head", None),
        P(None, "blk", "head", None),
        P("blk", None, "head", None),
        P("blk", None, "head", None),
        P(),
        P(),
        P("head", None, None),
        P(None, ("blk", "head"), None),
        P(),
    )
    def one_device(queries, new_keys, *rest):
        requests, per_req = queries.shape[0], queries.shape[1]
        owners = mesh.shape["blk"] == 2 * new_keys.shape[2] == 16 and mesh.shape["head"] == 2 and requests == 2
        fits = rest[1].shape[1] == per_req == 128 and queries.shape[2] == 2 * new_keys.shape[2]
        return (by_heads if owners and fits else shards)(queries, new_keys, *rest)

    return jax.shard_map(
        one_device,
        mesh=mesh,
        in_specs=placed,
        out_specs=P(None, ("blk", "head"), None),
        check_vma=False,
    )
```

```python
import functools

import jax
import jax.numpy as jnp
from jax import lax
from jax.experimental import pallas as pl
from jax.experimental.pallas import tpu as pltpu
from jax.sharding import PartitionSpec as P

soft_cap = 50.0
score_scale = 144.0 ** (-0.5)
norm_eps = 1e-06
log2_e = 1.4426950408889634
key_tile = 256
mib = 1024 * 1024
in_vmem = pl.BlockSpec(memory_space=pltpu.VMEM)
in_hbm = pl.BlockSpec(memory_space=pltpu.HBM)
in_smem = pl.BlockSpec(memory_space=pltpu.SMEM)


def kernel_params(limit_mib):
    return pltpu.CompilerParams(vmem_limit_bytes=limit_mib * mib)


def split_heads(source, staged):
    rows, heads, head_dim = source.shape
    staged[0 : rows * heads, :] = source.reshape(rows * heads, head_dim).astype(jnp.float32)
    for head in range(heads):
        yield head, staged[pl.ds(head, rows, stride=heads), :].astype(jnp.bfloat16)


def pack_kernel(share_ref, *refs):
    *caches, queries, out, held_kv, held_q, made, staged, in_sem, out_sem = refs
    cores, _, rows, heads, head_dim = queries.shape
    group = heads // out.shape[0]
    tasks = []
    if caches:
        pool_k, pool_v, new_k, new_v = caches
        pages = pool_k.shape[0]
        for core, pool in enumerate((pool_k, pool_v)):
            tasks += [(pool.at[page], core, page) for page in range(pages)]
        for part, new in enumerate((new_k, new_v)):
            tasks += [(new.at[core], core, pages + part) for core in range(cores)]
    arrivals = [pltpu.make_async_copy(source, held_kv.at[i], in_sem.at[i]) for i, (source, _, _) in enumerate(tasks)]
    for core in range(cores):
        source = queries.at[core, share_ref[0]]
        arrivals.append(pltpu.make_async_copy(source, held_q.at[core], in_sem.at[len(tasks) + core]))
    for arrival in arrivals:
        arrival.start()
    leaving = []

    def leave(core, part):
        leaving.append(pltpu.make_async_copy(made.at[:, core, part], out.at[:, core, part], out_sem.at[len(leaving)]))
        leaving[-1].start()

    for i, (_, core, part) in enumerate(tasks):
        arrivals[i].wait()
        for head, picked in split_heads(held_kv[i], staged.at[i % 2]):
            made[head, core, part] = picked
        leave(core, part)
    last = out.shape[2] - 1
    for core in range(cores):
        arrivals[len(tasks) + core].wait()
        for head, picked in split_heads(held_q[core], staged.at[core % 2]):
            first = head % group * rows
            made[head // group, core, last, first : first + rows, :] = picked
        leave(core, last)
    for copy in leaving:
        copy.wait()


def pack(share, queries, kv_heads, caches=()):
    cores, _, rows, heads, head_dim = queries.shape
    group = heads // kv_heads
    parts, pieces, page_rows = 1, 0, group * rows
    if caches:
        pages = caches[0].shape[0]
        parts, pieces = pages + 3, 2 * pages + 2 * cores
    shape = (kv_heads, cores, parts, page_rows, head_dim)
    operands = [pltpu.with_memory_space_constraint(x, pltpu.HBM) for x in (*caches, queries)]
    return pl.pallas_call(
        pack_kernel,
        in_specs=[in_smem] + [in_hbm] * len(operands),
        out_specs=in_hbm,
        out_shape=pltpu.HBM(shape, jnp.bfloat16),
        scratch_shapes=[
            pltpu.VMEM((max(pieces, 1), page_rows, kv_heads, head_dim), jnp.bfloat16),
            pltpu.VMEM((cores, rows, heads, head_dim), jnp.bfloat16),
            pltpu.VMEM(shape, jnp.bfloat16),
            pltpu.VMEM((2, rows * heads, head_dim), jnp.float32),
            pltpu.SemaphoreType.DMA((pieces + cores,)),
            pltpu.SemaphoreType.DMA((pieces + cores,)),
        ],
        compiler_params=kernel_params(16),
        cost_estimate=pl.CostEstimate(flops=0, bytes_accessed=parts * mib, transcendentals=0),
        name="pack_cache" if caches else "pack_queries",
    )(share, *operands)


def spread_kernel(place_ref, queries, got, keep, send, held, made, staged, sems):
    core, share, side = place_ref[0], place_ref[1], place_ref[3]
    own = pltpu.make_async_copy(queries.at[core, share], held.at[core], sems.at[0])
    other = pltpu.make_async_copy(got, held.at[1 - core], sems.at[1])
    own.start()
    other.start()
    own.wait()
    other.wait()
    rows, heads, _ = got.shape
    group = heads // (2 * made.shape[1])
    for block in range(2):
        for head, picked in split_heads(held[block], staged.at[block]):
            owner, first = head // group, head % group * rows
            made[owner % 2, owner // 2, block, first : first + rows, :] = picked
    copies = [
        pltpu.make_async_copy(made.at[side], keep, sems.at[2]),
        pltpu.make_async_copy(made.at[1 - side], send, sems.at[3]),
    ]
    for copy in copies:
        copy.start()
    for copy in copies:
        copy.wait()


def spread(place, queries, got, kv_heads):
    rows, heads, head_dim = got.shape
    shape = (kv_heads // 2, 2, heads // kv_heads * rows, head_dim)
    return pl.pallas_call(
        spread_kernel,
        in_specs=[in_smem, in_hbm, in_hbm],
        out_specs=[in_hbm, in_hbm],
        out_shape=[pltpu.HBM(shape, jnp.bfloat16)] * 2,
        scratch_shapes=[
            pltpu.VMEM((2, rows, heads, head_dim), jnp.bfloat16),
            pltpu.VMEM((2,) + shape, jnp.bfloat16),
            pltpu.VMEM((2, rows * heads, head_dim), jnp.float32),
            pltpu.SemaphoreType.DMA((4,)),
        ],
        compiler_params=kernel_params(12),
        cost_estimate=pl.CostEstimate(flops=0, bytes_accessed=mib, transcendentals=0),
        name="spread_queries",
    )(place, *[pltpu.with_memory_space_constraint(x, pltpu.HBM) for x in (queries, got)])


def gather_kernel(place_ref, keep, got, *refs):
    *outs, sems = refs
    side, level = place_ref[3], place_ref[2]
    copies = []
    for step, out in enumerate(outs):
        copies.append(pltpu.make_async_copy(keep.at[level ^ step], out.at[side], sems.at[2 * step]))
        copies.append(pltpu.make_async_copy(got.at[level ^ step], out.at[1 - side], sems.at[2 * step + 1]))
    for copy in copies:
        copy.start()
    for copy in copies:
        copy.wait()


def gather(place, keep, got):
    levels = keep.shape[0]
    return pl.pallas_call(
        gather_kernel,
        in_specs=[in_smem, in_hbm, in_hbm],
        out_specs=[in_hbm] * levels,
        out_shape=[pltpu.HBM((2,) + keep.shape[1:], jnp.bfloat16)] * levels,
        scratch_shapes=[pltpu.SemaphoreType.DMA((2 * levels,))],
        compiler_params=kernel_params(4),
        cost_estimate=pl.CostEstimate(flops=0, bytes_accessed=mib, transcendentals=0),
        name="gather_queries",
    )(place, *[pltpu.with_memory_space_constraint(x, pltpu.HBM) for x in (keep, got)])


def add_keys(
    queries, query_part, total, per_head, group, share, page_rows, first_block, block_count, keys, values, start=None, causal=False
):
    block_rows = per_head * group
    rows = block_count * block_rows
    query = queries[first_block : first_block + block_count, query_part].reshape(rows, keys.shape[1])
    scores = lax.dot_general(query, keys, (((1,), (1,)), ((), ())), preferred_element_type=jnp.float32)
    weights = jnp.exp2((soft_cap * log2_e) * jnp.tanh(scores * (score_scale / soft_cap)))
    if causal:
        row = lax.broadcasted_iota(jnp.int32, weights.shape, 0)
        offset = row // block_rows * page_rows + row % per_head + share * per_head
        weights = jnp.where(lax.broadcasted_iota(jnp.int32, weights.shape, 1) <= offset, weights, 0.0)
    product = jnp.dot(weights.astype(jnp.bfloat16), values, preferred_element_type=jnp.float32)
    here = pl.ds(first_block * block_rows, rows)
    total[here, :] = product if start is None else start[here, :] + product


def add_new_keys(add, message, pages):
    blocks, _, page_rows, head_dim = message.shape
    half, tile_blocks = blocks // 2, key_tile // page_rows
    ones = jnp.ones((key_tile, head_dim), jnp.bfloat16)
    for block in range(0, blocks, tile_blocks):
        keys = message[block : block + tile_blocks, pages].reshape(key_tile, head_dim)
        values = message[block : block + tile_blocks, pages + 1].reshape(key_tile, head_dim)
        values = jnp.concatenate([values, ones], axis=1)
        start = None if block == 0 else add.args[2]
        add(block, tile_blocks, keys, values, start=start, causal=True)
        later = block + tile_blocks
        while later < blocks:
            count = min(half, blocks - later)
            add(later, count, keys, values, start=start)
            later += count


def new_kernel(pages, group, place_ref, message, total):
    page_rows = message.shape[2]
    per_head = page_rows // group
    share = 1 - place_ref[1]
    add_new_keys(functools.partial(add_keys, message, pages + 2, total, per_head, group, share, page_rows), message, pages)


def attend_new(place, message, *, pages, group):
    blocks, _, page_rows, head_dim = message.shape
    seen = blocks * page_rows * blocks // 2 * page_rows
    return pl.pallas_call(
        functools.partial(new_kernel, pages, group),
        in_specs=[in_smem, in_vmem],
        out_specs=in_vmem,
        out_shape=jax.ShapeDtypeStruct((blocks * page_rows, 2 * head_dim), jnp.float32),
        compiler_params=kernel_params(20),
        cost_estimate=pl.CostEstimate(flops=8 * seen * head_dim, bytes_accessed=4 * mib, transcendentals=2 * seen),
        name="attend_new",
    )(place, message)


def attend_kernel(pages, own_share, given, place_ref, table_ref, len_ref, message, other, *rest):
    out, cache_k, cache_v, total, made, held, others, in_sem, other_sem, out_sem = rest[-10:]
    fetch = pltpu.make_async_copy(other.at[:, 0:pages], others, other_sem)
    fetch.start()
    share = place_ref[1] if own_share else 1 - place_ref[1]
    queries, query_part = (held, 0) if own_share else (message, pages + 2)
    arrivals = []
    for step, source in enumerate(rest[:-10] if own_share else ()):
        count = source.shape[0]
        here = pl.ds((place_ref[2] ^ step) * count, count)
        arrivals.append(pltpu.make_async_copy(source, held.at[here], in_sem.at[step]))
        arrivals[-1].start()
    blocks, _, page_rows, head_dim = message.shape
    slots = table_ref.shape[1]
    group = out.shape[2] // head_dim
    per_head = out.shape[1]
    block_rows = per_head * group
    core = place_ref[0]
    cached = len_ref[core]
    half = blocks // 2
    tile_blocks = key_tile // page_rows
    copies = []

    add = functools.partial(add_keys, queries, query_part, total, per_head, group, share, page_rows)

    def leave(first):
        for block in range(first, first + half):
            here = pl.ds(block * block_rows, block_rows)
            attended = (total[here, 0:head_dim] / total[here, head_dim : 2 * head_dim]).astype(jnp.bfloat16)
            for head in range(group):
                made[block, :, head * head_dim : (head + 1) * head_dim] = attended[head * per_head : (head + 1) * per_head, :]
        here = pl.ds(first, half)
        copies.append(pltpu.make_async_copy(made.at[here], out.at[here], out_sem.at[len(copies)]))
        copies[-1].start()

    for arrival in arrivals:
        arrival.wait()
    if not given:
        add_new_keys(add, message, pages)
    fetch.wait()
    for tile in range(0, slots, tile_blocks):
        for slot in range(tile, tile + tile_blocks):
            page = table_ref[core, slot]
            mine = message[page // pages, page % pages]
            theirs = others[page // pages, page % pages]
            seen = slot * page_rows + lax.broadcasted_iota(jnp.int32, (page_rows, head_dim), 0) < cached
            here = pl.ds(slot * page_rows, page_rows)
            cache_k[here, :] = jnp.where(core == 0, mine, theirs)
            values = jnp.where(core == 0, theirs, mine).astype(jnp.float32)
            cache_v[here, 0:head_dim] = jnp.where(seen, values, 0.0).astype(jnp.bfloat16)
            cache_v[here, head_dim : 2 * head_dim] = jnp.where(seen, 1.0, 0.0).astype(jnp.bfloat16)
        here = slice(tile * page_rows, tile * page_rows + key_tile)
        for first in (0, half):
            add(first, half, cache_k[here, :], cache_v[here, :], start=rest[0] if given and tile == 0 else total)
            if tile + tile_blocks == slots:
                leave(first)
    for copy in copies:
        copy.wait()


def attend(place, page_table, cache_len, message, other, queries, given=None, *, pages, group):
    blocks, _, page_rows, head_dim = message.shape
    slots = page_table.shape[1]
    block_rows = page_rows
    operands = [message, other]
    operands += [pltpu.with_memory_space_constraint(x, pltpu.HBM) for x in queries]
    specs = [in_smem] * 3 + [in_vmem, pl.BlockSpec(memory_space=pl.ANY)] + [in_hbm] * len(queries)
    if given is not None:
        operands.append(given)
        specs.append(in_vmem)
    seen = blocks * block_rows * (slots + blocks // 2) * page_rows
    return pl.pallas_call(
        functools.partial(attend_kernel, pages, bool(queries), given is not None),
        in_specs=specs,
        out_specs=in_hbm,
        out_shape=pltpu.HBM((blocks, block_rows // group, group * head_dim), jnp.bfloat16),
        scratch_shapes=[
            pltpu.VMEM((slots * page_rows, head_dim), jnp.bfloat16),
            pltpu.VMEM((slots * page_rows, 2 * head_dim), jnp.bfloat16),
            pltpu.VMEM((blocks * block_rows, 2 * head_dim), jnp.float32),
            pltpu.VMEM((blocks, block_rows // group, group * head_dim), jnp.bfloat16),
            pltpu.VMEM((blocks, 1, block_rows, head_dim) if queries else (8, 128), jnp.bfloat16),
            pltpu.VMEM((blocks, pages, page_rows, head_dim), jnp.bfloat16),
            pltpu.SemaphoreType.DMA((max(len(queries), 1),)),
            pltpu.SemaphoreType.DMA(()),
            pltpu.SemaphoreType.DMA((2,)),
        ],
        compiler_params=kernel_params(24),
        cost_estimate=pl.CostEstimate(flops=8 * seen * head_dim, bytes_accessed=8 * mib, transcendentals=2 * seen),
        name="attend",
    )(place, page_table, cache_len, *operands)


def project_kernel(begin, attended, weight, *refs):
    (*arrived, out), (rows, held, sem) = refs[:-3], refs[-3:]
    if arrived:
        *arrived, out, squares_out = (*arrived, out)
    tiles, _, tile = held.shape
    arrivals = []
    for i in range(tiles):
        columns = pl.ds(begin + i * tile, tile)
        arrivals.append(pltpu.make_async_copy(weight.at[:, columns], held.at[i], sem.at[i]))
        arrivals[-1].start()
    sources, count, features = attended.shape
    requests = rows.shape[0] // count
    for source in range(sources):
        at, first = source % requests * count, source // requests * features
        rows[at : at + count, first : first + features] = attended[source]
    squares = 0.0
    for i in range(tiles):
        here = slice(i * tile, (i + 1) * tile)
        arrivals[i].wait()
        product = jnp.dot(rows[...], held[i], preferred_element_type=jnp.float32)
        at = i * tile
        for piece in arrived:
            if 0 <= at < piece.shape[1]:
                product += piece[:, at : at + tile].astype(jnp.float32)
                squares += squares_by_lane(product)
            at -= piece.shape[1]
        out[:, here] = product.astype(out.dtype)
    if arrived:
        squares_out[...] = squares


def squares_by_lane(x):
    return sum(x[:, i : i + 128] * x[:, i : i + 128] for i in range(0, x.shape[1], 128))


def project(attended, weight, requests, begin, columns, tile, dtype, arrived=()):
    sources, count, features = attended.shape
    depth = weight.shape[0]
    rows = requests * count
    operands = [attended, pltpu.with_memory_space_constraint(weight, pltpu.HBM)]
    outs = [jax.ShapeDtypeStruct((rows, columns), dtype)]
    if arrived:
        operands += arrived
        outs.append(jax.ShapeDtypeStruct((rows, 128), jnp.float32))
    return pl.pallas_call(
        functools.partial(project_kernel, begin),
        in_specs=[in_vmem, in_hbm] + [in_vmem] * (len(operands) - 2),
        out_specs=[in_vmem] * len(outs),
        out_shape=outs,
        scratch_shapes=[
            pltpu.VMEM((rows, depth), jnp.bfloat16),
            pltpu.VMEM((columns // tile, depth, tile), jnp.bfloat16),
            pltpu.SemaphoreType.DMA((columns // tile,)),
        ],
        compiler_params=kernel_params(12 + 2 * depth * columns // mib),
        cost_estimate=pl.CostEstimate(flops=2 * rows * depth * columns, bytes_accessed=2 * depth * columns, transcendentals=0),
        name="project",
    )(*operands)


def wait_here(x):
    return pl.pallas_call(
        lambda *_: None,
        in_specs=[pl.BlockSpec(memory_space=pl.ANY)],
        out_specs=pl.BlockSpec(memory_space=pl.ANY),
        out_shape=jax.ShapeDtypeStruct(x.shape, x.dtype),
        input_output_aliases={0: 0},
        cost_estimate=pl.CostEstimate(flops=5000000000, bytes_accessed=0, transcendentals=0),
        name="wait_here",
    )(x)


def finish_kernel(projected, squares_ref, *refs):
    *arrived, residual, gain, out, made, sem = refs
    requests, count, width = residual.shape
    rows = made.shape[1]
    split = width - sum(piece.shape[1] for piece in arrived)
    copies = []
    for step in range(made.shape[0]):
        request, first = step * rows // count, step * rows % count
        here = slice(step * rows, (step + 1) * rows)
        place = slice(first, first + rows)
        parts, squares, begin = [(slice(0, split), projected[here, 0:split])], squares_ref[here, :], split
        for piece in arrived:
            columns = slice(begin, begin + piece.shape[1])
            x = projected[here, columns] + piece[here, :].astype(jnp.float32)
            parts.append((columns, x))
            squares += squares_by_lane(x)
            begin = columns.stop
        inv_rms = lax.rsqrt(jnp.sum(squares, axis=-1, keepdims=True) / width + norm_eps)
        for columns, x in parts:
            mixed = residual[request, place, columns].astype(jnp.float32) + gain[:, columns] * x * inv_rms
            made[step, :, columns] = mixed.astype(jnp.bfloat16)
        copies.append(pltpu.make_async_copy(made.at[step], out.at[request, place], sem.at[step]))
        copies[-1].start()
    for copy in copies:
        copy.wait()


def finish(projected, squares, arrived, residual, gain):
    requests, count, width = residual.shape
    rows = 32
    steps = requests * count // rows
    return pl.pallas_call(
        finish_kernel,
        in_specs=[in_vmem] * (len(arrived) + 4),
        out_specs=in_hbm,
        out_shape=pltpu.HBM(residual.shape, jnp.bfloat16),
        scratch_shapes=[pltpu.VMEM((steps, rows, width), jnp.bfloat16), pltpu.SemaphoreType.DMA((steps,))],
        compiler_params=kernel_params(16),
        cost_estimate=pl.CostEstimate(flops=0, bytes_accessed=6 * mib, transcendentals=0),
        name="finish",
    )(projected, squares, *arrived, residual, gain.reshape(1, width))


def by_heads(
    queries,
    new_keys,
    new_values,
    pool_keys,
    pool_values,
    page_table,
    cache_len,
    out_weight,
    residual,
    post_gain,
):
    req_count, per_req, heads_here, head_dim = queries.shape
    kv_here = new_keys.shape[2]
    pages = pool_keys.shape[0]
    blk_count = lax.axis_size("blk")
    shares = lax.axis_size("head")
    group = heads_here // kv_here
    blk = lax.axis_index("blk")
    core, mine = blk % 2, lax.axis_index("head")
    place = jnp.stack([core, mine, blk // 4, blk // 2 % 2])
    width = out_weight.shape[2]
    weight = out_weight.reshape(heads_here * head_dim, width)
    queries = queries.reshape(req_count, shares, per_req // shares, heads_here, head_dim)
    exchange = functools.partial(lax.all_to_all, axis_name="blk", split_axis=0, concat_axis=0, tiled=True)

    def across(x, bits):
        return lax.ppermute(x, "blk", [(i, i ^ bits) for i in range(blk_count)])

    message = pack((1 - mine)[None], queries, kv_here, (pool_keys, pool_values, new_keys, new_values))
    message = exchange(message.reshape((blk_count,) + message.shape[2:]))
    got = lax.dynamic_slice(queries, (1 - core, mine, 0, 0, 0), (1, 1) + queries.shape[2:])
    got = across(got.reshape(queries.shape[2:]), 1)
    keep, send = spread(place, queries, got, kv_here)
    asked = list(gather(place, keep, across(send, 2)))
    asked[1] = across(asked[1], 4)
    message, *asked = lax.optimization_barrier((message, *asked))
    other = across(message, 1)
    asked = [across(x, 4 * step) if step > 1 else x for step, x in enumerate(asked)]
    asked = [x.reshape(4, 1, *x.shape[2:]) for x in asked]
    attend_share = functools.partial(attend, place, page_table, cache_len, message, other, pages=pages, group=group)

    first = attend_share([], attend_new(place, message, pages=pages, group=group))
    first, *asked = lax.optimization_barrier((first, *asked))
    first = exchange(first)
    second = attend_share(asked)
    first, second = lax.optimization_barrier((first, second))
    tile = width // 9
    begin = 0
    arrived = []
    for piece, tiles in enumerate((3, 4, 2)):
        if piece == 2:
            first, arrived[0] = lax.optimization_barrier((first, wait_here(arrived[0])))
        (sent,) = project(first, weight, req_count, begin, tiles * tile, tile, jnp.bfloat16)
        begin += tiles * tile
        if piece == 0:
            sent, second = lax.optimization_barrier((sent, second))
            second = exchange(second)
        else:
            first, sent = lax.optimization_barrier((first, sent))
        arrived.append(lax.ppermute(sent, "head", [(0, 1), (1, 0)]))
    projected, squares = project(second, weight, req_count, 0, width, tile, jnp.float32, arrived[:1])
    return finish(projected, squares, arrived[1:], residual, post_gain)


def group_pages(page_count, page_len):
    width = max(1, min(page_count, 2048 // page_len))
    while page_count % width:
        width -= 1
    return width


def attend_pages(running, grouped, key_pages, value_pages, valid_keys):
    page_count, page_len, kv_heads, head_dim = key_pages.shape
    tok_rows = valid_keys.shape[1]
    width = group_pages(page_count, page_len)
    groups = page_count // width
    key_groups = key_pages.reshape(groups, width * page_len, kv_heads, head_dim)
    value_groups = value_pages.reshape(groups, width * page_len, kv_heads, head_dim)
    valid_groups = (
        valid_keys.reshape(groups, width, tok_rows, page_len)
        .transpose(0, 2, 1, 3)
        .reshape(groups, tok_rows, width * page_len)
    )

    def compute(carry_in, key_block, value_block, valid_block):
        numerator, denominator = carry_in
        scores = (
            jnp.einsum("tkgd,skd->kgts", grouped, key_block, preferred_element_type=jnp.float32)
            * score_scale
        )
        capped = soft_cap * jnp.tanh(scores / soft_cap)
        weights = jnp.where(valid_block[None, None], jnp.exp(capped), 0.0).astype(jnp.bfloat16)
        numerator = numerator + jnp.einsum(
            "kgts,skd->tkgd", weights, value_block, preferred_element_type=jnp.float32
        )
        denominator = denominator + jnp.sum(weights.astype(jnp.float32), axis=-1)
        return (numerator, denominator)

    def one_group(carry_in, inputs):
        key_block, value_block, valid_block = inputs
        carry_out = compute(carry_in, key_block, value_block, valid_block)
        return (carry_out, None)

    result, _ = lax.scan(one_group, running, (key_groups, value_groups, valid_groups))
    return result


def shards(
    queries,
    new_keys,
    new_values,
    pool_keys,
    pool_values,
    page_table,
    cache_len,
    out_weight,
    residual,
    post_gain,
):
    req_count, per_req, heads_here, head_dim = queries.shape
    tok_dev = req_count * per_req
    kv_here = new_keys.shape[2]
    page_len = pool_keys.shape[1]
    slot_count = page_table.shape[1]
    blk_place = lax.axis_index("blk")
    row_ids = jnp.arange(tok_dev, dtype=jnp.int32)
    row_request = row_ids // per_req
    row_offset = blk_place * per_req + row_ids % per_req
    grouped = queries.reshape(tok_dev, kv_here, heads_here // kv_here, head_dim)
    page_rows = jnp.arange(page_len, dtype=jnp.int32)
    request_ids = jnp.arange(req_count, dtype=jnp.int32)
    row_onehot = row_request[:, None] == request_ids[None, :]
    start_carry = (
        jnp.zeros((tok_dev, kv_here, heads_here // kv_here, head_dim), jnp.float32),
        jnp.zeros((kv_here, heads_here // kv_here, tok_dev), jnp.float32),
    )
    pieces = (
        lax.all_gather(pool_keys, "blk", axis=0, tiled=True),
        lax.all_gather(pool_values, "blk", axis=0, tiled=True),
    )
    page_ids = jnp.arange(pieces[0].shape[0], dtype=jnp.int32)
    matches = page_ids[:, None, None] == page_table[None, :, :]
    slot_index = jnp.sum(
        jnp.where(matches, jnp.arange(slot_count, dtype=jnp.int32)[None, None, :], 0), axis=2
    )
    owned_page = jnp.any(matches, axis=2)
    position = slot_index[:, :, None] * page_len + page_rows[None, None, :]
    keep_keys = owned_page[:, :, None] & (position < cache_len[None, :, None])
    running = attend_pages(
        start_carry,
        grouped,
        pieces[0],
        pieces[1],
        jnp.any(keep_keys[:, None, :, :] & row_onehot[None, :, :, None], axis=2),
    )
    pieces = (
        lax.all_gather(new_keys, "blk", axis=1, tiled=True),
        lax.all_gather(new_values, "blk", axis=1, tiled=True),
    )
    piece_pages = pieces[0].shape[1] // page_len
    page_index = jnp.arange(req_count * piece_pages, dtype=jnp.int32)
    firsts = page_index % piece_pages * page_len
    key_pages = pieces[0].reshape(req_count * piece_pages, page_len, kv_here, head_dim)
    value_pages = pieces[1].reshape(req_count * piece_pages, page_len, kv_here, head_dim)
    offsets = firsts[:, None] + page_rows[None, :]
    same_request = (page_index // piece_pages)[:, None] == row_request[None, :]
    running = attend_pages(
        running,
        grouped,
        key_pages,
        value_pages,
        same_request[:, :, None] & (offsets[:, None, :] <= row_offset[None, :, None]),
    )
    numerator, denominator = running
    attended = (numerator / jnp.transpose(denominator, (2, 0, 1))[..., None]).astype(jnp.bfloat16)
    head_count = lax.axis_size("head")
    share = per_req // head_count
    feature_len = heads_here * head_dim
    attended = (
        attended.reshape(req_count, head_count, share, feature_len)
        .transpose(1, 0, 2, 3)
        .reshape(tok_dev, feature_len)
    )
    weight_rows = out_weight.reshape(feature_len, out_weight.shape[2])
    projected = lax.psum_scatter(
        jnp.dot(attended, weight_rows, preferred_element_type=jnp.float32).astype(jnp.bfloat16),
        "head",
        scatter_dimension=0,
        tiled=True,
    ).astype(jnp.float32)
    projected = projected.reshape(req_count, share, projected.shape[1])
    inv_rms = lax.rsqrt(jnp.mean(projected * projected, axis=-1, keepdims=True) + norm_eps)
    mixed_out = residual.astype(jnp.float32) + post_gain * projected * inv_rms
    return mixed_out.astype(jnp.bfloat16)


def solution(mesh):
    placed = (
        P(None, "blk", "head", None),
        P(None, "blk", "head", None),
        P(None, "blk", "head", None),
        P("blk", None, "head", None),
        P("blk", None, "head", None),
        P(),
        P(),
        P("head", None, None),
        P(None, ("blk", "head"), None),
        P(),
    )
    def one_device(queries, new_keys, *rest):
        requests, per_req = queries.shape[0], queries.shape[1]
        owners = mesh.shape["blk"] == 2 * new_keys.shape[2] == 16 and mesh.shape["head"] == 2 and requests == 2
        fits = rest[1].shape[1] == per_req == 128 and queries.shape[2] == 2 * new_keys.shape[2]
        return (by_heads if owners and fits else shards)(queries, new_keys, *rest)

    return jax.shard_map(
        one_device,
        mesh=mesh,
        in_specs=placed,
        out_specs=P(None, ("blk", "head"), None),
        check_vma=False,
    )
```
